32 devices in a mesh: atoms: 16 (over z, x, core), beads: 2 (over y).
Axes of the slice: x: 2, y: 2, z: 4, core: 2. Of those that a mesh axis runs over, the one named last changes fastest.
Arguments:
- positions: float32 [8, 3, 2048], P('beads', None, 'atoms'), may hold values from 0 to 1
- velocities: float32 [8, 3, 2048], P('beads', None, 'atoms'), may hold values from -3 to 3
- charges_in: float32 [8, 2048], P('beads', 'atoms'), may hold values from -3 to 3
- species: int32 [2048], P('atoms'), may hold values from 0 to 7
- neighbors: int32 [8, 2048], P(None, 'atoms'), may hold values from -32 to 32
- k_index: int32 [3, 2048], replicated, may hold values from -8 to 8
- kernel: float32 [2048], replicated, may hold values from 0.1 to 1
- chi_table: float32 [8], replicated, may hold values from -2 to 2
- hard_table: float32 [8], replicated, may hold values from 1 to 4
- bond_table: float32 [8], replicated, may hold values from 0.2 to 0.8
- mass_table: float32 [8], replicated, may hold values from 1 to 8
Outputs:
- new_positions: float32 [8, 3, 2048], P('beads', None, 'atoms')
- new_velocities: float32 [8, 3, 2048], P('beads', None, 'atoms')
- charges: float32 [8, 2048], P('beads', 'atoms')
The draws below stay inside these ranges and needn't reach their ends.
Inputs may be any that keep to these rules, and one draw needn't show every extreme that they name: species index the tables. `neighbors`: neighbour offsets count in atom order, cyclically over 2048 atoms.
All inputs are finite; a program needn't handle non-finite values.
Results may differ from the reference program's by a relative error of at most 0.00021.
Values sent between devices are 32-bit elements; how exact they have to be, the bound alone decides.
No kernel may reach another device: no remote copies, remote signals or barrier semaphores. Data moves between devices by JAX's collectives and lax.ppermute only.
A program may use at most 64 MiB of HBM per device.

```python
import math
import jax
import jax.numpy as jnp
from jax import lax

KVEC = 2048
KMAX = 8
QITERS = 2
NBR = 8
RIM = 32
SPECIES = 8
ATOMS = 2048
BEADS = 8


def touch_ends(drawn, rng, low, top_value):
    shape = drawn.shape
    spot = [jax.random.randint(jax.random.fold_in(rng, axis), (), 0, shape[axis]) for axis in range(len(shape))]
    drawn = drawn.at[tuple(spot)].set(low)
    longest = shape.index(max(shape))
    spot[longest] = (spot[longest] + 1) % shape[longest]
    return drawn.at[tuple(spot)].set(top_value)


def level_of(own_key, shape, pieces, smallest, high):
    level, own = 1.0, jax.random.fold_in(own_key, 6)
    for axis_at, blocks in pieces:
        draws = jnp.exp(jax.random.uniform(jax.random.fold_in(own, axis_at), (blocks,), jnp.float32, smallest / len(pieces), high / len(pieces)))
        level = level * jnp.repeat(draws, shape[axis_at] // blocks).reshape([-1 if axis == axis_at else 1 for axis in range(len(shape))])
    return level


def gaussian(own_key, dims, spread, most, split=(), kind=jnp.bfloat16):
    gain = level_of(own_key, dims, split, -0.22, 0.18) if split else 1.0
    values = jax.random.normal(own_key, dims, jnp.float32) * spread * gain
    return jnp.minimum(jnp.maximum(values, -most), most).astype(kind)


def setup_inputs(seed: int = 0) -> dict:
    splits = jax.random.split(jax.random.key(seed), 12)
    positions = jnp.clip(1.0 * jax.random.uniform(splits[0], (BEADS, 3, ATOMS), jnp.float32) ** level_of(splits[0], (BEADS, 3, ATOMS), ((0, 2), (2, 16)), -0.2, 0.2), 0.0, 1.0)
    velocities = gaussian(splits[1], (BEADS, 3, ATOMS), 0.5, 3.0, ((0, 2), (2, 16)), jnp.float32)
    charges_in = gaussian(splits[2], (BEADS, ATOMS), 0.5, 3.0, ((0, 2), (1, 16)), jnp.float32)
    species = touch_ends(jax.random.randint(splits[3], (ATOMS,), 0, SPECIES), jax.random.fold_in(splits[3], 1), 0, SPECIES - 1).astype(jnp.int32)
    neighbors = touch_ends(jax.random.randint(splits[4], (NBR, ATOMS), -RIM, RIM + 1), jax.random.fold_in(splits[4], 1), -RIM, RIM).astype(jnp.int32)
    k_index = touch_ends(jax.random.randint(splits[5], (3, KVEC), -KMAX, KMAX + 1), jax.random.fold_in(splits[5], 1), -KMAX, KMAX).astype(jnp.int32)
    kernel = jnp.clip(jnp.exp(jax.random.uniform(splits[6], (KVEC,), jnp.float32, math.log(0.1), math.log(1.0))), 0.1, 1.0)
    chi_table = jnp.clip(jax.random.uniform(splits[7], (SPECIES,), jnp.float32, -2.0, 2.0), -2.0, 2.0)
    hard_table = jnp.clip(jnp.exp(jax.random.uniform(splits[8], (SPECIES,), jnp.float32, math.log(1.0), math.log(4.0))), 1.0, 4.0)
    bond_table = jnp.clip(jax.random.uniform(splits[9], (SPECIES,), jnp.float32, 0.2, 0.8), 0.2, 0.8)
    mass_table = jnp.clip(jnp.exp(jax.random.uniform(splits[10], (SPECIES,), jnp.float32, math.log(1.0), math.log(8.0))), 1.0, 8.0)
    return dict(positions=positions, velocities=velocities, charges_in=charges_in, species=species, neighbors=neighbors, k_index=k_index, kernel=kernel, chi_table=chi_table, hard_table=hard_table, bond_table=bond_table, mass_table=mass_table)


two_pi = 2.0 * math.pi
ewald_gain = 4.0
mixing = 0.5
spring_rate = 0.5
time_step = 0.05
HIGH = lax.Precision.HIGHEST

def phase_tables(bead_pos, wave):
    angle = two_pi * (bead_pos[0][:, None] * wave[0] + bead_pos[1][:, None] * wave[1] + bead_pos[2][:, None] * wave[2])
    return (jnp.cos(angle), jnp.sin(angle))

def reference(positions, velocities, charges_in, species, neighbors, k_index, kernel, chi_table, hard_table, bond_table, mass_table):
    wave = k_index.astype(jnp.float32)
    ewald_scale = ewald_gain / math.sqrt(KVEC * ATOMS)
    onehot = (species[None, :] == jnp.arange(SPECIES, dtype=jnp.int32)[:, None]).astype(jnp.float32)

    def lookup(table):
        return lax.optimization_barrier(jnp.sum(table[:, None] * onehot, 0))
    electroneg = lookup(chi_table)
    hardness = lookup(hard_table)
    bond_term = lookup(bond_table)
    atom_mass = lookup(mass_table)
    neighbour_index = (jnp.arange(ATOMS, dtype=jnp.int32)[None, :] + neighbors) % ATOMS

    def factor_one(inputs):
        bead_pos, charge_row = inputs
        cosine, sine_part = phase_tables(bead_pos, wave)
        return jnp.stack([jnp.dot(charge_row, cosine, precision=HIGH), jnp.dot(charge_row, sine_part, precision=HIGH)], 0)

    def potential_one(inputs):
        bead_pos, pair = inputs
        cosine, sine_part = phase_tables(bead_pos, wave)
        coeff = kernel[None, :] * pair
        return jnp.dot(cosine, coeff[0], precision=HIGH) + jnp.dot(sine_part, coeff[1], precision=HIGH)

    def force_one(inputs):
        bead_pos, pair = inputs
        cosine, sine_part = phase_tables(bead_pos, wave)
        coeff = kernel[None, :] * pair
        mixed = sine_part * coeff[0][None, :] - cosine * coeff[1][None, :]
        return jnp.einsum('dk,ak->da', wave, mixed, precision=HIGH)
    charge = charges_in
    for rounds in range(QITERS):
        pair = lax.map(factor_one, (positions, charge))
        potential = ewald_scale * lax.map(potential_one, (positions, pair))
        weighted = bond_term[None, :] * charge
        neighbour_sum = lax.optimization_barrier(jnp.sum(weighted[:, neighbour_index], 1))
        relaxed = (1.0 - mixing) * charge + mixing * (-(electroneg + potential + bond_term * neighbour_sum) / hardness)
        charge = relaxed - lax.optimization_barrier(jnp.sum(relaxed, 1, keepdims=True)) / ATOMS
    pair = lax.map(factor_one, (positions, charge))
    ewald_force = two_pi * ewald_scale * charge[:, None, :] * lax.map(force_one, (positions, pair))
    laplace = 2.0 * positions - jnp.roll(positions, 1, 0) - jnp.roll(positions, -1, 0)
    acceleration = ewald_force / atom_mass[None, None, :] - spring_rate * laplace
    new_velocities = velocities + time_step * acceleration
    new_positions = positions + time_step * new_velocities
    return (new_positions, new_velocities, charge)
```

```python
import functools
import math

import jax
import jax.numpy as jnp
from jax import lax
from jax.experimental import pallas as pl
from jax.experimental.pallas import tpu as pltpu
from jax.sharding import PartitionSpec as P

KVEC = 2048
QITERS = 2
SPECIES = 8
KMAX = 8
MODES = 160

two_pi = 2.0 * math.pi
ewald_gain = 4.0
mixing = 0.5
spring_rate = 0.5
time_step = 0.05

COS = (
    0.9999999998855522,
    -19.739208743453656,
    64.93938907588092,
    -85.45665831455305,
    60.242131335932854,
    -26.404668174676782,
    7.800131403864327,
    -1.4531122801527303,
)
SIN = (
    6.2831853025115,
    -41.34170040531697,
    81.60513138577565,
    -76.70301535354703,
    42.02592698387527,
    -14.89984666196953,
    3.2381375032044204,
)

F32 = jnp.float32
BF16 = jnp.bfloat16
NT = (((1,), (1,)), ((), ()))
NN = (((1,), (0,)), ((), ()))


def horner(coeffs, x):
    value = jnp.full_like(x, coeffs[-1])
    for coeff in coeffs[-2::-1]:
        value = value * x + coeff
    return value


def turns(multiple, x):
    t = multiple * x
    t = t - jnp.floor(t + 0.5)
    square = t * t
    return horner(COS, square), t * horner(SIN, square)


def halves(x):
    high = x.astype(BF16)
    return high, (x - high.astype(F32)).astype(BF16)


def rows_of(one, two, rest):
    high, low = halves(jnp.concatenate([one, two], 0))
    rest_high = rest.astype(BF16).astype(F32)
    both = jnp.concatenate([rest_high, rest - rest_high], 0).astype(BF16)
    return jnp.concatenate([high, both, low], 0)


def product(left, high, low, dims):
    main = lax.dot_general(left, high, dims, preferred_element_type=F32)
    one = main[0:8] + main[32:40]
    two = main[8:16] + main[40:48]
    rest = main[16:24] + main[24:32]
    if low is not None:
        minor = lax.dot_general(left[0:32], low, dims, preferred_element_type=F32)
        one = one + minor[0:8]
        two = two + minor[8:16]
        rest = rest + minor[16:24]
    return one, two, rest


def pack_kernel(ranks, pos, charge, species, neighbors, out, edges):
    beads, _, width = pos.shape
    spec = species[...].astype(F32)
    near = neighbors[...].astype(F32)
    pad = jnp.zeros((3, width), F32)
    blocks = [
        jnp.concatenate([pos[b], charge[b : b + 1, :], spec, pad], 0) for b in range(beads)
    ]
    for rank in range(ranks):
        out[rank, 0:8, :] = near
        out[rank, 8:16, :] = blocks[rank % beads]
    edges[0] = pos[0]
    edges[1] = pos[beads - 1]


def weight_kernel(k_index, kernel, out):
    count = k_index.shape[1]
    k = k_index[...]
    first, second, third = k[0:1], k[1:2], k[2:3]
    flip = (first < 0) | ((first == 0) & (second < 0))
    sign = jnp.where(flip, -1, 1)
    p, q, r = sign * first, sign * second, sign * third
    wide = 16 * (p - 1)
    with_p = jnp.where(q > 0, wide + q - 1, jnp.where(q < 0, wide + 7 - q, 135 + p))
    without_p = jnp.where(q > 0, 127 + q, 144)
    mode = jnp.where(p > 0, with_p, without_p)
    at = lax.broadcasted_iota(jnp.int32, (MODES, count), 0)
    chosen = jnp.where(at == mode, 1.0, 0.0).astype(BF16)
    row = lax.broadcasted_iota(jnp.int32, (8, count), 0)
    weight = kernel[...]
    here = row + 1 == jnp.abs(r)
    even = jnp.where(here, weight, 0.0)
    odd = jnp.where(here, jnp.where(r < 0, -weight, weight), 0.0)
    zero = jnp.where((row == 0) & (r == 0), weight, 0.0)
    even, odd, zero = product(rows_of(even, odd, zero), chosen, None, NT)
    out[0:8, :] = even
    out[8:16, :] = odd
    out[16:24, :] = zero


def bead_kernel(
    scale,
    inverse_atoms,
    beads,
    rank_ref,
    got,
    weights,
    chi_table,
    hard_table,
    bond_table,
    out,
    cos_high,
    cos_low,
    sin_high,
    sin_low,
    left,
    z_cos,
    z_sin,
    charges,
):
    ranks, _, width = got.shape
    lane = lax.broadcasted_iota(jnp.int32, (8, width), 1)
    row = lax.broadcasted_iota(jnp.int32, (8, width), 0)
    multiple = (row + 1).astype(F32)
    single = jnp.where(row == 0, 1.0, 0.0)
    blank = jnp.zeros((8, width), F32)

    def at(j):
        return slice(j * width, (j + 1) * width)

    def everywhere(x):
        return jnp.broadcast_to(x, (8, width))

    def column_sum(x):
        return everywhere(jnp.sum(x, axis=0, keepdims=True))

    chi, hard, bond, charge = [], [], [], []
    for j in range(ranks):
        cx, sx = turns(multiple, got[j, 8:9, :])
        cy, sy = turns(multiple, got[j, 9:10, :])
        cz, sz = turns(multiple, got[j, 10:11, :])
        z_cos[:, at(j)] = cz
        z_sin[:, at(j)] = sz

        def keep(rows, cosine, sine):
            high, low = halves(cosine)
            cos_high[rows, at(j)] = high
            cos_low[rows, at(j)] = low
            high, low = halves(sine)
            sin_high[rows, at(j)] = high
            sin_low[rows, at(j)] = low

        for p in range(8):
            cp, sp = everywhere(cx[p : p + 1]), everywhere(sx[p : p + 1])
            cc, ss, sc, cs = cp * cy, sp * sy, sp * cy, cp * sy
            keep(
                slice(16 * p, 16 * p + 16),
                jnp.concatenate([cc - ss, cc + ss], 0),
                jnp.concatenate([sc + cs, sc - cs], 0),
            )
        keep(slice(128, 144), jnp.concatenate([cy, cx], 0), jnp.concatenate([sy, sx], 0))
        keep(
            slice(144, 160),
            jnp.concatenate([single, blank], 0),
            jnp.concatenate([blank, blank], 0),
        )
        species = everywhere(got[j, 12:13, :])
        c, h, b = blank, blank, blank
        for kind in range(SPECIES):
            this = species == float(kind)
            c = jnp.where(this, chi_table[kind], c)
            h = jnp.where(this, hard_table[kind], h)
            b = jnp.where(this, bond_table[kind], b)
        chi.append(c)
        hard.append(mixing / h)
        bond.append(b)
        charge.append(everywhere(got[j, 11:12, :]))

    even, odd, zero = weights[0:8, :], weights[8:16, :], weights[16:24, :]

    def coefficients(charge):
        for j in range(ranks):
            left[:, at(j)] = rows_of(
                charge[j] * z_cos[:, at(j)], charge[j] * z_sin[:, at(j)], charge[j] * single
            )
        t_cc, t_cs, t_c0 = product(left[...], cos_high[...], cos_low[...], NT)
        t_sc, t_ss, t_s0 = product(left[...], sin_high[...], sin_low[...], NT)
        v_cos = (even * t_cc - odd * t_ss, even * t_cs + odd * t_sc, zero * t_c0)
        v_sin = (even * t_sc + odd * t_cs, even * t_ss - odd * t_cc, zero * t_s0)
        return v_cos, v_sin

    for rounds in range(QITERS):
        v_cos, v_sin = coefficients(charge)
        from_cos = product(rows_of(*v_cos), cos_high[...], cos_low[...], NN)
        from_sin = product(rows_of(*v_sin), sin_high[...], sin_low[...], NN)
        u_c, u_s, u_0 = (a + b for a, b in zip(from_cos, from_sin))
        weighted = [b * q for b, q in zip(bond, charge)]
        relaxed = []
        total = blank
        for j in range(ranks):
            potential = scale * column_sum(
                z_cos[:, at(j)] * u_c[:, at(j)] + z_sin[:, at(j)] * u_s[:, at(j)] + u_0[:, at(j)]
            )
            before = weighted[(j - 1) % ranks]
            after = weighted[(j + 1) % ranks]
            lower = jnp.where(lane < 3 * width // 4, weighted[j], before)
            upper = jnp.where(lane >= width // 4, weighted[j], after)
            place = (lane + got[j, 0:8, :].astype(jnp.int32)) & (width - 1)
            near = jnp.where(
                lane < width // 2,
                jnp.take_along_axis(lower, place, axis=1),
                jnp.take_along_axis(upper, place, axis=1),
            )
            new = (1.0 - mixing) * charge[j] - hard[j] * (
                chi[j] + potential + bond[j] * column_sum(near)
            )
            relaxed.append(new)
            total = total + new
        mean = jnp.sum(total, axis=1, keepdims=True) * inverse_atoms
        charge = [new - mean for new in relaxed]

    for j in range(ranks):
        charges[:, at(j)] = charge[j]
    (v_cc, v_cs, v_c0), (v_sc, v_ss, v_s0) = coefficients(charge)
    mode = lax.broadcasted_iota(jnp.int32, (8, MODES), 1)
    inner = mode & 15
    wave_x = jnp.where(
        mode < 128, (mode >> 4) + 1, jnp.where((mode >= 136) & (mode < 144), mode - 135, 0)
    ).astype(F32)
    wave_y = jnp.where(
        mode < 128,
        jnp.where(inner < 8, inner + 1, 7 - inner),
        jnp.where(mode < 136, mode - 127, 0),
    ).astype(F32)
    span = beads * width
    base = pl.multiple_of((rank_ref[0] // beads) * span, span)
    own = pl.ds(base, span)
    ch, cl, sh, sl = (ref[:, own] for ref in (cos_high, cos_low, sin_high, sin_low))
    zc, zs, q = z_cos[:, own], z_sin[:, own], charges[:, own]

    def field(for_cos, for_sin):
        a = product(rows_of(*for_cos), ch, cl, NN)
        b = product(rows_of(*for_sin), sh, sl, NN)
        return (one + two for one, two in zip(a, b))

    def force(wave):
        u_c, u_s, u_0 = field(
            (-wave * v_sc, -wave * v_ss, -wave * v_s0), (wave * v_cc, wave * v_cs, wave * v_c0)
        )
        return zc * u_c + zs * u_s + u_0

    along_x = force(wave_x)
    along_y = force(wave_y)
    u_c, u_s, _ = field((v_cc, v_cs, v_c0), (v_sc, v_ss, v_s0))
    wide_multiple = jnp.broadcast_to(multiple[:, 0:1], (8, span))
    along_z = wide_multiple * (zs * u_c - zc * u_s)
    factor = (two_pi * scale) * q
    for t in range(beads):
        cut = at(t)
        fx, fy, fz = (
            factor[:, cut] * column_sum(f[:, cut]) for f in (along_x, along_y, along_z)
        )
        out[t] = jnp.where(row == 0, fx, jnp.where(row == 1, fy, jnp.where(row == 2, fz, q[:, cut])))


def move_kernel(low_at, high_at, pos, vel, got, low, high, species, mass_table, pos_out, vel_out, charge_out):
    beads, dims, width = pos.shape
    kinds = jnp.broadcast_to(species[...], (dims, width))
    mass = jnp.zeros((dims, width), F32)
    for kind in range(SPECIES):
        mass = jnp.where(kinds == kind, mass_table[kind], mass)
    for b in range(beads):
        here = pos[b]
        before = pos[b - 1] if b > 0 else low[low_at]
        after = pos[b + 1] if b < beads - 1 else high[high_at]
        laplace = 2.0 * here - before - after
        fresh = vel[b] + time_step * (got[b, 0:3, :] / mass - spring_rate * laplace)
        vel_out[b] = fresh
        pos_out[b] = here + time_step * fresh
        charge_out[b : b + 1, :] = got[b, 3:4, :]


VMEM = pl.BlockSpec(memory_space=pltpu.VMEM)
SMEM = pl.BlockSpec(memory_space=pltpu.SMEM)


def body(
    positions,
    velocities,
    charges_in,
    species,
    neighbors,
    k_index,
    kernel,
    chi_table,
    hard_table,
    bond_table,
    mass_table,
):
    beads, dims, width = positions.shape
    ranks = lax.axis_size("atoms")
    chain = lax.axis_size("beads")
    atoms = ranks * width
    scale = ewald_gain / math.sqrt(KVEC * atoms)
    kinds = species[None, :]
    shape = jax.ShapeDtypeStruct

    packed, edges = pl.pallas_call(
        functools.partial(pack_kernel, ranks),
        out_shape=(shape((ranks, 16, width), F32), shape((2, dims, width), F32)),
        in_specs=[VMEM] * 4,
        out_specs=(VMEM, VMEM),
        name="pack",
    )(positions, charges_in, kinds, neighbors)
    if chain == 2:
        low = high = lax.ppermute(edges, "beads", [(0, 1), (1, 0)])
        low_at, high_at = 1, 0
    else:
        forward = [(i, (i + 1) % chain) for i in range(chain)]
        low = lax.ppermute(edges[1:2], "beads", forward)
        high = lax.ppermute(edges[0:1], "beads", [(b, a) for a, b in forward])
        low_at, high_at = 0, 0
    got = lax.all_to_all(packed, "atoms", 0, 0, tiled=True)

    weights = pl.pallas_call(
        weight_kernel,
        out_shape=shape((24, MODES), F32),
        in_specs=[VMEM] * 2,
        out_specs=VMEM,
        name="weights",
        cost_estimate=pl.CostEstimate(flops=10**9, bytes_accessed=10**5, transcendentals=0),
    )(k_index, kernel[None, :])

    rank = lax.axis_index("atoms").astype(jnp.int32)[None]
    result = pl.pallas_call(
        functools.partial(bead_kernel, scale, 1.0 / atoms, beads),
        out_shape=shape((beads, 8, width), F32),
        in_specs=[SMEM, VMEM, VMEM, SMEM, SMEM, SMEM],
        out_specs=VMEM,
        scratch_shapes=[
            pltpu.VMEM((MODES, atoms), BF16),
            pltpu.VMEM((MODES, atoms), BF16),
            pltpu.VMEM((MODES, atoms), BF16),
            pltpu.VMEM((MODES, atoms), BF16),
            pltpu.VMEM((48, atoms), BF16),
            pltpu.VMEM((8, atoms), F32),
            pltpu.VMEM((8, atoms), F32),
            pltpu.VMEM((8, atoms), F32),
        ],
        compiler_params=pltpu.CompilerParams(vmem_limit_bytes=32 * 1024 * 1024),
        name="bead",
    )(rank, got, weights, chi_table, hard_table, bond_table)

    groups = [list(range(g, g + beads)) for g in range(0, ranks, beads)]
    home = lax.all_to_all(result, "atoms", 0, 0, axis_index_groups=groups, tiled=True)

    return pl.pallas_call(
        functools.partial(move_kernel, low_at, high_at),
        out_shape=(
            shape(positions.shape, F32),
            shape(positions.shape, F32),
            shape(charges_in.shape, F32),
        ),
        in_specs=[VMEM] * 6 + [SMEM],
        out_specs=(VMEM, VMEM, VMEM),
        name="move",
    )(positions, velocities, home, low, high, kinds, mass_table)


def solution(mesh):
    return jax.shard_map(
        body,
        mesh=mesh,
        in_specs=(
            P("beads", None, "atoms"),
            P("beads", None, "atoms"),
            P("beads", "atoms"),
            P("atoms"),
            P(None, "atoms"),
            P(),
            P(),
            P(),
            P(),
            P(),
            P(),
        ),
        out_specs=(P("beads", None, "atoms"), P("beads", None, "atoms"), P("beads", "atoms")),
        check_vma=False,
    )
```

```python
import functools
import math

import jax
import jax.numpy as jnp
from jax import lax
from jax.experimental import pallas as pl
from jax.experimental.pallas import tpu as pltpu
from jax.sharding import PartitionSpec as P

KVEC = 2048
QITERS = 2
SPECIES = 8
KMAX = 8
MODES = 160

two_pi = 2.0 * math.pi
ewald_gain = 4.0
mixing = 0.5
spring_rate = 0.5
time_step = 0.05

COS = (
    0.9999999998855522,
    -19.739208743453656,
    64.93938907588092,
    -85.45665831455305,
    60.242131335932854,
    -26.404668174676782,
    7.800131403864327,
    -1.4531122801527303,
)
SIN = (
    6.2831853025115,
    -41.34170040531697,
    81.60513138577565,
    -76.70301535354703,
    42.02592698387527,
    -14.89984666196953,
    3.2381375032044204,
)

F32 = jnp.float32
BF16 = jnp.bfloat16
NT = (((1,), (1,)), ((), ()))
NN = (((1,), (0,)), ((), ()))


def horner(coeffs, x):
    value = jnp.full_like(x, coeffs[-1])
    for coeff in coeffs[-2::-1]:
        value = value * x + coeff
    return value


def turns(multiple, x):
    t = multiple * x
    t = t - jnp.floor(t + 0.5)
    square = t * t
    return horner(COS, square), t * horner(SIN, square)


def halves(x):
    high = x.astype(BF16)
    return high, (x - high.astype(F32)).astype(BF16)


def rows_of(one, two, rest):
    high, low = halves(jnp.concatenate([one, two], 0))
    rest_high = rest.astype(BF16).astype(F32)
    both = jnp.concatenate([rest_high, rest - rest_high], 0).astype(BF16)
    return jnp.concatenate([high, both, low], 0)


def product(left, high, low, dims):
    main = lax.dot_general(left, high, dims, preferred_element_type=F32)
    one = main[0:8] + main[32:40]
    two = main[8:16] + main[40:48]
    rest = main[16:24] + main[24:32]
    if low is not None:
        minor = lax.dot_general(left[0:32], low, dims, preferred_element_type=F32)
        one = one + minor[0:8]
        two = two + minor[8:16]
        rest = rest + minor[16:24]
    return one, two, rest


def partner(me, t, count):
    if count & (count - 1) == 0:
        return me ^ abs(t)
    return (me + t + count) % count


def pack_kernel(ranks, pos, charge, species, neighbors, out):
    dims, beads, width = pos.shape
    spec = species[...].astype(F32)
    near = neighbors[...].astype(F32)
    pad = jnp.zeros((3, width), F32)
    blocks = [
        jnp.concatenate([pos[d, b : b + 1, :] for d in range(dims)] + [charge[b : b + 1, :], spec, pad], 0)
        for b in range(beads)
    ]
    for rank in range(ranks):
        out[rank, 0:8, :] = near
        out[rank, 8:16, :] = blocks[rank % beads]


def weight_kernel(k_index, kernel, pos, after, out, edges):
    del after
    dims, beads, _ = pos.shape
    for d in range(dims):
        edges[d : d + 1, :] = pos[d, 0:1, :]
        edges[dims + d : dims + d + 1, :] = pos[d, beads - 1 : beads, :]
    count = k_index.shape[1]
    k = k_index[...]
    first, second, third = k[0:1], k[1:2], k[2:3]
    flip = (first < 0) | ((first == 0) & (second < 0))
    sign = jnp.where(flip, -1, 1)
    p, q, r = sign * first, sign * second, sign * third
    wide = 16 * (p - 1)
    with_p = jnp.where(q > 0, wide + q - 1, jnp.where(q < 0, wide + 7 - q, 135 + p))
    without_p = jnp.where(q > 0, 127 + q, 144)
    mode = jnp.where(p > 0, with_p, without_p)
    at = lax.broadcasted_iota(jnp.int32, (MODES, count), 0)
    chosen = jnp.where(at == mode, 1.0, 0.0).astype(BF16)
    row = lax.broadcasted_iota(jnp.int32, (8, count), 0)
    weight = kernel[...]
    here = row + 1 == jnp.abs(r)
    even = jnp.where(here, weight, 0.0)
    odd = jnp.where(here, jnp.where(r < 0, -weight, weight), 0.0)
    zero = jnp.where((row == 0) & (r == 0), weight, 0.0)
    even, odd, zero = product(rows_of(even, odd, zero), chosen, None, NT)
    out[0:8, :] = even
    out[8:16, :] = odd
    out[16:24, :] = zero


def bead_kernel(
    scale,
    inverse_atoms,
    beads,
    rank_ref,
    got,
    weights_hbm,
    edges,
    chi_table,
    hard_table,
    bond_table,
    *refs,
):
    outs = refs[:beads]
    (
        cos_high,
        cos_low,
        sin_high,
        sin_low,
        left,
        z_cos,
        z_sin,
        charges,
        weights,
        mine,
        arrived,
    ) = refs[beads:]
    bring = pltpu.make_async_copy(weights_hbm, weights, arrived)
    bring.start()
    ranks, _, width = got.shape
    lane = lax.broadcasted_iota(jnp.int32, (8, width), 1)
    row = lax.broadcasted_iota(jnp.int32, (8, width), 0)
    multiple = (row + 1).astype(F32)
    single = jnp.where(row == 0, 1.0, 0.0)
    blank = jnp.zeros((8, width), F32)

    def at(j):
        return slice(j * width, (j + 1) * width)

    def everywhere(x):
        return jnp.broadcast_to(x, (8, width))

    def column_sum(x):
        return everywhere(jnp.sum(x, axis=0, keepdims=True))

    chi, hard, bond, charge = [], [], [], []
    for j in range(ranks):
        cx, sx = turns(multiple, got[j, 8:9, :])
        cy, sy = turns(multiple, got[j, 9:10, :])
        cz, sz = turns(multiple, got[j, 10:11, :])
        z_cos[:, at(j)] = cz
        z_sin[:, at(j)] = sz

        def keep(rows, cosine, sine):
            high, low = halves(cosine)
            cos_high[rows, at(j)] = high
            cos_low[rows, at(j)] = low
            high, low = halves(sine)
            sin_high[rows, at(j)] = high
            sin_low[rows, at(j)] = low

        for p in range(8):
            cp, sp = everywhere(cx[p : p + 1]), everywhere(sx[p : p + 1])
            cc, ss, sc, cs = cp * cy, sp * sy, sp * cy, cp * sy
            keep(
                slice(16 * p, 16 * p + 16),
                jnp.concatenate([cc - ss, cc + ss], 0),
                jnp.concatenate([sc + cs, sc - cs], 0),
            )
        keep(slice(128, 144), jnp.concatenate([cy, cx], 0), jnp.concatenate([sy, sx], 0))
        keep(
            slice(144, 160),
            jnp.concatenate([single, blank], 0),
            jnp.concatenate([blank, blank], 0),
        )
        species = everywhere(got[j, 12:13, :])
        c, h, b = blank, blank, blank
        for kind in range(SPECIES):
            this = species == float(kind)
            c = jnp.where(this, chi_table[kind], c)
            h = jnp.where(this, hard_table[kind], h)
            b = jnp.where(this, bond_table[kind], b)
        chi.append(c)
        hard.append(mixing / h)
        bond.append(b)
        charge.append(everywhere(got[j, 11:12, :]))

    bring.wait()
    even, odd, zero = weights[0:8, :], weights[8:16, :], weights[16:24, :]

    def coefficients(charge):
        for j in range(ranks):
            left[:, at(j)] = rows_of(
                charge[j] * z_cos[:, at(j)], charge[j] * z_sin[:, at(j)], charge[j] * single
            )
        t_cc, t_cs, t_c0 = product(left[...], cos_high[...], cos_low[...], NT)
        t_sc, t_ss, t_s0 = product(left[...], sin_high[...], sin_low[...], NT)
        v_cos = (even * t_cc - odd * t_ss, even * t_cs + odd * t_sc, zero * t_c0)
        v_sin = (even * t_sc + odd * t_cs, even * t_ss - odd * t_cc, zero * t_s0)
        return v_cos, v_sin

    for rounds in range(QITERS):
        v_cos, v_sin = coefficients(charge)
        from_cos = product(rows_of(*v_cos), cos_high[...], cos_low[...], NN)
        from_sin = product(rows_of(*v_sin), sin_high[...], sin_low[...], NN)
        u_c, u_s, u_0 = (a + b for a, b in zip(from_cos, from_sin))
        weighted = [b * q for b, q in zip(bond, charge)]
        relaxed = []
        total = blank
        for j in range(ranks):
            potential = scale * column_sum(
                z_cos[:, at(j)] * u_c[:, at(j)] + z_sin[:, at(j)] * u_s[:, at(j)] + u_0[:, at(j)]
            )
            before = weighted[(j - 1) % ranks]
            after = weighted[(j + 1) % ranks]
            lower = jnp.where(lane < 3 * width // 4, weighted[j], before)
            upper = jnp.where(lane >= width // 4, weighted[j], after)
            place = (lane + got[j, 0:8, :].astype(jnp.int32)) & (width - 1)
            near = jnp.where(
                lane < width // 2,
                jnp.take_along_axis(lower, place, axis=1),
                jnp.take_along_axis(upper, place, axis=1),
            )
            new = (1.0 - mixing) * charge[j] - hard[j] * (
                chi[j] + potential + bond[j] * column_sum(near)
            )
            relaxed.append(new)
            total = total + new
        mean = jnp.sum(total, axis=1, keepdims=True) * inverse_atoms
        charge = [new - mean for new in relaxed]

    for j in range(ranks):
        charges[:, at(j)] = charge[j]
    (v_cc, v_cs, v_c0), (v_sc, v_ss, v_s0) = coefficients(charge)
    mode = lax.broadcasted_iota(jnp.int32, (8, MODES), 1)
    inner = mode & 15
    wave_x = jnp.where(
        mode < 128, (mode >> 4) + 1, jnp.where((mode >= 136) & (mode < 144), mode - 135, 0)
    ).astype(F32)
    wave_y = jnp.where(
        mode < 128,
        jnp.where(inner < 8, inner + 1, 7 - inner),
        jnp.where(mode < 136, mode - 127, 0),
    ).astype(F32)
    span = beads * width
    base = pl.multiple_of((rank_ref[0] // beads) * span, span)
    own = pl.ds(base, span)
    ch, cl, sh, sl = (ref[:, own] for ref in (cos_high, cos_low, sin_high, sin_low))
    zc, zs, q = z_cos[:, own], z_sin[:, own], charges[:, own]

    def field(for_cos, for_sin):
        a = product(rows_of(*for_cos), ch, cl, NN)
        b = product(rows_of(*for_sin), sh, sl, NN)
        return (one + two for one, two in zip(a, b))

    def force(wave):
        u_c, u_s, u_0 = field(
            (-wave * v_sc, -wave * v_ss, -wave * v_s0), (wave * v_cc, wave * v_cs, wave * v_c0)
        )
        return zc * u_c + zs * u_s + u_0

    along_x = force(wave_x)
    along_y = force(wave_y)
    u_c, u_s, _ = field((v_cc, v_cs, v_c0), (v_sc, v_ss, v_s0))
    wide_multiple = jnp.broadcast_to(multiple[:, 0:1], (8, span))
    along_z = wide_multiple * (zs * u_c - zc * u_s)
    factor = (two_pi * scale) * q
    for t in range(beads):
        cut = at(t)
        fx, fy, fz = (
            factor[:, cut] * column_sum(f[:, cut]) for f in (along_x, along_y, along_z)
        )
        mine[:, cut] = jnp.where(
            row == 0, fx, jnp.where(row == 1, fy, jnp.where(row == 2, fz, q[:, cut]))
        )
    me = rank_ref[0] % beads
    for t in range(beads):
        there = pl.multiple_of(partner(me, t, beads) * width, width)
        outs[t][...] = mine[0:4, pl.ds(there, width)]


def move_kernel(low_at, high_at, rank_ref, pos, vel, low, high, species, mass_table, *refs):
    dims, beads, width = pos.shape
    got, (pos_out, vel_out, charge_out, home) = refs[:beads], refs[beads:]
    me = rank_ref[0] % beads
    for t in range(beads):
        bead = partner(me, -t, beads)
        for d in range(dims + 1):
            home[pl.ds(d * beads + bead, 1), :] = got[t][d : d + 1, :]
    kinds = jnp.broadcast_to(species[...], (beads, width))
    mass = jnp.zeros((beads, width), F32)
    for kind in range(SPECIES):
        mass = jnp.where(kinds == kind, mass_table[kind], mass)
    for d in range(dims):
        here = pos[d]
        before = jnp.concatenate([low[low_at + d : low_at + d + 1, :], here[: beads - 1]], 0)
        after = jnp.concatenate([here[1:], high[high_at + d : high_at + d + 1, :]], 0)
        laplace = 2.0 * here - before - after
        force = home[d * beads : (d + 1) * beads, :]
        fresh = vel[d] + time_step * (force / mass - spring_rate * laplace)
        vel_out[d] = fresh
        pos_out[d] = here + time_step * fresh
    charge_out[...] = home[dims * beads : (dims + 1) * beads, :]


VMEM = pl.BlockSpec(memory_space=pltpu.VMEM)
SMEM = pl.BlockSpec(memory_space=pltpu.SMEM)
ANY = pl.BlockSpec(memory_space=pl.ANY)


def body(
    positions,
    velocities,
    charges_in,
    species,
    neighbors,
    k_index,
    kernel,
    chi_table,
    hard_table,
    bond_table,
    mass_table,
):
    beads, dims, width = positions.shape
    ranks = lax.axis_size("atoms")
    chain = lax.axis_size("beads")
    atoms = ranks * width
    scale = ewald_gain / math.sqrt(KVEC * atoms)
    kinds = species[None, :]
    shape = jax.ShapeDtypeStruct

    places = positions.transpose(1, 0, 2)
    speeds = velocities.transpose(1, 0, 2)

    packed = pl.pallas_call(
        functools.partial(pack_kernel, ranks),
        out_shape=shape((ranks, 16, width), F32),
        in_specs=[VMEM] * 4,
        out_specs=VMEM,
        name="pack",
    )(places, charges_in, kinds, neighbors)
    got = lax.all_to_all(packed, "atoms", 0, 0, tiled=True)

    weights, edges = pl.pallas_call(
        weight_kernel,
        out_shape=(shape((24, MODES), F32), shape((2 * dims, width), F32)),
        in_specs=[VMEM] * 3 + [ANY],
        out_specs=(VMEM, VMEM),
        name="weights",
        cost_estimate=pl.CostEstimate(flops=10**9, bytes_accessed=10**5, transcendentals=0),
    )(k_index, kernel[None, :], places, packed)
    if chain == 2:
        low = high = lax.ppermute(edges, "beads", [(0, 1), (1, 0)])
        low_at, high_at = dims, 0
    else:
        forward = [(i, (i + 1) % chain) for i in range(chain)]
        low = lax.ppermute(edges[dims:], "beads", forward)
        high = lax.ppermute(edges[:dims], "beads", [(b, a) for a, b in forward])
        low_at, high_at = 0, 0

    rank = lax.axis_index("atoms").astype(jnp.int32)[None]
    results = pl.pallas_call(
        functools.partial(bead_kernel, scale, 1.0 / atoms, beads),
        out_shape=[shape((4, width), F32)] * beads,
        in_specs=[SMEM, VMEM, ANY, ANY, SMEM, SMEM, SMEM],
        out_specs=[VMEM] * beads,
        scratch_shapes=[
            pltpu.VMEM((MODES, atoms), BF16),
            pltpu.VMEM((MODES, atoms), BF16),
            pltpu.VMEM((MODES, atoms), BF16),
            pltpu.VMEM((MODES, atoms), BF16),
            pltpu.VMEM((48, atoms), BF16),
            pltpu.VMEM((8, atoms), F32),
            pltpu.VMEM((8, atoms), F32),
            pltpu.VMEM((8, atoms), F32),
            pltpu.VMEM((24, MODES), F32),
            pltpu.VMEM((8, beads * width), F32),
            pltpu.SemaphoreType.DMA,
        ],
        compiler_params=pltpu.CompilerParams(vmem_limit_bytes=32 * 1024 * 1024),
        name="bead",
    )(rank, got, weights, low, chi_table, hard_table, bond_table)

    home = [results[0]]
    for t in range(1, beads):
        pairs = [(r, r // beads * beads + partner(r % beads, t, beads)) for r in range(ranks)]
        home.append(lax.ppermute(results[t], "atoms", pairs))

    new_places, new_speeds, charge = pl.pallas_call(
        functools.partial(move_kernel, low_at, high_at),
        out_shape=(
            shape(places.shape, F32),
            shape(places.shape, F32),
            shape(charges_in.shape, F32),
        ),
        in_specs=[SMEM] + [VMEM] * 5 + [SMEM] + [VMEM] * beads,
        out_specs=(VMEM, VMEM, VMEM),
        scratch_shapes=[pltpu.VMEM(((dims + 1) * beads, width), F32)],
        name="move",
    )(rank, places, speeds, low, high, kinds, mass_table, *home)
    return new_places.transpose(1, 0, 2), new_speeds.transpose(1, 0, 2), charge


def solution(mesh):
    return jax.shard_map(
        body,
        mesh=mesh,
        in_specs=(
            P("beads", None, "atoms"),
            P("beads", None, "atoms"),
            P("beads", "atoms"),
            P("atoms"),
            P(None, "atoms"),
            P(),
            P(),
            P(),
            P(),
            P(),
            P(),
        ),
        out_specs=(P("beads", None, "atoms"), P("beads", None, "atoms"), P("beads", "atoms")),
        check_vma=False,
    )
```

```python
import functools
import math

import jax
import jax.numpy as jnp
from jax import lax
from jax.experimental import pallas as pl
from jax.experimental.pallas import tpu as pltpu
from jax.sharding import PartitionSpec as P

KVEC = 2048
QITERS = 2
SPECIES = 8
KMAX = 8
MODES = 160

two_pi = 2.0 * math.pi
ewald_gain = 4.0
mixing = 0.5
spring_rate = 0.5
time_step = 0.05

COS = (
    0.9999999998855522,
    -19.739208743453656,
    64.93938907588092,
    -85.45665831455305,
    60.242131335932854,
    -26.404668174676782,
    7.800131403864327,
    -1.4531122801527303,
)
SIN = (
    6.2831853025115,
    -41.34170040531697,
    81.60513138577565,
    -76.70301535354703,
    42.02592698387527,
    -14.89984666196953,
    3.2381375032044204,
)

F32 = jnp.float32
BF16 = jnp.bfloat16
NT = (((1,), (1,)), ((), ()))
NN = (((1,), (0,)), ((), ()))


def horner(coeffs, x):
    value = jnp.full_like(x, coeffs[-1])
    for coeff in coeffs[-2::-1]:
        value = value * x + coeff
    return value


def turns(multiple, x):
    t = multiple * x
    t = t - jnp.floor(t + 0.5)
    square = t * t
    return horner(COS, square), t * horner(SIN, square)


def halves(x):
    high = x.astype(BF16)
    return high, (x - high.astype(F32)).astype(BF16)


def rows_of(one, two, rest):
    high, low = halves(jnp.concatenate([one, two], 0))
    rest_high = rest.astype(BF16).astype(F32)
    both = jnp.concatenate([rest_high, rest - rest_high], 0).astype(BF16)
    return jnp.concatenate([high, both, low], 0)


def product(left, high, low, dims):
    main = lax.dot_general(left, high, dims, preferred_element_type=F32)
    one = main[0:8] + main[32:40]
    two = main[8:16] + main[40:48]
    rest = main[16:24] + main[24:32]
    if low is not None:
        minor = lax.dot_general(left[0:32], low, dims, preferred_element_type=F32)
        one = one + minor[0:8]
        two = two + minor[8:16]
        rest = rest + minor[16:24]
    return one, two, rest


def partner(me, t, count):
    if count & (count - 1) == 0:
        return me ^ abs(t)
    return (me + t + count) % count


def lookup(tables, kinds):
    found = [jnp.zeros(kinds.shape, F32) for _ in tables]
    for kind in range(SPECIES):
        here = kinds == kind
        found = [jnp.where(here, table[kind], x) for table, x in zip(tables, found)]
    return found


def pack_kernel(ranks, pos, charge, species, neighbors, chi_table, hard_table, bond_table, out):
    dims, beads, width = pos.shape
    near = neighbors[...].astype(F32)
    chi, hard, bond = lookup((chi_table, hard_table, bond_table), species[...])
    shared = [chi, mixing / hard, bond, jnp.zeros((1, width), F32)]
    for b in range(beads):
        own = [pos[d, b : b + 1, :] for d in range(dims)] + [charge[b : b + 1, :]]
        block = jnp.concatenate(own + shared, 0)
        for rank in range(b, ranks, beads):
            out[rank, 0:8, :] = near
            out[rank, 8:16, :] = block


def weight_kernel(k_index, kernel, pos, after, out, edges):
    del after
    dims, beads, _ = pos.shape
    for d in range(dims):
        edges[d : d + 1, :] = pos[d, 0:1, :]
        edges[dims + d : dims + d + 1, :] = pos[d, beads - 1 : beads, :]
    count = k_index.shape[1]
    k = k_index[...]
    first, second, third = k[0:1], k[1:2], k[2:3]
    flip = (first < 0) | ((first == 0) & (second < 0))
    sign = jnp.where(flip, -1, 1)
    p, q, r = sign * first, sign * second, sign * third
    wide = 16 * (p - 1)
    with_p = jnp.where(q > 0, wide + q - 1, jnp.where(q < 0, wide + 7 - q, 135 + p))
    without_p = jnp.where(q > 0, 127 + q, 144)
    mode = jnp.where(p > 0, with_p, without_p)
    at = lax.broadcasted_iota(jnp.int32, (MODES, count), 0)
    chosen = jnp.where(at == mode, 1.0, 0.0).astype(BF16)
    row = lax.broadcasted_iota(jnp.int32, (8, count), 0)
    weight = kernel[...]
    here = row + 1 == jnp.abs(r)
    even = jnp.where(here, weight, 0.0)
    odd = jnp.where(here, jnp.where(r < 0, -weight, weight), 0.0)
    zero = jnp.where((row == 0) & (r == 0), weight, 0.0)
    even, odd, zero = product(rows_of(even, odd, zero), chosen, None, NT)
    out[0:8, :] = even
    out[8:16, :] = odd
    out[16:24, :] = zero


def bead_kernel(
    scale,
    inverse_atoms,
    beads,
    rank_ref,
    got,
    weights_hbm,
    *refs,
):
    outs = refs[:beads]
    (
        cos_high,
        cos_low,
        sin_high,
        sin_low,
        left,
        z_cos,
        z_sin,
        charges,
        weights,
        mine,
        arrived,
    ) = refs[beads:]
    bring = pltpu.make_async_copy(weights_hbm, weights, arrived)
    bring.start()
    ranks, _, width = got.shape
    lane = lax.broadcasted_iota(jnp.int32, (8, width), 1)
    row = lax.broadcasted_iota(jnp.int32, (8, width), 0)
    multiple = (row + 1).astype(F32)
    single = jnp.where(row == 0, 1.0, 0.0)
    blank = jnp.zeros((8, width), F32)

    def at(j):
        return slice(j * width, (j + 1) * width)

    def everywhere(x):
        return jnp.broadcast_to(x, (8, width))

    def column_sum(x):
        return everywhere(jnp.sum(x, axis=0, keepdims=True))

    chi, hard, bond, charge = [], [], [], []
    for j in range(ranks):
        cx, sx = turns(multiple, got[j, 8:9, :])
        cy, sy = turns(multiple, got[j, 9:10, :])
        cz, sz = turns(multiple, got[j, 10:11, :])
        z_cos[:, at(j)] = cz
        z_sin[:, at(j)] = sz

        def keep(rows, cosine, sine):
            high, low = halves(cosine)
            cos_high[rows, at(j)] = high
            cos_low[rows, at(j)] = low
            high, low = halves(sine)
            sin_high[rows, at(j)] = high
            sin_low[rows, at(j)] = low

        for p in range(8):
            cp, sp = everywhere(cx[p : p + 1]), everywhere(sx[p : p + 1])
            cc, ss, sc, cs = cp * cy, sp * sy, sp * cy, cp * sy
            keep(
                slice(16 * p, 16 * p + 16),
                jnp.concatenate([cc - ss, cc + ss], 0),
                jnp.concatenate([sc + cs, sc - cs], 0),
            )
        keep(slice(128, 144), jnp.concatenate([cy, cx], 0), jnp.concatenate([sy, sx], 0))
        keep(
            slice(144, 160),
            jnp.concatenate([single, blank], 0),
            jnp.concatenate([blank, blank], 0),
        )
        charge.append(everywhere(got[j, 11:12, :]))
        chi.append(everywhere(got[j, 12:13, :]))
        hard.append(everywhere(got[j, 13:14, :]))
        bond.append(everywhere(got[j, 14:15, :]))

    bring.wait()
    even, odd, zero = weights[0:8, :], weights[8:16, :], weights[16:24, :]

    def coefficients(charge):
        for j in range(ranks):
            left[:, at(j)] = rows_of(
                charge[j] * z_cos[:, at(j)], charge[j] * z_sin[:, at(j)], charge[j] * single
            )
        t_cc, t_cs, t_c0 = product(left[...], cos_high[...], cos_low[...], NT)
        t_sc, t_ss, t_s0 = product(left[...], sin_high[...], sin_low[...], NT)
        v_cos = (even * t_cc - odd * t_ss, even * t_cs + odd * t_sc, zero * t_c0)
        v_sin = (even * t_sc + odd * t_cs, even * t_ss - odd * t_cc, zero * t_s0)
        return v_cos, v_sin

    for rounds in range(QITERS):
        v_cos, v_sin = coefficients(charge)
        from_cos = product(rows_of(*v_cos), cos_high[...], cos_low[...], NN)
        from_sin = product(rows_of(*v_sin), sin_high[...], sin_low[...], NN)
        u_c, u_s, u_0 = (a + b for a, b in zip(from_cos, from_sin))
        weighted = [b * q for b, q in zip(bond, charge)]
        relaxed = []
        total = blank
        for j in range(ranks):
            potential = scale * column_sum(
                z_cos[:, at(j)] * u_c[:, at(j)] + z_sin[:, at(j)] * u_s[:, at(j)] + u_0[:, at(j)]
            )
            before = weighted[(j - 1) % ranks]
            after = weighted[(j + 1) % ranks]
            lower = jnp.where(lane < 3 * width // 4, weighted[j], before)
            upper = jnp.where(lane >= width // 4, weighted[j], after)
            place = (lane + got[j, 0:8, :].astype(jnp.int32)) & (width - 1)
            near = jnp.where(
                lane < width // 2,
                jnp.take_along_axis(lower, place, axis=1),
                jnp.take_along_axis(upper, place, axis=1),
            )
            new = (1.0 - mixing) * charge[j] - hard[j] * (
                chi[j] + potential + bond[j] * column_sum(near)
            )
            relaxed.append(new)
            total = total + new
        mean = jnp.sum(total, axis=1, keepdims=True) * inverse_atoms
        charge = [new - mean for new in relaxed]

    for j in range(ranks):
        charges[:, at(j)] = charge[j]
    (v_cc, v_cs, v_c0), (v_sc, v_ss, v_s0) = coefficients(charge)
    mode = lax.broadcasted_iota(jnp.int32, (8, MODES), 1)
    inner = mode & 15
    wave_x = jnp.where(
        mode < 128, (mode >> 4) + 1, jnp.where((mode >= 136) & (mode < 144), mode - 135, 0)
    ).astype(F32)
    wave_y = jnp.where(
        mode < 128,
        jnp.where(inner < 8, inner + 1, 7 - inner),
        jnp.where(mode < 136, mode - 127, 0),
    ).astype(F32)
    span = beads * width
    base = pl.multiple_of((rank_ref[0] // beads) * span, span)
    own = pl.ds(base, span)
    ch, cl, sh, sl = (ref[:, own] for ref in (cos_high, cos_low, sin_high, sin_low))
    zc, zs, q = z_cos[:, own], z_sin[:, own], charges[:, own]

    def field(for_cos, for_sin):
        a = product(rows_of(*for_cos), ch, cl, NN)
        b = product(rows_of(*for_sin), sh, sl, NN)
        return (one + two for one, two in zip(a, b))

    def force(wave):
        u_c, u_s, u_0 = field(
            (-wave * v_sc, -wave * v_ss, -wave * v_s0), (wave * v_cc, wave * v_cs, wave * v_c0)
        )
        return zc * u_c + zs * u_s + u_0

    along_x = force(wave_x)
    along_y = force(wave_y)
    u_c, u_s, _ = field((v_cc, v_cs, v_c0), (v_sc, v_ss, v_s0))
    wide_multiple = jnp.broadcast_to(multiple[:, 0:1], (8, span))
    along_z = wide_multiple * (zs * u_c - zc * u_s)
    factor = (two_pi * scale) * q
    for t in range(beads):
        cut = at(t)
        fx, fy, fz = (
            factor[:, cut] * column_sum(f[:, cut]) for f in (along_x, along_y, along_z)
        )
        mine[:, cut] = jnp.where(
            row == 0, fx, jnp.where(row == 1, fy, jnp.where(row == 2, fz, q[:, cut]))
        )
    me = rank_ref[0] % beads
    for t in range(beads):
        there = pl.multiple_of(partner(me, t, beads) * width, width)
        outs[t][...] = mine[0:4, pl.ds(there, width)]


def move_kernel(low_at, high_at, rank_ref, pos, vel, low, high, species, mass_table, *refs):
    dims, beads, width = pos.shape
    got, (pos_out, vel_out, charge_out, home) = refs[:beads], refs[beads:]
    me = rank_ref[0] % beads
    for t in range(beads):
        bead = partner(me, -t, beads)
        for d in range(dims + 1):
            home[pl.ds(d * beads + bead, 1), :] = got[t][d : d + 1, :]
    (mass,) = lookup((mass_table,), jnp.broadcast_to(species[...], (beads, width)))
    for d in range(dims):
        here = pos[d]
        before = jnp.concatenate([low[low_at + d : low_at + d + 1, :], here[: beads - 1]], 0)
        after = jnp.concatenate([here[1:], high[high_at + d : high_at + d + 1, :]], 0)
        laplace = 2.0 * here - before - after
        force = home[d * beads : (d + 1) * beads, :]
        fresh = vel[d] + time_step * (force / mass - spring_rate * laplace)
        vel_out[d] = fresh
        pos_out[d] = here + time_step * fresh
    charge_out[...] = home[dims * beads : (dims + 1) * beads, :]


VMEM = pl.BlockSpec(memory_space=pltpu.VMEM)
SMEM = pl.BlockSpec(memory_space=pltpu.SMEM)
ANY = pl.BlockSpec(memory_space=pl.ANY)


def params(mebibytes):
    return pltpu.CompilerParams(vmem_limit_bytes=mebibytes << 20)


def body(
    positions,
    velocities,
    charges_in,
    species,
    neighbors,
    k_index,
    kernel,
    chi_table,
    hard_table,
    bond_table,
    mass_table,
):
    beads, dims, width = positions.shape
    ranks = lax.axis_size("atoms")
    chain = lax.axis_size("beads")
    atoms = ranks * width
    scale = ewald_gain / math.sqrt(KVEC * atoms)
    kinds = species[None, :]
    shape = jax.ShapeDtypeStruct

    places = positions.transpose(1, 0, 2)
    speeds = velocities.transpose(1, 0, 2)

    packed = pl.pallas_call(
        functools.partial(pack_kernel, ranks),
        out_shape=shape((ranks, 16, width), F32),
        in_specs=[VMEM] * 4 + [SMEM] * 3,
        out_specs=VMEM,
        compiler_params=params(4),
        name="pack",
    )(places, charges_in, kinds, neighbors, chi_table, hard_table, bond_table)
    got = lax.all_to_all(packed, "atoms", 0, 0, tiled=True)

    weights, edges = pl.pallas_call(
        weight_kernel,
        out_shape=(shape((24, MODES), F32), shape((2 * dims, width), F32)),
        in_specs=[VMEM] * 3 + [ANY],
        out_specs=(VMEM, VMEM),
        compiler_params=params(8),
        name="weights",
        cost_estimate=pl.CostEstimate(flops=10**9, bytes_accessed=10**5, transcendentals=0),
    )(k_index, kernel[None, :], places, packed)
    if chain == 2:
        low = high = lax.ppermute(edges, "beads", [(0, 1), (1, 0)])
        low_at, high_at = dims, 0
    else:
        forward = [(i, (i + 1) % chain) for i in range(chain)]
        low = lax.ppermute(edges[dims:], "beads", forward)
        high = lax.ppermute(edges[:dims], "beads", [(b, a) for a, b in forward])
        low_at, high_at = 0, 0

    rank = lax.axis_index("atoms").astype(jnp.int32)[None]
    results = pl.pallas_call(
        functools.partial(bead_kernel, scale, 1.0 / atoms, beads),
        out_shape=[shape((4, width), F32)] * beads,
        in_specs=[SMEM, VMEM, ANY],
        out_specs=[VMEM] * beads,
        scratch_shapes=[
            pltpu.VMEM((MODES, atoms), BF16),
            pltpu.VMEM((MODES, atoms), BF16),
            pltpu.VMEM((MODES, atoms), BF16),
            pltpu.VMEM((MODES, atoms), BF16),
            pltpu.VMEM((48, atoms), BF16),
            pltpu.VMEM((8, atoms), F32),
            pltpu.VMEM((8, atoms), F32),
            pltpu.VMEM((8, atoms), F32),
            pltpu.VMEM((24, MODES), F32),
            pltpu.VMEM((8, beads * width), F32),
            pltpu.SemaphoreType.DMA,
        ],
        compiler_params=params(24),
        name="bead",
        cost_estimate=pl.CostEstimate(flops=10**10, bytes_accessed=10**6, transcendentals=0),
    )(rank, got, weights)

    home = [results[0]]
    for t in range(1, beads):
        pairs = [(r, r // beads * beads + partner(r % beads, t, beads)) for r in range(ranks)]
        home.append(lax.ppermute(results[t], "atoms", pairs))

    new_places, new_speeds, charge = pl.pallas_call(
        functools.partial(move_kernel, low_at, high_at),
        out_shape=(
            shape(places.shape, F32),
            shape(places.shape, F32),
            shape(charges_in.shape, F32),
        ),
        in_specs=[SMEM] + [VMEM] * 5 + [SMEM] + [VMEM] * beads,
        out_specs=(VMEM, VMEM, VMEM),
        scratch_shapes=[pltpu.VMEM(((dims + 1) * beads, width), F32)],
        compiler_params=params(4),
        name="move",
    )(rank, places, speeds, low, high, kinds, mass_table, *home)
    return new_places.transpose(1, 0, 2), new_speeds.transpose(1, 0, 2), charge


def solution(mesh):
    return jax.shard_map(
        body,
        mesh=mesh,
        in_specs=(
            P("beads", None, "atoms"),
            P("beads", None, "atoms"),
            P("beads", "atoms"),
            P("atoms"),
            P(None, "atoms"),
            P(),
            P(),
            P(),
            P(),
            P(),
            P(),
        ),
        out_specs=(P("beads", None, "atoms"), P("beads", None, "atoms"), P("beads", "atoms")),
        check_vma=False,
    )
```

```python
import functools
import math

import jax
import jax.numpy as jnp
from jax import lax
from jax.experimental import pallas as pl
from jax.experimental.pallas import tpu as pltpu
from jax.sharding import PartitionSpec as P

KVEC = 2048
QITERS = 2
SPECIES = 8
KMAX = 8
MODES = 160

two_pi = 2.0 * math.pi
ewald_gain = 4.0
mixing = 0.5
spring_rate = 0.5
time_step = 0.05

COS = (
    0.9999999998855522,
    -19.739208743453656,
    64.93938907588092,
    -85.45665831455305,
    60.242131335932854,
    -26.404668174676782,
    7.800131403864327,
    -1.4531122801527303,
)
SIN = (
    6.2831853025115,
    -41.34170040531697,
    81.60513138577565,
    -76.70301535354703,
    42.02592698387527,
    -14.89984666196953,
    3.2381375032044204,
)

F32 = jnp.float32
BF16 = jnp.bfloat16
NT = (((1,), (1,)), ((), ()))
NN = (((1,), (0,)), ((), ()))


def horner(coeffs, x):
    value = jnp.full_like(x, coeffs[-1])
    for coeff in coeffs[-2::-1]:
        value = value * x + coeff
    return value


def turns(multiple, x):
    t = multiple * x
    t = t - jnp.floor(t + 0.5)
    square = t * t
    return horner(COS, square), t * horner(SIN, square)


def halves(x):
    high = x.astype(BF16)
    return high, (x - high.astype(F32)).astype(BF16)


def rows_of(one, two, rest):
    high, low = halves(jnp.concatenate([one, two], 0))
    rest_high = rest.astype(BF16).astype(F32)
    both = jnp.concatenate([rest_high, rest - rest_high], 0).astype(BF16)
    return jnp.concatenate([high, both, low], 0)


def product(left, high, low, dims):
    main = lax.dot_general(left, high, dims, preferred_element_type=F32)
    one = main[0:8] + main[32:40]
    two = main[8:16] + main[40:48]
    rest = main[16:24] + main[24:32]
    if low is not None:
        minor = lax.dot_general(left[0:32], low, dims, preferred_element_type=F32)
        one = one + minor[0:8]
        two = two + minor[8:16]
        rest = rest + minor[16:24]
    return one, two, rest


def partner(me, t, count):
    if count & (count - 1) == 0:
        return me ^ abs(t)
    return (me + t + count) % count


def lookup(tables, kinds):
    found = [jnp.zeros(kinds.shape, F32) for _ in tables]
    for kind in range(SPECIES):
        here = kinds == kind
        found = [jnp.where(here, table[kind], x) for table, x in zip(tables, found)]
    return found


def pack_kernel(ranks, pos, charge, species, neighbors, chi_table, hard_table, bond_table, out):
    dims, beads, width = pos.shape
    near = neighbors[...].astype(F32)
    chi, hard, bond = lookup((chi_table, hard_table, bond_table), species[...])
    shared = [chi, mixing / hard, bond, jnp.zeros((1, width), F32)]
    for b in range(beads):
        own = [pos[d, b : b + 1, :] for d in range(dims)] + [charge[b : b + 1, :]]
        block = jnp.concatenate(own + shared, 0)
        for rank in range(b, ranks, beads):
            out[rank, 0:8, :] = near
            out[rank, 8:16, :] = block


def weight_kernel(k_index, kernel, pos, species, mass_table, after, out, edges, pull):
    del after
    (mass,) = lookup((mass_table,), species[...])
    pull[...] = time_step / mass
    dims, beads, _ = pos.shape
    for d in range(dims):
        edges[d : d + 1, :] = pos[d, 0:1, :]
        edges[dims + d : dims + d + 1, :] = pos[d, beads - 1 : beads, :]
    count = k_index.shape[1]
    k = k_index[...]
    first, second, third = k[0:1], k[1:2], k[2:3]
    flip = (first < 0) | ((first == 0) & (second < 0))
    sign = jnp.where(flip, -1, 1)
    p, q, r = sign * first, sign * second, sign * third
    wide = 16 * (p - 1)
    with_p = jnp.where(q > 0, wide + q - 1, jnp.where(q < 0, wide + 7 - q, 135 + p))
    without_p = jnp.where(q > 0, 127 + q, 144)
    mode = jnp.where(p > 0, with_p, without_p)
    at = lax.broadcasted_iota(jnp.int32, (MODES, count), 0)
    chosen = jnp.where(at == mode, 1.0, 0.0).astype(BF16)
    row = lax.broadcasted_iota(jnp.int32, (8, count), 0)
    weight = kernel[...]
    here = row + 1 == jnp.abs(r)
    even = jnp.where(here, weight, 0.0)
    odd = jnp.where(here, jnp.where(r < 0, -weight, weight), 0.0)
    zero = jnp.where((row == 0) & (r == 0), weight, 0.0)
    even, odd, zero = product(rows_of(even, odd, zero), chosen, None, NT)
    out[0:8, :] = even
    out[8:16, :] = odd
    out[16:24, :] = zero


def bead_kernel(
    scale,
    inverse_atoms,
    beads,
    rank_ref,
    got,
    weights_hbm,
    *refs,
):
    outs = refs[:beads]
    (
        cos_high,
        cos_low,
        sin_high,
        sin_low,
        left,
        z_cos,
        z_sin,
        charges,
        weights,
        mine,
        arrived,
    ) = refs[beads:]
    bring = pltpu.make_async_copy(weights_hbm, weights, arrived)
    bring.start()
    ranks, _, width = got.shape
    lane = lax.broadcasted_iota(jnp.int32, (8, width), 1)
    row = lax.broadcasted_iota(jnp.int32, (8, width), 0)
    multiple = (row + 1).astype(F32)
    single = jnp.where(row == 0, 1.0, 0.0)
    blank = jnp.zeros((8, width), F32)

    def at(j):
        return slice(j * width, (j + 1) * width)

    def everywhere(x):
        return jnp.broadcast_to(x, (8, width))

    def column_sum(x):
        return everywhere(jnp.sum(x, axis=0, keepdims=True))

    chi, hard, bond, charge = [], [], [], []
    for j in range(ranks):
        cx, sx = turns(multiple, got[j, 8:9, :])
        cy, sy = turns(multiple, got[j, 9:10, :])
        cz, sz = turns(multiple, got[j, 10:11, :])
        z_cos[:, at(j)] = cz
        z_sin[:, at(j)] = sz

        def keep(rows, cosine, sine):
            high, low = halves(cosine)
            cos_high[rows, at(j)] = high
            cos_low[rows, at(j)] = low
            high, low = halves(sine)
            sin_high[rows, at(j)] = high
            sin_low[rows, at(j)] = low

        for p in range(8):
            cp, sp = everywhere(cx[p : p + 1]), everywhere(sx[p : p + 1])
            cc, ss, sc, cs = cp * cy, sp * sy, sp * cy, cp * sy
            keep(
                slice(16 * p, 16 * p + 16),
                jnp.concatenate([cc - ss, cc + ss], 0),
                jnp.concatenate([sc + cs, sc - cs], 0),
            )
        keep(slice(128, 144), jnp.concatenate([cy, cx], 0), jnp.concatenate([sy, sx], 0))
        keep(
            slice(144, 160),
            jnp.concatenate([single, blank], 0),
            jnp.concatenate([blank, blank], 0),
        )
        charge.append(everywhere(got[j, 11:12, :]))
        chi.append(everywhere(got[j, 12:13, :]))
        hard.append(everywhere(got[j, 13:14, :]))
        bond.append(everywhere(got[j, 14:15, :]))

    bring.wait()
    even, odd, zero = weights[0:8, :], weights[8:16, :], weights[16:24, :]

    def coefficients(charge):
        for j in range(ranks):
            left[:, at(j)] = rows_of(
                charge[j] * z_cos[:, at(j)], charge[j] * z_sin[:, at(j)], charge[j] * single
            )
        t_cc, t_cs, t_c0 = product(left[...], cos_high[...], cos_low[...], NT)
        t_sc, t_ss, t_s0 = product(left[...], sin_high[...], sin_low[...], NT)
        v_cos = (even * t_cc - odd * t_ss, even * t_cs + odd * t_sc, zero * t_c0)
        v_sin = (even * t_sc + odd * t_cs, even * t_ss - odd * t_cc, zero * t_s0)
        return v_cos, v_sin

    for rounds in range(QITERS):
        v_cos, v_sin = coefficients(charge)
        from_cos = product(rows_of(*v_cos), cos_high[...], cos_low[...], NN)
        from_sin = product(rows_of(*v_sin), sin_high[...], sin_low[...], NN)
        u_c, u_s, u_0 = (a + b for a, b in zip(from_cos, from_sin))
        weighted = [b * q for b, q in zip(bond, charge)]
        relaxed = []
        total = blank
        for j in range(ranks):
            potential = scale * column_sum(
                z_cos[:, at(j)] * u_c[:, at(j)] + z_sin[:, at(j)] * u_s[:, at(j)] + u_0[:, at(j)]
            )
            before = weighted[(j - 1) % ranks]
            after = weighted[(j + 1) % ranks]
            lower = jnp.where(lane < 3 * width // 4, weighted[j], before)
            upper = jnp.where(lane >= width // 4, weighted[j], after)
            place = (lane + got[j, 0:8, :].astype(jnp.int32)) & (width - 1)
            near = jnp.where(
                lane < width // 2,
                jnp.take_along_axis(lower, place, axis=1),
                jnp.take_along_axis(upper, place, axis=1),
            )
            new = (1.0 - mixing) * charge[j] - hard[j] * (
                chi[j] + potential + bond[j] * column_sum(near)
            )
            relaxed.append(new)
            total = total + new
        mean = jnp.sum(total, axis=1, keepdims=True) * inverse_atoms
        charge = [new - mean for new in relaxed]

    for j in range(ranks):
        charges[:, at(j)] = charge[j]
    (v_cc, v_cs, v_c0), (v_sc, v_ss, v_s0) = coefficients(charge)
    mode = lax.broadcasted_iota(jnp.int32, (8, MODES), 1)
    inner = mode & 15
    wave_x = jnp.where(
        mode < 128, (mode >> 4) + 1, jnp.where((mode >= 136) & (mode < 144), mode - 135, 0)
    ).astype(F32)
    wave_y = jnp.where(
        mode < 128,
        jnp.where(inner < 8, inner + 1, 7 - inner),
        jnp.where(mode < 136, mode - 127, 0),
    ).astype(F32)
    span = beads * width
    base = pl.multiple_of((rank_ref[0] // beads) * span, span)
    own = pl.ds(base, span)
    ch, cl, sh, sl = (ref[:, own] for ref in (cos_high, cos_low, sin_high, sin_low))
    zc, zs, q = z_cos[:, own], z_sin[:, own], charges[:, own]

    def field(for_cos, for_sin):
        a = product(rows_of(*for_cos), ch, cl, NN)
        b = product(rows_of(*for_sin), sh, sl, NN)
        return (one + two for one, two in zip(a, b))

    def force(wave):
        u_c, u_s, u_0 = field(
            (-wave * v_sc, -wave * v_ss, -wave * v_s0), (wave * v_cc, wave * v_cs, wave * v_c0)
        )
        return zc * u_c + zs * u_s + u_0

    along_x = force(wave_x)
    along_y = force(wave_y)
    u_c, u_s, _ = field((v_cc, v_cs, v_c0), (v_sc, v_ss, v_s0))
    wide_multiple = jnp.broadcast_to(multiple[:, 0:1], (8, span))
    along_z = wide_multiple * (zs * u_c - zc * u_s)
    factor = (two_pi * scale) * q
    for t in range(beads):
        cut = at(t)
        fx, fy, fz = (
            factor[:, cut] * column_sum(f[:, cut]) for f in (along_x, along_y, along_z)
        )
        mine[:, cut] = jnp.where(
            row == 0, fx, jnp.where(row == 1, fy, jnp.where(row == 2, fz, q[:, cut]))
        )
    me = rank_ref[0] % beads
    for t in range(beads):
        there = pl.multiple_of(partner(me, t, beads) * width, width)
        outs[t][...] = mine[0:4, pl.ds(there, width)]


def move_kernel(low_at, high_at, rank_ref, pos, vel, low, high, pull, *refs):
    dims, beads, width = pos.shape
    got, (pos_out, vel_out, charge_out, home) = refs[:beads], refs[beads:]
    me = rank_ref[0] % beads
    for t in range(beads):
        bead = partner(me, -t, beads)
        for d in range(dims + 1):
            home[pl.ds(d * beads + bead, 1), :] = got[t][d : d + 1, :]
    gain = jnp.broadcast_to(pull[...], (beads, width))
    for d in range(dims):
        here = pos[d]
        before = jnp.concatenate([low[low_at + d : low_at + d + 1, :], here[: beads - 1]], 0)
        after = jnp.concatenate([here[1:], high[high_at + d : high_at + d + 1, :]], 0)
        laplace = 2.0 * here - before - after
        force = home[d * beads : (d + 1) * beads, :]
        fresh = vel[d] + (gain * force - (time_step * spring_rate) * laplace)
        vel_out[d] = fresh
        pos_out[d] = here + time_step * fresh
    charge_out[...] = home[dims * beads : (dims + 1) * beads, :]


VMEM = pl.BlockSpec(memory_space=pltpu.VMEM)
SMEM = pl.BlockSpec(memory_space=pltpu.SMEM)
ANY = pl.BlockSpec(memory_space=pl.ANY)


def params(mebibytes):
    return pltpu.CompilerParams(vmem_limit_bytes=mebibytes << 20)


def body(
    positions,
    velocities,
    charges_in,
    species,
    neighbors,
    k_index,
    kernel,
    chi_table,
    hard_table,
    bond_table,
    mass_table,
):
    beads, dims, width = positions.shape
    ranks = lax.axis_size("atoms")
    chain = lax.axis_size("beads")
    atoms = ranks * width
    scale = ewald_gain / math.sqrt(KVEC * atoms)
    kinds = species[None, :]
    shape = jax.ShapeDtypeStruct

    places = positions.transpose(1, 0, 2)
    speeds = velocities.transpose(1, 0, 2)

    packed = pl.pallas_call(
        functools.partial(pack_kernel, ranks),
        out_shape=shape((ranks, 16, width), F32),
        in_specs=[VMEM] * 4 + [SMEM] * 3,
        out_specs=VMEM,
        name="pack",
    )(places, charges_in, kinds, neighbors, chi_table, hard_table, bond_table)
    got = lax.all_to_all(packed, "atoms", 0, 0, tiled=True)

    weights, edges, pull = pl.pallas_call(
        weight_kernel,
        out_shape=(
            shape((24, MODES), F32),
            shape((2 * dims, width), F32),
            shape((1, width), F32),
        ),
        in_specs=[VMEM] * 4 + [SMEM, ANY],
        out_specs=(VMEM, VMEM, VMEM),
        compiler_params=params(8),
        name="weights",
        cost_estimate=pl.CostEstimate(flops=10**9, bytes_accessed=10**5, transcendentals=0),
    )(k_index, kernel[None, :], places, kinds, mass_table, packed)
    if chain == 2:
        low = high = lax.ppermute(edges, "beads", [(0, 1), (1, 0)])
        low_at, high_at = dims, 0
    else:
        forward = [(i, (i + 1) % chain) for i in range(chain)]
        low = lax.ppermute(edges[dims:], "beads", forward)
        high = lax.ppermute(edges[:dims], "beads", [(b, a) for a, b in forward])
        low_at, high_at = 0, 0

    rank = lax.axis_index("atoms").astype(jnp.int32)[None]
    results = pl.pallas_call(
        functools.partial(bead_kernel, scale, 1.0 / atoms, beads),
        out_shape=[shape((4, width), F32)] * beads,
        in_specs=[SMEM, VMEM, ANY],
        out_specs=[VMEM] * beads,
        scratch_shapes=[
            pltpu.VMEM((MODES, atoms), BF16),
            pltpu.VMEM((MODES, atoms), BF16),
            pltpu.VMEM((MODES, atoms), BF16),
            pltpu.VMEM((MODES, atoms), BF16),
            pltpu.VMEM((48, atoms), BF16),
            pltpu.VMEM((8, atoms), F32),
            pltpu.VMEM((8, atoms), F32),
            pltpu.VMEM((8, atoms), F32),
            pltpu.VMEM((24, MODES), F32),
            pltpu.VMEM((8, beads * width), F32),
            pltpu.SemaphoreType.DMA,
        ],
        compiler_params=params(24),
        name="bead",
        cost_estimate=pl.CostEstimate(flops=10**10, bytes_accessed=10**6, transcendentals=0),
    )(rank, got, weights)

    home = [results[0]]
    for t in range(1, beads):
        pairs = [(r, r // beads * beads + partner(r % beads, t, beads)) for r in range(ranks)]
        home.append(lax.ppermute(results[t], "atoms", pairs))

    new_places, new_speeds, charge = pl.pallas_call(
        functools.partial(move_kernel, low_at, high_at),
        out_shape=(
            shape(places.shape, F32),
            shape(places.shape, F32),
            shape(charges_in.shape, F32),
        ),
        in_specs=[SMEM] + [VMEM] * (5 + beads),
        out_specs=(VMEM, VMEM, VMEM),
        scratch_shapes=[pltpu.VMEM(((dims + 1) * beads, width), F32)],
        compiler_params=params(4),
        name="move",
    )(rank, places, speeds, low, high, pull, *home)
    return new_places.transpose(1, 0, 2), new_speeds.transpose(1, 0, 2), charge


def solution(mesh):
    return jax.shard_map(
        body,
        mesh=mesh,
        in_specs=(
            P("beads", None, "atoms"),
            P("beads", None, "atoms"),
            P("beads", "atoms"),
            P("atoms"),
            P(None, "atoms"),
            P(),
            P(),
            P(),
            P(),
            P(),
            P(),
        ),
        out_specs=(P("beads", None, "atoms"), P("beads", None, "atoms"), P("beads", "atoms")),
        check_vma=False,
    )
```

```python
import functools
import math

import jax
import jax.numpy as jnp
from jax import lax
from jax.experimental import pallas as pl
from jax.experimental.pallas import tpu as pltpu
from jax.sharding import PartitionSpec as P

KVEC = 2048
QITERS = 2
SPECIES = 8
KMAX = 8
MODES = 160

two_pi = 2.0 * math.pi
ewald_gain = 4.0
mixing = 0.5
spring_rate = 0.5
time_step = 0.05

COS = (
    0.9999999998855522,
    -19.739208743453656,
    64.93938907588092,
    -85.45665831455305,
    60.242131335932854,
    -26.404668174676782,
    7.800131403864327,
    -1.4531122801527303,
)
SIN = (
    6.2831853025115,
    -41.34170040531697,
    81.60513138577565,
    -76.70301535354703,
    42.02592698387527,
    -14.89984666196953,
    3.2381375032044204,
)

F32 = jnp.float32
BF16 = jnp.bfloat16
NT = (((1,), (1,)), ((), ()))
NN = (((1,), (0,)), ((), ()))


def horner(coeffs, x):
    value = jnp.full_like(x, coeffs[-1])
    for coeff in coeffs[-2::-1]:
        value = value * x + coeff
    return value


def turns(multiple, x):
    t = multiple * x
    t = t - jnp.floor(t + 0.5)
    square = t * t
    return horner(COS, square), t * horner(SIN, square)


def halves(x):
    high = x.astype(BF16)
    return high, (x - high.astype(F32)).astype(BF16)


def rows_of(one, two, rest):
    high, low = halves(jnp.concatenate([one, two], 0))
    rest_high = rest.astype(BF16).astype(F32)
    both = jnp.concatenate([rest_high, rest - rest_high], 0).astype(BF16)
    return jnp.concatenate([high, both, low], 0)


def product(left, high, low, dims):
    main = lax.dot_general(left, high, dims, preferred_element_type=F32)
    one = main[0:8] + main[32:40]
    two = main[8:16] + main[40:48]
    rest = main[16:24] + main[24:32]
    if low is not None:
        minor = lax.dot_general(left[0:32], low, dims, preferred_element_type=F32)
        one = one + minor[0:8]
        two = two + minor[8:16]
        rest = rest + minor[16:24]
    return one, two, rest


def partner(me, t, count):
    if count & (count - 1) == 0:
        return me ^ abs(t)
    return (me + t + count) % count


def lookup(tables, kinds):
    found = [jnp.zeros(kinds.shape, F32) for _ in tables]
    for kind in range(SPECIES):
        here = kinds == kind
        found = [jnp.where(here, table[kind], x) for table, x in zip(tables, found)]
    return found


def pack_kernel(
    pos_hbm,
    charge_hbm,
    species_hbm,
    neighbors_hbm,
    chi_hbm,
    hard_hbm,
    bond_hbm,
    out,
    pos,
    charge,
    species,
    neighbors,
    chi_table,
    hard_table,
    bond_table,
    arrived,
):
    sources = (pos_hbm, charge_hbm, species_hbm, neighbors_hbm, chi_hbm, hard_hbm, bond_hbm)
    targets = (pos, charge, species, neighbors, chi_table, hard_table, bond_table)
    copies = [
        pltpu.make_async_copy(source, target, arrived.at[i])
        for i, (source, target) in enumerate(zip(sources, targets))
    ]
    for copy in copies:
        copy.start()
    for copy in copies:
        copy.wait()
    dims, beads, width = pos.shape
    chi, hard, bond = lookup((chi_table, hard_table, bond_table), species[...])
    shared = [chi, mixing / hard, bond, jnp.zeros((1, width), F32)]
    for b in range(beads):
        own = [pos[d, b : b + 1, :] for d in range(dims)] + [charge[b : b + 1, :]]
        out[b] = jnp.concatenate(own + shared, 0)
    out[beads] = neighbors[...].astype(F32)


def sort_kernel(beads, groups, rank_ref, *refs):
    got, outs = refs[:groups], refs[groups:]
    me, group = rank_ref[0] % beads, rank_ref[0] // beads
    for k in range(groups):
        source = partner(group, -k, groups)
        near = got[k][beads]
        for t in range(beads):
            outs[t][source, 0:8, :] = near
            outs[t][source, 8:16, :] = got[k][partner(me, t, beads)]


def weight_kernel(k_index, kernel, pos, species, mass_table, after, out, edges, pull):
    del after
    (mass,) = lookup((mass_table,), species[...])
    pull[...] = time_step / mass
    dims, beads, _ = pos.shape
    for d in range(dims):
        edges[d : d + 1, :] = pos[d, 0:1, :]
        edges[dims + d : dims + d + 1, :] = pos[d, beads - 1 : beads, :]
    count = k_index.shape[1]
    k = k_index[...]
    first, second, third = k[0:1], k[1:2], k[2:3]
    flip = (first < 0) | ((first == 0) & (second < 0))
    sign = jnp.where(flip, -1, 1)
    p, q, r = sign * first, sign * second, sign * third
    wide = 16 * (p - 1)
    with_p = jnp.where(q > 0, wide + q - 1, jnp.where(q < 0, wide + 7 - q, 135 + p))
    without_p = jnp.where(q > 0, 127 + q, 144)
    mode = jnp.where(p > 0, with_p, without_p)
    at = lax.broadcasted_iota(jnp.int32, (MODES, count), 0)
    chosen = jnp.where(at == mode, 1.0, 0.0).astype(BF16)
    row = lax.broadcasted_iota(jnp.int32, (8, count), 0)
    weight = kernel[...]
    here = row + 1 == jnp.abs(r)
    even = jnp.where(here, weight, 0.0)
    odd = jnp.where(here, jnp.where(r < 0, -weight, weight), 0.0)
    zero = jnp.where((row == 0) & (r == 0), weight, 0.0)
    even, odd, zero = product(rows_of(even, odd, zero), chosen, None, NT)
    out[0:8, :] = even
    out[8:16, :] = odd
    out[16:24, :] = zero


def bead_kernel(
    scale,
    inverse_atoms,
    beads,
    rank_ref,
    weights_hbm,
    *refs,
):
    blocks, outs = refs[:beads], refs[beads : 2 * beads]
    (
        got,
        cos_high,
        cos_low,
        sin_high,
        sin_low,
        left,
        z_cos,
        z_sin,
        charges,
        weights,
        mine,
        arrived,
    ) = refs[2 * beads :]
    bring = pltpu.make_async_copy(weights_hbm, weights, arrived)
    bring.start()
    ranks, _, width = got.shape
    me = rank_ref[0] % beads
    for t in range(beads):
        source = partner(me, -t, beads)
        for group in range(ranks // beads):
            got[group * beads + source] = blocks[t][group]
    lane = lax.broadcasted_iota(jnp.int32, (8, width), 1)
    row = lax.broadcasted_iota(jnp.int32, (8, width), 0)
    multiple = (row + 1).astype(F32)
    single = jnp.where(row == 0, 1.0, 0.0)
    blank = jnp.zeros((8, width), F32)

    def at(j):
        return slice(j * width, (j + 1) * width)

    def everywhere(x):
        return jnp.broadcast_to(x, (8, width))

    def column_sum(x):
        return everywhere(jnp.sum(x, axis=0, keepdims=True))

    chi, hard, bond, charge = [], [], [], []
    for j in range(ranks):
        cx, sx = turns(multiple, got[j, 8:9, :])
        cy, sy = turns(multiple, got[j, 9:10, :])
        cz, sz = turns(multiple, got[j, 10:11, :])
        z_cos[:, at(j)] = cz
        z_sin[:, at(j)] = sz

        def keep(rows, cosine, sine):
            high, low = halves(cosine)
            cos_high[rows, at(j)] = high
            cos_low[rows, at(j)] = low
            high, low = halves(sine)
            sin_high[rows, at(j)] = high
            sin_low[rows, at(j)] = low

        for p in range(8):
            cp, sp = everywhere(cx[p : p + 1]), everywhere(sx[p : p + 1])
            cc, ss, sc, cs = cp * cy, sp * sy, sp * cy, cp * sy
            keep(
                slice(16 * p, 16 * p + 16),
                jnp.concatenate([cc - ss, cc + ss], 0),
                jnp.concatenate([sc + cs, sc - cs], 0),
            )
        keep(slice(128, 144), jnp.concatenate([cy, cx], 0), jnp.concatenate([sy, sx], 0))
        keep(
            slice(144, 160),
            jnp.concatenate([single, blank], 0),
            jnp.concatenate([blank, blank], 0),
        )
        charge.append(everywhere(got[j, 11:12, :]))
        chi.append(everywhere(got[j, 12:13, :]))
        hard.append(everywhere(got[j, 13:14, :]))
        bond.append(everywhere(got[j, 14:15, :]))

    bring.wait()
    even, odd, zero = weights[0:8, :], weights[8:16, :], weights[16:24, :]

    def coefficients(charge):
        for j in range(ranks):
            left[:, at(j)] = rows_of(
                charge[j] * z_cos[:, at(j)], charge[j] * z_sin[:, at(j)], charge[j] * single
            )
        t_cc, t_cs, t_c0 = product(left[...], cos_high[...], cos_low[...], NT)
        t_sc, t_ss, t_s0 = product(left[...], sin_high[...], sin_low[...], NT)
        v_cos = (even * t_cc - odd * t_ss, even * t_cs + odd * t_sc, zero * t_c0)
        v_sin = (even * t_sc + odd * t_cs, even * t_ss - odd * t_cc, zero * t_s0)
        return v_cos, v_sin

    for rounds in range(QITERS):
        v_cos, v_sin = coefficients(charge)
        from_cos = product(rows_of(*v_cos), cos_high[...], cos_low[...], NN)
        from_sin = product(rows_of(*v_sin), sin_high[...], sin_low[...], NN)
        u_c, u_s, u_0 = (a + b for a, b in zip(from_cos, from_sin))
        weighted = [b * q for b, q in zip(bond, charge)]
        relaxed = []
        total = blank
        for j in range(ranks):
            potential = scale * column_sum(
                z_cos[:, at(j)] * u_c[:, at(j)] + z_sin[:, at(j)] * u_s[:, at(j)] + u_0[:, at(j)]
            )
            before = weighted[(j - 1) % ranks]
            after = weighted[(j + 1) % ranks]
            lower = jnp.where(lane < 3 * width // 4, weighted[j], before)
            upper = jnp.where(lane >= width // 4, weighted[j], after)
            place = (lane + got[j, 0:8, :].astype(jnp.int32)) & (width - 1)
            near = jnp.where(
                lane < width // 2,
                jnp.take_along_axis(lower, place, axis=1),
                jnp.take_along_axis(upper, place, axis=1),
            )
            new = (1.0 - mixing) * charge[j] - hard[j] * (
                chi[j] + potential + bond[j] * column_sum(near)
            )
            relaxed.append(new)
            total = total + new
        mean = jnp.sum(total, axis=1, keepdims=True) * inverse_atoms
        charge = [new - mean for new in relaxed]

    for j in range(ranks):
        charges[:, at(j)] = charge[j]
    (v_cc, v_cs, v_c0), (v_sc, v_ss, v_s0) = coefficients(charge)
    mode = lax.broadcasted_iota(jnp.int32, (8, MODES), 1)
    inner = mode & 15
    wave_x = jnp.where(
        mode < 128, (mode >> 4) + 1, jnp.where((mode >= 136) & (mode < 144), mode - 135, 0)
    ).astype(F32)
    wave_y = jnp.where(
        mode < 128,
        jnp.where(inner < 8, inner + 1, 7 - inner),
        jnp.where(mode < 136, mode - 127, 0),
    ).astype(F32)
    span = beads * width
    base = pl.multiple_of((rank_ref[0] // beads) * span, span)
    own = pl.ds(base, span)
    ch, cl, sh, sl = (ref[:, own] for ref in (cos_high, cos_low, sin_high, sin_low))
    zc, zs, q = z_cos[:, own], z_sin[:, own], charges[:, own]

    def field(for_cos, for_sin):
        a = product(rows_of(*for_cos), ch, cl, NN)
        b = product(rows_of(*for_sin), sh, sl, NN)
        return (one + two for one, two in zip(a, b))

    def force(wave):
        u_c, u_s, u_0 = field(
            (-wave * v_sc, -wave * v_ss, -wave * v_s0), (wave * v_cc, wave * v_cs, wave * v_c0)
        )
        return zc * u_c + zs * u_s + u_0

    along_x = force(wave_x)
    along_y = force(wave_y)
    u_c, u_s, _ = field((v_cc, v_cs, v_c0), (v_sc, v_ss, v_s0))
    wide_multiple = jnp.broadcast_to(multiple[:, 0:1], (8, span))
    along_z = wide_multiple * (zs * u_c - zc * u_s)
    factor = (two_pi * scale) * q
    for t in range(beads):
        cut = at(t)
        fx, fy, fz = (
            factor[:, cut] * column_sum(f[:, cut]) for f in (along_x, along_y, along_z)
        )
        mine[:, cut] = jnp.where(
            row == 0, fx, jnp.where(row == 1, fy, jnp.where(row == 2, fz, q[:, cut]))
        )
    for t in range(beads):
        there = pl.multiple_of(partner(me, t, beads) * width, width)
        outs[t][...] = mine[0:4, pl.ds(there, width)]


def move_kernel(low_at, high_at, rank_ref, pos, vel, low, high, pull, *refs):
    dims, beads, width = pos.shape
    got, (pos_out, vel_out, charge_out, home) = refs[:beads], refs[beads:]
    me = rank_ref[0] % beads
    for t in range(beads):
        bead = partner(me, -t, beads)
        for d in range(dims + 1):
            home[pl.ds(d * beads + bead, 1), :] = got[t][d : d + 1, :]
    gain = jnp.broadcast_to(pull[...], (beads, width))
    for d in range(dims):
        here = pos[d]
        before = jnp.concatenate([low[low_at + d : low_at + d + 1, :], here[: beads - 1]], 0)
        after = jnp.concatenate([here[1:], high[high_at + d : high_at + d + 1, :]], 0)
        laplace = 2.0 * here - before - after
        force = home[d * beads : (d + 1) * beads, :]
        fresh = vel[d] + (gain * force - (time_step * spring_rate) * laplace)
        vel_out[d] = fresh
        pos_out[d] = here + time_step * fresh
    charge_out[...] = home[dims * beads : (dims + 1) * beads, :]


VMEM = pl.BlockSpec(memory_space=pltpu.VMEM)
SMEM = pl.BlockSpec(memory_space=pltpu.SMEM)
ANY = pl.BlockSpec(memory_space=pl.ANY)
HBM = pl.BlockSpec(memory_space=pltpu.HBM)


def stay(x):
    return pltpu.with_memory_space_constraint(x, pltpu.HBM)


def params(mebibytes):
    return pltpu.CompilerParams(vmem_limit_bytes=mebibytes << 20)


def body(
    positions,
    velocities,
    charges_in,
    species,
    neighbors,
    k_index,
    kernel,
    chi_table,
    hard_table,
    bond_table,
    mass_table,
):
    beads, dims, width = positions.shape
    ranks = lax.axis_size("atoms")
    chain = lax.axis_size("beads")
    atoms = ranks * width
    scale = ewald_gain / math.sqrt(KVEC * atoms)
    kinds = species[None, :]
    shape = jax.ShapeDtypeStruct

    places = positions.transpose(1, 0, 2)
    speeds = velocities.transpose(1, 0, 2)

    rank = lax.axis_index("atoms").astype(jnp.int32)[None]
    groups = ranks // beads

    def among_groups(x, k):
        pairs = [(r, partner(r // beads, k, groups) * beads + r % beads) for r in range(ranks)]
        return lax.ppermute(x, "atoms", pairs)

    def in_group(x, t):
        pairs = [(r, r // beads * beads + partner(r % beads, t, beads)) for r in range(ranks)]
        return lax.ppermute(x, "atoms", pairs)

    packed = pl.pallas_call(
        pack_kernel,
        out_shape=shape((beads + 1, 8, width), F32),
        in_specs=[HBM] * 7,
        out_specs=VMEM,
        scratch_shapes=[
            pltpu.VMEM(places.shape, F32),
            pltpu.VMEM(charges_in.shape, F32),
            pltpu.VMEM(kinds.shape, jnp.int32),
            pltpu.VMEM(neighbors.shape, jnp.int32),
            pltpu.SMEM((SPECIES,), F32),
            pltpu.SMEM((SPECIES,), F32),
            pltpu.SMEM((SPECIES,), F32),
            pltpu.SemaphoreType.DMA((7,)),
        ],
        compiler_params=params(4),
        name="pack",
    )(*map(stay, (places, charges_in, kinds, neighbors, chi_table, hard_table, bond_table)))
    gathered = [packed] + [among_groups(packed, k) for k in range(1, groups)]
    sorted_blocks = pl.pallas_call(
        functools.partial(sort_kernel, beads, groups),
        out_shape=[shape((groups, 16, width), F32)] * beads,
        in_specs=[SMEM] + [VMEM] * groups,
        out_specs=[VMEM] * beads,
        compiler_params=params(4),
        name="sort",
    )(rank, *gathered)
    blocks = [sorted_blocks[0]] + [in_group(sorted_blocks[t], t) for t in range(1, beads)]

    weights, edges, pull = pl.pallas_call(
        weight_kernel,
        out_shape=(
            shape((24, MODES), F32),
            shape((2 * dims, width), F32),
            shape((1, width), F32),
        ),
        in_specs=[VMEM] * 4 + [SMEM, ANY],
        out_specs=(VMEM, VMEM, VMEM),
        compiler_params=params(8),
        name="weights",
        cost_estimate=pl.CostEstimate(flops=10**9, bytes_accessed=10**5, transcendentals=0),
    )(k_index, kernel[None, :], places, kinds, mass_table, packed)
    if chain == 2:
        low = high = lax.ppermute(edges, "beads", [(0, 1), (1, 0)])
        low_at, high_at = dims, 0
    else:
        forward = [(i, (i + 1) % chain) for i in range(chain)]
        low = lax.ppermute(edges[dims:], "beads", forward)
        high = lax.ppermute(edges[:dims], "beads", [(b, a) for a, b in forward])
        low_at, high_at = 0, 0

    results = pl.pallas_call(
        functools.partial(bead_kernel, scale, 1.0 / atoms, beads),
        out_shape=[shape((4, width), F32)] * beads,
        in_specs=[SMEM, ANY] + [VMEM] * beads,
        out_specs=[VMEM] * beads,
        scratch_shapes=[
            pltpu.VMEM((ranks, 16, width), F32),
            pltpu.VMEM((MODES, atoms), BF16),
            pltpu.VMEM((MODES, atoms), BF16),
            pltpu.VMEM((MODES, atoms), BF16),
            pltpu.VMEM((MODES, atoms), BF16),
            pltpu.VMEM((48, atoms), BF16),
            pltpu.VMEM((8, atoms), F32),
            pltpu.VMEM((8, atoms), F32),
            pltpu.VMEM((8, atoms), F32),
            pltpu.VMEM((24, MODES), F32),
            pltpu.VMEM((8, beads * width), F32),
            pltpu.SemaphoreType.DMA,
        ],
        compiler_params=params(24),
        name="bead",
        cost_estimate=pl.CostEstimate(flops=10**10, bytes_accessed=10**6, transcendentals=0),
    )(rank, weights, *blocks)

    home = [results[0]] + [in_group(results[t], t) for t in range(1, beads)]

    new_places, new_speeds, charge = pl.pallas_call(
        functools.partial(move_kernel, low_at, high_at),
        out_shape=(
            shape(places.shape, F32),
            shape(places.shape, F32),
            shape(charges_in.shape, F32),
        ),
        in_specs=[SMEM] + [VMEM] * (5 + beads),
        out_specs=(VMEM, VMEM, VMEM),
        scratch_shapes=[pltpu.VMEM(((dims + 1) * beads, width), F32)],
        compiler_params=params(4),
        name="move",
    )(rank, places, speeds, low, high, pull, *home)
    return new_places.transpose(1, 0, 2), new_speeds.transpose(1, 0, 2), charge


def solution(mesh):
    return jax.shard_map(
        body,
        mesh=mesh,
        in_specs=(
            P("beads", None, "atoms"),
            P("beads", None, "atoms"),
            P("beads", "atoms"),
            P("atoms"),
            P(None, "atoms"),
            P(),
            P(),
            P(),
            P(),
            P(),
            P(),
        ),
        out_specs=(P("beads", None, "atoms"), P("beads", None, "atoms"), P("beads", "atoms")),
        check_vma=False,
    )
```

```python
import functools
import math

import jax
import jax.numpy as jnp
from jax import lax
from jax.experimental import pallas as pl
from jax.experimental.pallas import tpu as pltpu
from jax.sharding import PartitionSpec as P

KVEC = 2048
QITERS = 2
SPECIES = 8
KMAX = 8
MODES = 160

two_pi = 2.0 * math.pi
ewald_gain = 4.0
mixing = 0.5
spring_rate = 0.5
time_step = 0.05

COS = (
    0.9999999998855522,
    -19.739208743453656,
    64.93938907588092,
    -85.45665831455305,
    60.242131335932854,
    -26.404668174676782,
    7.800131403864327,
    -1.4531122801527303,
)
SIN = (
    6.2831853025115,
    -41.34170040531697,
    81.60513138577565,
    -76.70301535354703,
    42.02592698387527,
    -14.89984666196953,
    3.2381375032044204,
)

F32 = jnp.float32
BF16 = jnp.bfloat16
NT = (((1,), (1,)), ((), ()))
NN = (((1,), (0,)), ((), ()))


def horner(coeffs, x):
    value = jnp.full_like(x, coeffs[-1])
    for coeff in coeffs[-2::-1]:
        value = value * x + coeff
    return value


def turns(multiple, x):
    t = multiple * x
    t = t - jnp.floor(t + 0.5)
    square = t * t
    return horner(COS, square), t * horner(SIN, square)


def halves(x):
    high = x.astype(BF16)
    return high, (x - high.astype(F32)).astype(BF16)


def rows_of(one, two, rest):
    high, low = halves(jnp.concatenate([one, two], 0))
    rest_high = rest.astype(BF16).astype(F32)
    both = jnp.concatenate([rest_high, rest - rest_high], 0).astype(BF16)
    return jnp.concatenate([high, both, low], 0)


def product(left, high, low, dims):
    main = lax.dot_general(left, high, dims, preferred_element_type=F32)
    one = main[0:8] + main[32:40]
    two = main[8:16] + main[40:48]
    rest = main[16:24] + main[24:32]
    if low is not None:
        minor = lax.dot_general(left[0:32], low, dims, preferred_element_type=F32)
        one = one + minor[0:8]
        two = two + minor[8:16]
        rest = rest + minor[16:24]
    return one, two, rest


def partner(me, t, count):
    if count & (count - 1) == 0:
        return me ^ abs(t)
    return (me + t + count) % count


def lookup(tables, kinds):
    found = [jnp.zeros(kinds.shape, F32) for _ in tables]
    for kind in range(SPECIES):
        here = kinds == kind
        found = [jnp.where(here, table[kind], x) for table, x in zip(tables, found)]
    return found


def pack_kernel(
    ranks, pos_hbm, charge_hbm, species_hbm, neighbors_hbm, out, pos, charge, species, neighbors, arrived
):
    sources = (pos_hbm, charge_hbm, species_hbm, neighbors_hbm)
    targets = (pos, charge, species, neighbors)
    copies = [
        pltpu.make_async_copy(source, target, arrived.at[i])
        for i, (source, target) in enumerate(zip(sources, targets))
    ]
    for copy in copies:
        copy.start()
    for copy in copies:
        copy.wait()
    dims, beads, _ = pos.shape
    near = neighbors[...].astype(F32)
    shared = [species[...].astype(F32)] + [near[n : n + 1, :] for n in range(near.shape[0])]
    for b in range(beads):
        own = [pos[d, b : b + 1, :] for d in range(dims)] + [charge[b : b + 1, :]]
        for rank in range(b, ranks, beads):
            for i, line in enumerate(own + shared):
                out[rank, i] = line


def weight_kernel(k_index, kernel, pos, species, mass_table, after, out, edges, pull):
    del after
    (mass,) = lookup((mass_table,), species[...])
    pull[...] = time_step / mass
    dims, beads, _ = pos.shape
    for d in range(dims):
        edges[d : d + 1, :] = pos[d, 0:1, :]
        edges[dims + d : dims + d + 1, :] = pos[d, beads - 1 : beads, :]
    count = k_index.shape[1]
    k = k_index[...]
    first, second, third = k[0:1], k[1:2], k[2:3]
    flip = (first < 0) | ((first == 0) & (second < 0))
    sign = jnp.where(flip, -1, 1)
    p, q, r = sign * first, sign * second, sign * third
    wide = 16 * (p - 1)
    with_p = jnp.where(q > 0, wide + q - 1, jnp.where(q < 0, wide + 7 - q, 135 + p))
    without_p = jnp.where(q > 0, 127 + q, 144)
    mode = jnp.where(p > 0, with_p, without_p)
    at = lax.broadcasted_iota(jnp.int32, (MODES, count), 0)
    chosen = jnp.where(at == mode, 1.0, 0.0).astype(BF16)
    row = lax.broadcasted_iota(jnp.int32, (8, count), 0)
    weight = kernel[...]
    here = row + 1 == jnp.abs(r)
    even = jnp.where(here, weight, 0.0)
    odd = jnp.where(here, jnp.where(r < 0, -weight, weight), 0.0)
    zero = jnp.where((row == 0) & (r == 0), weight, 0.0)
    even, odd, zero = product(rows_of(even, odd, zero), chosen, None, NT)
    out[0:8, :] = even
    out[8:16, :] = odd
    out[16:24, :] = zero


def bead_kernel(
    scale,
    inverse_atoms,
    beads,
    rank_ref,
    weights_hbm,
    got,
    chi_hbm,
    hard_hbm,
    bond_hbm,
    *refs,
):
    outs = refs[:beads]
    (
        cos_high,
        cos_low,
        sin_high,
        sin_low,
        left,
        z_cos,
        z_sin,
        charges,
        weights,
        mine,
        kinds,
        chi,
        hard,
        bond,
        chi_table,
        hard_table,
        bond_table,
        arrived,
    ) = refs[beads:]
    bring = [
        pltpu.make_async_copy(source, target, arrived.at[i])
        for i, (source, target) in enumerate(
            (
                (weights_hbm, weights),
                (chi_hbm, chi_table),
                (hard_hbm, hard_table),
                (bond_hbm, bond_table),
            )
        )
    ]
    for copy in bring:
        copy.start()
    ranks, lines, _, width = got.shape
    me = rank_ref[0] % beads
    lane = lax.broadcasted_iota(jnp.int32, (8, width), 1)
    row = lax.broadcasted_iota(jnp.int32, (8, width), 0)
    multiple = (row + 1).astype(F32)
    single = jnp.where(row == 0, 1.0, 0.0)
    blank = jnp.zeros((8, width), F32)

    def at(j):
        return slice(j * width, (j + 1) * width)

    def everywhere(x):
        return jnp.broadcast_to(x, (8, width))

    def column_sum(x):
        return everywhere(jnp.sum(x, axis=0, keepdims=True))

    charge, place = [], []
    for j in range(ranks):
        cx, sx = turns(multiple, got[j, 0])
        cy, sy = turns(multiple, got[j, 1])
        cz, sz = turns(multiple, got[j, 2])
        z_cos[:, at(j)] = cz
        z_sin[:, at(j)] = sz

        def keep(rows, cosine, sine):
            high, low = halves(cosine)
            cos_high[rows, at(j)] = high
            cos_low[rows, at(j)] = low
            high, low = halves(sine)
            sin_high[rows, at(j)] = high
            sin_low[rows, at(j)] = low

        for p in range(8):
            cp, sp = everywhere(cx[p : p + 1]), everywhere(sx[p : p + 1])
            cc, ss, sc, cs = cp * cy, sp * sy, sp * cy, cp * sy
            keep(
                slice(16 * p, 16 * p + 16),
                jnp.concatenate([cc - ss, cc + ss], 0),
                jnp.concatenate([sc + cs, sc - cs], 0),
            )
        keep(slice(128, 144), jnp.concatenate([cy, cx], 0), jnp.concatenate([sy, sx], 0))
        keep(
            slice(144, 160),
            jnp.concatenate([single, blank], 0),
            jnp.concatenate([blank, blank], 0),
        )
        charge.append(everywhere(got[j, 3]))
        kinds[j : j + 1, :] = got[j, 4]
        near = jnp.concatenate([got[j, i] for i in range(5, lines)], 0)
        place.append((lane + near.astype(jnp.int32)) & (width - 1))

    for copy in bring:
        copy.wait()
    chi[...], hardness, bond[...] = lookup((chi_table, hard_table, bond_table), kinds[...])
    hard[...] = mixing / hardness
    even, odd, zero = weights[0:8, :], weights[8:16, :], weights[16:24, :]

    def coefficients(charge):
        for j in range(ranks):
            left[:, at(j)] = rows_of(
                charge[j] * z_cos[:, at(j)], charge[j] * z_sin[:, at(j)], charge[j] * single
            )
        t_cc, t_cs, t_c0 = product(left[...], cos_high[...], cos_low[...], NT)
        t_sc, t_ss, t_s0 = product(left[...], sin_high[...], sin_low[...], NT)
        v_cos = (even * t_cc - odd * t_ss, even * t_cs + odd * t_sc, zero * t_c0)
        v_sin = (even * t_sc + odd * t_cs, even * t_ss - odd * t_cc, zero * t_s0)
        return v_cos, v_sin

    for rounds in range(QITERS):
        v_cos, v_sin = coefficients(charge)
        from_cos = product(rows_of(*v_cos), cos_high[...], cos_low[...], NN)
        from_sin = product(rows_of(*v_sin), sin_high[...], sin_low[...], NN)
        u_c, u_s, u_0 = (a + b for a, b in zip(from_cos, from_sin))
        weighted = [everywhere(bond[j : j + 1, :]) * charge[j] for j in range(ranks)]
        relaxed = []
        total = blank
        for j in range(ranks):
            potential = scale * column_sum(
                z_cos[:, at(j)] * u_c[:, at(j)] + z_sin[:, at(j)] * u_s[:, at(j)] + u_0[:, at(j)]
            )
            before = weighted[(j - 1) % ranks]
            after = weighted[(j + 1) % ranks]
            lower = jnp.where(lane < 3 * width // 4, weighted[j], before)
            upper = jnp.where(lane >= width // 4, weighted[j], after)
            near = jnp.where(
                lane < width // 2,
                jnp.take_along_axis(lower, place[j], axis=1),
                jnp.take_along_axis(upper, place[j], axis=1),
            )
            new = (1.0 - mixing) * charge[j] - everywhere(hard[j : j + 1, :]) * (
                everywhere(chi[j : j + 1, :])
                + potential
                + everywhere(bond[j : j + 1, :]) * column_sum(near)
            )
            relaxed.append(new)
            total = total + new
        mean = jnp.sum(total, axis=1, keepdims=True) * inverse_atoms
        charge = [new - mean for new in relaxed]

    for j in range(ranks):
        charges[:, at(j)] = charge[j]
    (v_cc, v_cs, v_c0), (v_sc, v_ss, v_s0) = coefficients(charge)
    mode = lax.broadcasted_iota(jnp.int32, (8, MODES), 1)
    inner = mode & 15
    wave_x = jnp.where(
        mode < 128, (mode >> 4) + 1, jnp.where((mode >= 136) & (mode < 144), mode - 135, 0)
    ).astype(F32)
    wave_y = jnp.where(
        mode < 128,
        jnp.where(inner < 8, inner + 1, 7 - inner),
        jnp.where(mode < 136, mode - 127, 0),
    ).astype(F32)
    span = beads * width
    base = pl.multiple_of((rank_ref[0] // beads) * span, span)
    own = pl.ds(base, span)
    ch, cl, sh, sl = (ref[:, own] for ref in (cos_high, cos_low, sin_high, sin_low))
    zc, zs, q = z_cos[:, own], z_sin[:, own], charges[:, own]

    def field(for_cos, for_sin):
        a = product(rows_of(*for_cos), ch, cl, NN)
        b = product(rows_of(*for_sin), sh, sl, NN)
        return (one + two for one, two in zip(a, b))

    def force(wave):
        u_c, u_s, u_0 = field(
            (-wave * v_sc, -wave * v_ss, -wave * v_s0), (wave * v_cc, wave * v_cs, wave * v_c0)
        )
        return zc * u_c + zs * u_s + u_0

    along_x = force(wave_x)
    along_y = force(wave_y)
    u_c, u_s, _ = field((v_cc, v_cs, v_c0), (v_sc, v_ss, v_s0))
    wide_multiple = jnp.broadcast_to(multiple[:, 0:1], (8, span))
    along_z = wide_multiple * (zs * u_c - zc * u_s)
    factor = (two_pi * scale) * q
    for t in range(beads):
        cut = at(t)
        fx, fy, fz = (
            factor[:, cut] * column_sum(f[:, cut]) for f in (along_x, along_y, along_z)
        )
        mine[:, cut] = jnp.where(
            row == 0, fx, jnp.where(row == 1, fy, jnp.where(row == 2, fz, q[:, cut]))
        )
    for t in range(beads):
        there = pl.multiple_of(partner(me, t, beads) * width, width)
        outs[t][...] = mine[0:4, pl.ds(there, width)]


def move_kernel(low_at, high_at, rank_ref, pos, vel, low, high, pull, *refs):
    dims, beads, width = pos.shape
    got, (pos_out, vel_out, charge_out, home) = refs[:beads], refs[beads:]
    me = rank_ref[0] % beads
    for t in range(beads):
        bead = partner(me, -t, beads)
        for d in range(dims + 1):
            home[pl.ds(d * beads + bead, 1), :] = got[t][d : d + 1, :]
    gain = jnp.broadcast_to(pull[...], (beads, width))
    for d in range(dims):
        here = pos[d]
        before = jnp.concatenate([low[low_at + d : low_at + d + 1, :], here[: beads - 1]], 0)
        after = jnp.concatenate([here[1:], high[high_at + d : high_at + d + 1, :]], 0)
        laplace = 2.0 * here - before - after
        force = home[d * beads : (d + 1) * beads, :]
        fresh = vel[d] + (gain * force - (time_step * spring_rate) * laplace)
        vel_out[d] = fresh
        pos_out[d] = here + time_step * fresh
    charge_out[...] = home[dims * beads : (dims + 1) * beads, :]


VMEM = pl.BlockSpec(memory_space=pltpu.VMEM)
SMEM = pl.BlockSpec(memory_space=pltpu.SMEM)
ANY = pl.BlockSpec(memory_space=pl.ANY)
HBM = pl.BlockSpec(memory_space=pltpu.HBM)


def stay(x):
    return pltpu.with_memory_space_constraint(x, pltpu.HBM)


def params(mebibytes):
    return pltpu.CompilerParams(vmem_limit_bytes=mebibytes << 20)


def body(
    positions,
    velocities,
    charges_in,
    species,
    neighbors,
    k_index,
    kernel,
    chi_table,
    hard_table,
    bond_table,
    mass_table,
):
    beads, dims, width = positions.shape
    ranks = lax.axis_size("atoms")
    chain = lax.axis_size("beads")
    atoms = ranks * width
    scale = ewald_gain / math.sqrt(KVEC * atoms)
    kinds = species[None, :]
    shape = jax.ShapeDtypeStruct

    places = positions.transpose(1, 0, 2)
    speeds = velocities.transpose(1, 0, 2)

    rank = lax.axis_index("atoms").astype(jnp.int32)[None]
    def in_group(x, t):
        pairs = [(r, r // beads * beads + partner(r % beads, t, beads)) for r in range(ranks)]
        return lax.ppermute(x, "atoms", pairs)

    lines = dims + 2 + neighbors.shape[0]
    packed = pl.pallas_call(
        functools.partial(pack_kernel, ranks),
        out_shape=shape((ranks, lines, 1, width), F32),
        in_specs=[HBM] * 4,
        out_specs=VMEM,
        scratch_shapes=[
            pltpu.VMEM(places.shape, F32),
            pltpu.VMEM(charges_in.shape, F32),
            pltpu.VMEM(kinds.shape, jnp.int32),
            pltpu.VMEM(neighbors.shape, jnp.int32),
            pltpu.SemaphoreType.DMA((4,)),
        ],
        compiler_params=params(4),
        name="pack",
    )(*map(stay, (places, charges_in, kinds, neighbors)))
    got = lax.all_to_all(packed, "atoms", 0, 0, tiled=True)

    weights, edges, pull = pl.pallas_call(
        weight_kernel,
        out_shape=(
            shape((24, MODES), F32),
            shape((2 * dims, width), F32),
            shape((1, width), F32),
        ),
        in_specs=[VMEM] * 4 + [SMEM, ANY],
        out_specs=(VMEM, VMEM, VMEM),
        compiler_params=params(8),
        name="weights",
        cost_estimate=pl.CostEstimate(flops=10**9, bytes_accessed=10**5, transcendentals=0),
    )(k_index, kernel[None, :], places, kinds, mass_table, packed)
    if chain == 2:
        low = high = lax.ppermute(edges, "beads", [(0, 1), (1, 0)])
        low_at, high_at = dims, 0
    else:
        forward = [(i, (i + 1) % chain) for i in range(chain)]
        low = lax.ppermute(edges[dims:], "beads", forward)
        high = lax.ppermute(edges[:dims], "beads", [(b, a) for a, b in forward])
        low_at, high_at = 0, 0

    results = pl.pallas_call(
        functools.partial(bead_kernel, scale, 1.0 / atoms, beads),
        out_shape=[shape((4, width), F32)] * beads,
        in_specs=[SMEM, ANY, VMEM] + [HBM] * 3,
        out_specs=[VMEM] * beads,
        scratch_shapes=[
            pltpu.VMEM((MODES, atoms), BF16),
            pltpu.VMEM((MODES, atoms), BF16),
            pltpu.VMEM((MODES, atoms), BF16),
            pltpu.VMEM((MODES, atoms), BF16),
            pltpu.VMEM((48, atoms), BF16),
            pltpu.VMEM((8, atoms), F32),
            pltpu.VMEM((8, atoms), F32),
            pltpu.VMEM((8, atoms), F32),
            pltpu.VMEM((24, MODES), F32),
            pltpu.VMEM((8, beads * width), F32),
            pltpu.VMEM((ranks, width), F32),
            pltpu.VMEM((ranks, width), F32),
            pltpu.VMEM((ranks, width), F32),
            pltpu.VMEM((ranks, width), F32),
            pltpu.SMEM((SPECIES,), F32),
            pltpu.SMEM((SPECIES,), F32),
            pltpu.SMEM((SPECIES,), F32),
            pltpu.SemaphoreType.DMA((4,)),
        ],
        compiler_params=params(24),
        name="bead",
        cost_estimate=pl.CostEstimate(flops=10**10, bytes_accessed=10**6, transcendentals=0),
    )(rank, weights, got, *map(stay, (chi_table, hard_table, bond_table)))

    home = [results[0]] + [in_group(results[t], t) for t in range(1, beads)]

    new_places, new_speeds, charge = pl.pallas_call(
        functools.partial(move_kernel, low_at, high_at),
        out_shape=(
            shape(places.shape, F32),
            shape(places.shape, F32),
            shape(charges_in.shape, F32),
        ),
        in_specs=[SMEM] + [VMEM] * (5 + beads),
        out_specs=(VMEM, VMEM, VMEM),
        scratch_shapes=[pltpu.VMEM(((dims + 1) * beads, width), F32)],
        compiler_params=params(4),
        name="move",
    )(rank, places, speeds, low, high, pull, *home)
    return new_places.transpose(1, 0, 2), new_speeds.transpose(1, 0, 2), charge


def solution(mesh):
    return jax.shard_map(
        body,
        mesh=mesh,
        in_specs=(
            P("beads", None, "atoms"),
            P("beads", None, "atoms"),
            P("beads", "atoms"),
            P("atoms"),
            P(None, "atoms"),
            P(),
            P(),
            P(),
            P(),
            P(),
            P(),
        ),
        out_specs=(P("beads", None, "atoms"), P("beads", None, "atoms"), P("beads", "atoms")),
        check_vma=False,
    )
```

```python
import functools
import math

import jax
import jax.numpy as jnp
from jax import lax
from jax.experimental import pallas as pl
from jax.experimental.pallas import tpu as pltpu
from jax.sharding import PartitionSpec as P

KVEC = 2048
QITERS = 2
SPECIES = 8
KMAX = 8
MODES = 128
REST = 32
ROWS = 4 * (MODES + REST)

two_pi = 2.0 * math.pi
ewald_gain = 4.0
mixing = 0.5
spring_rate = 0.5
time_step = 0.05

COS = (
    0.9999999998855522,
    -19.739208743453656,
    64.93938907588092,
    -85.45665831455305,
    60.242131335932854,
    -26.404668174676782,
    7.800131403864327,
    -1.4531122801527303,
)
SIN = (
    6.2831853025115,
    -41.34170040531697,
    81.60513138577565,
    -76.70301535354703,
    42.02592698387527,
    -14.89984666196953,
    3.2381375032044204,
)

F32 = jnp.float32
BF16 = jnp.bfloat16
NT = (((1,), (1,)), ((), ()))
NN = (((1,), (0,)), ((), ()))


def horner(coeffs, x):
    value = jnp.full_like(x, coeffs[-1])
    for coeff in coeffs[-2::-1]:
        value = value * x + coeff
    return value


def turns(multiple, x):
    t = multiple * x
    t = t - jnp.floor(t + 0.5)
    square = t * t
    return horner(COS, square), t * horner(SIN, square)


def halves(x):
    high = x.astype(BF16)
    return high, (x - high.astype(F32)).astype(BF16)


def rows_of(one, two, rest):
    high, low = halves(jnp.concatenate([one, two], 0))
    rest_high = rest.astype(BF16).astype(F32)
    both = jnp.concatenate([rest_high, rest - rest_high], 0).astype(BF16)
    return jnp.concatenate([high, both, low], 0)


def summed(x):
    return x[0:8] + x[32:40], x[8:16] + x[40:48], x[16:24] + x[24:32]


def partner(me, t, count):
    if count & (count - 1) == 0:
        return me ^ abs(t)
    return (me + t + count) % count


def lookup(tables, kinds):
    found = [jnp.zeros(kinds.shape, F32) for _ in tables]
    for kind in range(SPECIES):
        here = kinds == kind
        found = [jnp.where(here, table[kind], x) for table, x in zip(tables, found)]
    return found


def pack_kernel(
    ranks, pos_hbm, charge_hbm, species_hbm, neighbors_hbm, out, pos, charge, species, neighbors, arrived
):
    sources = (pos_hbm, charge_hbm, species_hbm, neighbors_hbm)
    targets = (pos, charge, species, neighbors)
    copies = [
        pltpu.make_async_copy(source, target, arrived.at[i])
        for i, (source, target) in enumerate(zip(sources, targets))
    ]
    for copy in copies:
        copy.start()
    for copy in copies:
        copy.wait()
    dims, beads, _ = pos.shape
    near = neighbors[...].astype(F32)
    shared = [species[...].astype(F32)] + [near[n : n + 1, :] for n in range(near.shape[0])]
    for b in range(beads):
        own = [pos[d, b : b + 1, :] for d in range(dims)] + [charge[b : b + 1, :]]
        for rank in range(b, ranks, beads):
            for i, line in enumerate(own + shared):
                out[rank, i] = line


def weight_kernel(k_index, kernel, pos, species, mass_table, after, out, edges, pull):
    del after
    (mass,) = lookup((mass_table,), species[...])
    pull[...] = time_step / mass
    dims, beads, _ = pos.shape
    for d in range(dims):
        edges[d : d + 1, :] = pos[d, 0:1, :]
        edges[dims + d : dims + d + 1, :] = pos[d, beads - 1 : beads, :]
    count = k_index.shape[1]
    k = k_index[...]
    first, second, third = k[0:1], k[1:2], k[2:3]
    flip = (first < 0) | ((first == 0) & (second < 0))
    sign = jnp.where(flip, -1, 1)
    p, q, r = sign * first, sign * second, sign * third
    wide = 16 * (p - 1)
    with_p = jnp.where(q > 0, wide + q - 1, jnp.where(q < 0, wide + 7 - q, 135 + p))
    without_p = jnp.where(q > 0, 127 + q, 144)
    mode = jnp.where(p > 0, with_p, without_p)
    at = lax.broadcasted_iota(jnp.int32, (MODES + 4 * REST, count), 0)
    at = jnp.where(at < MODES, at, MODES + (at & (REST - 1)))
    chosen = jnp.where(at == mode, 1.0, 0.0).astype(BF16)
    row = lax.broadcasted_iota(jnp.int32, (8, count), 0)
    weight = kernel[...]
    here = row + 1 == jnp.abs(r)
    even = jnp.where(here, weight, 0.0)
    odd = jnp.where(here, jnp.where(r < 0, -weight, weight), 0.0)
    zero = jnp.where((row == 0) & (r == 0), weight, 0.0)
    even, odd, zero = summed(
        lax.dot_general(rows_of(even, odd, zero), chosen, NT, preferred_element_type=F32)
    )
    lane = lax.broadcasted_iota(jnp.int32, even.shape, 1)
    out[0:8, :] = even
    out[8:16, :] = jnp.where((lane >= MODES) & (lane < MODES + 2 * REST), -odd, odd)
    out[16:24, :] = zero


def bead_kernel(
    scale,
    inverse_atoms,
    beads,
    rank_ref,
    weights_hbm,
    got,
    chi_hbm,
    hard_hbm,
    bond_hbm,
    *refs,
):
    outs = refs[:beads]
    (
        table,
        left,
        z_cos,
        z_sin,
        charges,
        weights,
        mine,
        kinds,
        chi,
        hard,
        bond,
        chi_table,
        hard_table,
        bond_table,
        arrived,
    ) = refs[beads:]
    bring = [
        pltpu.make_async_copy(source, target, arrived.at[i])
        for i, (source, target) in enumerate(
            (
                (weights_hbm, weights),
                (chi_hbm, chi_table),
                (hard_hbm, hard_table),
                (bond_hbm, bond_table),
            )
        )
    ]
    for copy in bring:
        copy.start()
    ranks, lines, _, width = got.shape
    me = rank_ref[0] % beads
    lane = lax.broadcasted_iota(jnp.int32, (8, width), 1)
    row = lax.broadcasted_iota(jnp.int32, (8, width), 0)
    multiple = (row + 1).astype(F32)
    single = jnp.where(row == 0, 1.0, 0.0)
    blank = jnp.zeros((8, width), F32)

    def at(j):
        return slice(j * width, (j + 1) * width)

    def everywhere(x):
        return jnp.broadcast_to(x, (8, width))

    def column_sum(x):
        return everywhere(jnp.sum(x, axis=0, keepdims=True))

    charge, place = [], []
    for j in range(ranks):
        cx, sx = turns(multiple, got[j, 0])
        cy, sy = turns(multiple, got[j, 1])
        cz, sz = turns(multiple, got[j, 2])
        z_cos[:, at(j)] = cz
        z_sin[:, at(j)] = sz

        def keep(start, step, cosine, sine):
            for part, x in enumerate(halves(cosine) + halves(sine)):
                table[start + part * step : start + part * step + 16, at(j)] = x

        for p in range(8):
            cp, sp = everywhere(cx[p : p + 1]), everywhere(sx[p : p + 1])
            cc, ss, sc, cs = cp * cy, sp * sy, sp * cy, cp * sy
            keep(
                16 * p,
                MODES,
                jnp.concatenate([cc - ss, cc + ss], 0),
                jnp.concatenate([sc + cs, sc - cs], 0),
            )
        keep(4 * MODES, REST, jnp.concatenate([cy, cx], 0), jnp.concatenate([sy, sx], 0))
        keep(
            4 * MODES + 16,
            REST,
            jnp.concatenate([single, blank], 0),
            jnp.concatenate([blank, blank], 0),
        )
        charge.append(everywhere(got[j, 3]))
        kinds[j : j + 1, :] = got[j, 4]
        near = jnp.concatenate([got[j, i] for i in range(5, lines)], 0)
        place.append((lane + near.astype(jnp.int32)) & (width - 1))

    for copy in bring:
        copy.wait()
    chi[...], hardness, bond[...] = lookup((chi_table, hard_table, bond_table), kinds[...])
    hard[...] = mixing / hardness
    even, odd, zero = weights[0:8, :], weights[8:16, :], weights[16:24, :]
    tile = lax.broadcasted_iota(jnp.int32, (8, 4 * REST), 1)
    is_sum = (tile & REST) == 0
    sign = jnp.where(tile < 2 * REST, -1.0, 1.0)
    main, rest = slice(0, MODES), slice(MODES, MODES + 4 * REST)

    def turned(x, lanes):
        return jnp.concatenate([x[:, lanes:], x[:, :lanes]], 1)

    def folded(x):
        cosine = x[:, 0:MODES] + x[:, MODES : 2 * MODES]
        sine = x[:, 2 * MODES : 3 * MODES] + x[:, 3 * MODES : 4 * MODES]
        last = x[:, 4 * MODES :]
        last = jnp.where(is_sum, last + turned(last, REST), 0.0)
        return cosine, sine, last + turned(last, 3 * REST)

    def coefficients(charge):
        for j in range(ranks):
            left[:, at(j)] = rows_of(
                charge[j] * z_cos[:, at(j)], charge[j] * z_sin[:, at(j)], charge[j] * single
            )
        products = lax.dot_general(left[...], table[...], NT, preferred_element_type=F32)
        (t_cc, t_sc, r_c), (t_cs, t_ss, r_s), (t_c0, t_s0, r_0) = map(folded, summed(products))
        w, o, z = even[:, main], odd[:, main], zero[:, main]
        wr, signed, zr = even[:, rest], odd[:, rest], zero[:, rest]
        with_cos = (
            w * t_cc - o * t_ss,
            w * t_sc + o * t_cs,
            wr * r_c + signed * turned(r_s, 2 * REST),
        )
        with_sin = (
            w * t_cs + o * t_sc,
            w * t_ss - o * t_cc,
            wr * r_s - signed * turned(r_c, 2 * REST),
        )
        alone = (z * t_c0, z * t_s0, zr * r_0)
        return with_cos, with_sin, alone

    def matrix(parts):
        x = rows_of(*(jnp.concatenate(part, 1) for part in parts))
        cosine, sine, last = x[:, 0:MODES], x[:, MODES : 2 * MODES], x[:, 2 * MODES :]
        return jnp.concatenate([cosine, cosine, sine, sine, last], 1)

    for rounds in range(QITERS):
        products = lax.dot_general(
            matrix(coefficients(charge)), table[...], NN, preferred_element_type=F32
        )
        u_c, u_s, u_0 = summed(products)
        weighted = [everywhere(bond[j : j + 1, :]) * charge[j] for j in range(ranks)]
        relaxed = []
        total = blank
        for j in range(ranks):
            potential = scale * column_sum(
                z_cos[:, at(j)] * u_c[:, at(j)] + z_sin[:, at(j)] * u_s[:, at(j)] + u_0[:, at(j)]
            )
            before = weighted[(j - 1) % ranks]
            after = weighted[(j + 1) % ranks]
            lower = jnp.where(lane < 3 * width // 4, weighted[j], before)
            upper = jnp.where(lane >= width // 4, weighted[j], after)
            near = jnp.where(
                lane < width // 2,
                jnp.take_along_axis(lower, place[j], axis=1),
                jnp.take_along_axis(upper, place[j], axis=1),
            )
            new = (1.0 - mixing) * charge[j] - everywhere(hard[j : j + 1, :]) * (
                everywhere(chi[j : j + 1, :])
                + potential
                + everywhere(bond[j : j + 1, :]) * column_sum(near)
            )
            relaxed.append(new)
            total = total + new
        mean = jnp.sum(total, axis=1, keepdims=True) * inverse_atoms
        charge = [new - mean for new in relaxed]

    for j in range(ranks):
        charges[:, at(j)] = charge[j]
    parts = coefficients(charge)
    mode = lax.broadcasted_iota(jnp.int32, (8, MODES), 1)
    inner = mode & 15
    few = tile & (REST - 1)
    waves = (
        (
            (mode >> 4) + 1,
            jnp.where((few >= 8) & (few < 16), few - 7, 0),
        ),
        (
            jnp.where(inner < 8, inner + 1, 7 - inner),
            jnp.where(few < 8, few + 1, 0),
        ),
    )

    def slope(part, wave):
        cosine, sine, last = part
        for_main, for_rest = (x.astype(F32) for x in wave)
        return -for_main * sine, for_main * cosine, sign * for_rest * turned(last, 2 * REST)

    stacked = [matrix([slope(part, wave) for part in parts]) for wave in waves]
    span = beads * width
    base = pl.multiple_of((rank_ref[0] // beads) * span, span)
    own = pl.ds(base, span)
    zc, zs, q = z_cos[:, own], z_sin[:, own], charges[:, own]
    products = lax.dot_general(
        jnp.concatenate(stacked + [matrix(parts)], 0),
        table[:, own],
        NN,
        preferred_element_type=F32,
    )
    (x_c, x_s, x_0), (y_c, y_s, y_0), (u_c, u_s, _) = (
        summed(products[48 * i : 48 * i + 48]) for i in range(3)
    )
    along_x = zc * x_c + zs * x_s + x_0
    along_y = zc * y_c + zs * y_s + y_0
    wide_multiple = jnp.broadcast_to(multiple[:, 0:1], (8, span))
    along_z = wide_multiple * (zs * u_c - zc * u_s)
    factor = (two_pi * scale) * q
    for t in range(beads):
        cut = at(t)
        fx, fy, fz = (
            factor[:, cut] * column_sum(f[:, cut]) for f in (along_x, along_y, along_z)
        )
        mine[:, cut] = jnp.where(
            row == 0, fx, jnp.where(row == 1, fy, jnp.where(row == 2, fz, q[:, cut]))
        )
    for t in range(beads):
        there = pl.multiple_of(partner(me, t, beads) * width, width)
        outs[t][...] = mine[0:4, pl.ds(there, width)]


def move_kernel(low_at, high_at, rank_ref, pos, vel, low, high, pull, *refs):
    dims, beads, width = pos.shape
    got, (pos_out, vel_out, charge_out, home) = refs[:beads], refs[beads:]
    me = rank_ref[0] % beads
    for t in range(beads):
        bead = partner(me, -t, beads)
        for d in range(dims + 1):
            home[pl.ds(d * beads + bead, 1), :] = got[t][d : d + 1, :]
    gain = jnp.broadcast_to(pull[...], (beads, width))
    for d in range(dims):
        here = pos[d]
        before = jnp.concatenate([low[low_at + d : low_at + d + 1, :], here[: beads - 1]], 0)
        after = jnp.concatenate([here[1:], high[high_at + d : high_at + d + 1, :]], 0)
        laplace = 2.0 * here - before - after
        force = home[d * beads : (d + 1) * beads, :]
        fresh = vel[d] + (gain * force - (time_step * spring_rate) * laplace)
        vel_out[d] = fresh
        pos_out[d] = here + time_step * fresh
    charge_out[...] = home[dims * beads : (dims + 1) * beads, :]


VMEM = pl.BlockSpec(memory_space=pltpu.VMEM)
SMEM = pl.BlockSpec(memory_space=pltpu.SMEM)
ANY = pl.BlockSpec(memory_space=pl.ANY)
HBM = pl.BlockSpec(memory_space=pltpu.HBM)


def stay(x):
    return pltpu.with_memory_space_constraint(x, pltpu.HBM)


def params(mebibytes):
    return pltpu.CompilerParams(vmem_limit_bytes=mebibytes << 20)


def body(
    positions,
    velocities,
    charges_in,
    species,
    neighbors,
    k_index,
    kernel,
    chi_table,
    hard_table,
    bond_table,
    mass_table,
):
    beads, dims, width = positions.shape
    ranks = lax.axis_size("atoms")
    chain = lax.axis_size("beads")
    atoms = ranks * width
    scale = ewald_gain / math.sqrt(KVEC * atoms)
    kinds = species[None, :]
    shape = jax.ShapeDtypeStruct

    places = positions.transpose(1, 0, 2)
    speeds = velocities.transpose(1, 0, 2)

    rank = lax.axis_index("atoms").astype(jnp.int32)[None]
    def in_group(x, t):
        pairs = [(r, r // beads * beads + partner(r % beads, t, beads)) for r in range(ranks)]
        return lax.ppermute(x, "atoms", pairs)

    lines = dims + 2 + neighbors.shape[0]
    packed = pl.pallas_call(
        functools.partial(pack_kernel, ranks),
        out_shape=shape((ranks, lines, 1, width), F32),
        in_specs=[HBM] * 4,
        out_specs=VMEM,
        scratch_shapes=[
            pltpu.VMEM(places.shape, F32),
            pltpu.VMEM(charges_in.shape, F32),
            pltpu.VMEM(kinds.shape, jnp.int32),
            pltpu.VMEM(neighbors.shape, jnp.int32),
            pltpu.SemaphoreType.DMA((4,)),
        ],
        compiler_params=params(4),
        name="pack",
    )(*map(stay, (places, charges_in, kinds, neighbors)))
    got = lax.all_to_all(packed, "atoms", 0, 0, tiled=True)

    weights, edges, pull = pl.pallas_call(
        weight_kernel,
        out_shape=(
            shape((24, MODES + 4 * REST), F32),
            shape((2 * dims, width), F32),
            shape((1, width), F32),
        ),
        in_specs=[VMEM] * 4 + [SMEM, ANY],
        out_specs=(VMEM, VMEM, VMEM),
        compiler_params=params(8),
        name="weights",
        cost_estimate=pl.CostEstimate(flops=10**9, bytes_accessed=10**5, transcendentals=0),
    )(k_index, kernel[None, :], places, kinds, mass_table, packed)
    if chain == 2:
        low = high = lax.ppermute(edges, "beads", [(0, 1), (1, 0)])
        low_at, high_at = dims, 0
    else:
        forward = [(i, (i + 1) % chain) for i in range(chain)]
        low = lax.ppermute(edges[dims:], "beads", forward)
        high = lax.ppermute(edges[:dims], "beads", [(b, a) for a, b in forward])
        low_at, high_at = 0, 0

    results = pl.pallas_call(
        functools.partial(bead_kernel, scale, 1.0 / atoms, beads),
        out_shape=[shape((4, width), F32)] * beads,
        in_specs=[SMEM, ANY, VMEM] + [HBM] * 3,
        out_specs=[VMEM] * beads,
        scratch_shapes=[
            pltpu.VMEM((ROWS, atoms), BF16),
            pltpu.VMEM((48, atoms), BF16),
            pltpu.VMEM((8, atoms), F32),
            pltpu.VMEM((8, atoms), F32),
            pltpu.VMEM((8, atoms), F32),
            pltpu.VMEM((24, MODES + 4 * REST), F32),
            pltpu.VMEM((8, beads * width), F32),
            pltpu.VMEM((ranks, width), F32),
            pltpu.VMEM((ranks, width), F32),
            pltpu.VMEM((ranks, width), F32),
            pltpu.VMEM((ranks, width), F32),
            pltpu.SMEM((SPECIES,), F32),
            pltpu.SMEM((SPECIES,), F32),
            pltpu.SMEM((SPECIES,), F32),
            pltpu.SemaphoreType.DMA((4,)),
        ],
        compiler_params=params(24),
        name="bead",
        cost_estimate=pl.CostEstimate(flops=10**10, bytes_accessed=10**6, transcendentals=0),
    )(rank, weights, got, *map(stay, (chi_table, hard_table, bond_table)))

    home = [results[0]] + [in_group(results[t], t) for t in range(1, beads)]

    new_places, new_speeds, charge = pl.pallas_call(
        functools.partial(move_kernel, low_at, high_at),
        out_shape=(
            shape(places.shape, F32),
            shape(places.shape, F32),
            shape(charges_in.shape, F32),
        ),
        in_specs=[SMEM] + [VMEM] * (5 + beads),
        out_specs=(VMEM, VMEM, VMEM),
        scratch_shapes=[pltpu.VMEM(((dims + 1) * beads, width), F32)],
        compiler_params=params(4),
        name="move",
    )(rank, places, speeds, low, high, pull, *home)
    return new_places.transpose(1, 0, 2), new_speeds.transpose(1, 0, 2), charge


def solution(mesh):
    return jax.shard_map(
        body,
        mesh=mesh,
        in_specs=(
            P("beads", None, "atoms"),
            P("beads", None, "atoms"),
            P("beads", "atoms"),
            P("atoms"),
            P(None, "atoms"),
            P(),
            P(),
            P(),
            P(),
            P(),
            P(),
        ),
        out_specs=(P("beads", None, "atoms"), P("beads", None, "atoms"), P("beads", "atoms")),
        check_vma=False,
    )
```

```python
import functools
import math

import jax
import jax.numpy as jnp
from jax import lax
from jax.experimental import pallas as pl
from jax.experimental.pallas import tpu as pltpu
from jax.sharding import PartitionSpec as P

KVEC = 2048
QITERS = 2
SPECIES = 8
KMAX = 8
MODES = 160

two_pi = 2.0 * math.pi
ewald_gain = 4.0
mixing = 0.5
spring_rate = 0.5
time_step = 0.05

COS = (
    0.9999999998855522,
    -19.739208743453656,
    64.93938907588092,
    -85.45665831455305,
    60.242131335932854,
    -26.404668174676782,
    7.800131403864327,
    -1.4531122801527303,
)
SIN = (
    6.2831853025115,
    -41.34170040531697,
    81.60513138577565,
    -76.70301535354703,
    42.02592698387527,
    -14.89984666196953,
    3.2381375032044204,
)

F32 = jnp.float32
BF16 = jnp.bfloat16
NT = (((1,), (1,)), ((), ()))
NN = (((1,), (0,)), ((), ()))


def horner(coeffs, x):
    value = jnp.full_like(x, coeffs[-1])
    for coeff in coeffs[-2::-1]:
        value = value * x + coeff
    return value


def turns(multiple, x):
    t = multiple * x
    t = t - jnp.floor(t + 0.5)
    square = t * t
    return horner(COS, square), t * horner(SIN, square)


def halves(x):
    high = x.astype(BF16)
    return high, (x - high.astype(F32)).astype(BF16)


def rows_of(one, two, rest):
    high, low = halves(jnp.concatenate([one, two], 0))
    rest_high = rest.astype(BF16).astype(F32)
    both = jnp.concatenate([rest_high, rest - rest_high], 0).astype(BF16)
    return jnp.concatenate([high, both, low], 0)


def product(left, high, low, dims):
    main = lax.dot_general(left, high, dims, preferred_element_type=F32)
    one = main[0:8] + main[32:40]
    two = main[8:16] + main[40:48]
    rest = main[16:24] + main[24:32]
    if low is not None:
        minor = lax.dot_general(left[0:32], low, dims, preferred_element_type=F32)
        one = one + minor[0:8]
        two = two + minor[8:16]
        rest = rest + minor[16:24]
    return one, two, rest


def partner(me, t, count):
    if count & (count - 1) == 0:
        return me ^ abs(t)
    return (me + t + count) % count


def lookup(tables, kinds):
    found = [jnp.zeros(kinds.shape, F32) for _ in tables]
    for kind in range(SPECIES):
        here = kinds == kind
        found = [jnp.where(here, table[kind], x) for table, x in zip(tables, found)]
    return found


def pack_kernel(
    ranks, pos_hbm, charge_hbm, species_hbm, neighbors_hbm, out, pos, charge, species, neighbors, arrived
):
    sources = (pos_hbm, charge_hbm, species_hbm, neighbors_hbm)
    targets = (pos, charge, species, neighbors)
    copies = [
        pltpu.make_async_copy(source, target, arrived.at[i])
        for i, (source, target) in enumerate(zip(sources, targets))
    ]
    for copy in copies:
        copy.start()
    for copy in copies:
        copy.wait()
    dims, beads, _ = pos.shape
    near = neighbors[...].astype(F32)
    shared = [species[...].astype(F32)] + [near[n : n + 1, :] for n in range(near.shape[0])]
    for b in range(beads):
        own = [pos[d, b : b + 1, :] for d in range(dims)] + [charge[b : b + 1, :]]
        for rank in range(b, ranks, beads):
            for i, line in enumerate(own + shared):
                out[rank, i] = line


def weight_kernel(k_index, kernel, pos, species, mass_table, after, out, edges, pull):
    del after
    (mass,) = lookup((mass_table,), species[...])
    pull[...] = time_step / mass
    dims, beads, _ = pos.shape
    for d in range(dims):
        edges[d : d + 1, :] = pos[d, 0:1, :]
        edges[dims + d : dims + d + 1, :] = pos[d, beads - 1 : beads, :]
    count = k_index.shape[1]
    k = k_index[...]
    first, second, third = k[0:1], k[1:2], k[2:3]
    flip = (first < 0) | ((first == 0) & (second < 0))
    sign = jnp.where(flip, -1, 1)
    p, q, r = sign * first, sign * second, sign * third
    wide = 16 * (p - 1)
    with_p = jnp.where(q > 0, wide + q - 1, jnp.where(q < 0, wide + 7 - q, 135 + p))
    without_p = jnp.where(q > 0, 127 + q, 144)
    mode = jnp.where(p > 0, with_p, without_p)
    at = lax.broadcasted_iota(jnp.int32, (MODES, count), 0)
    chosen = jnp.where(at == mode, 1.0, 0.0).astype(BF16)
    row = lax.broadcasted_iota(jnp.int32, (8, count), 0)
    weight = kernel[...]
    here = row + 1 == jnp.abs(r)
    even = jnp.where(here, weight, 0.0)
    odd = jnp.where(here, jnp.where(r < 0, -weight, weight), 0.0)
    zero = jnp.where((row == 0) & (r == 0), weight, 0.0)
    even, odd, zero = product(rows_of(even, odd, zero), chosen, None, NT)
    out[0:8, :] = even
    out[8:16, :] = odd
    out[16:24, :] = zero


def bead_kernel(
    scale,
    inverse_atoms,
    beads,
    rank_ref,
    weights_hbm,
    got,
    chi_hbm,
    hard_hbm,
    bond_hbm,
    *refs,
):
    outs = refs[:beads]
    (
        cos_high,
        cos_low,
        sin_high,
        sin_low,
        left,
        z_cos,
        z_sin,
        charges,
        weights,
        mine,
        kinds,
        chi,
        hard,
        bond,
        chi_table,
        hard_table,
        bond_table,
        arrived,
    ) = refs[beads:]
    bring = [
        pltpu.make_async_copy(source, target, arrived.at[i])
        for i, (source, target) in enumerate(
            (
                (weights_hbm, weights),
                (chi_hbm, chi_table),
                (hard_hbm, hard_table),
                (bond_hbm, bond_table),
            )
        )
    ]
    for copy in bring:
        copy.start()
    ranks, lines, _, width = got.shape
    me = rank_ref[0] % beads
    lane = lax.broadcasted_iota(jnp.int32, (8, width), 1)
    row = lax.broadcasted_iota(jnp.int32, (8, width), 0)
    multiple = (row + 1).astype(F32)
    single = jnp.where(row == 0, 1.0, 0.0)
    blank = jnp.zeros((8, width), F32)

    def at(j):
        return slice(j * width, (j + 1) * width)

    def everywhere(x):
        return jnp.broadcast_to(x, (8, width))

    def column_sum(x):
        return everywhere(jnp.sum(x, axis=0, keepdims=True))

    charge, place = [], []
    for j in range(ranks):
        cx, sx = turns(multiple, got[j, 0])
        cy, sy = turns(multiple, got[j, 1])
        cz, sz = turns(multiple, got[j, 2])
        z_cos[:, at(j)] = cz
        z_sin[:, at(j)] = sz

        def keep(rows, cosine, sine):
            high, low = halves(cosine)
            cos_high[rows, at(j)] = high
            cos_low[rows, at(j)] = low
            high, low = halves(sine)
            sin_high[rows, at(j)] = high
            sin_low[rows, at(j)] = low

        for p in range(8):
            cp, sp = everywhere(cx[p : p + 1]), everywhere(sx[p : p + 1])
            cc, ss, sc, cs = cp * cy, sp * sy, sp * cy, cp * sy
            keep(
                slice(16 * p, 16 * p + 16),
                jnp.concatenate([cc - ss, cc + ss], 0),
                jnp.concatenate([sc + cs, sc - cs], 0),
            )
        keep(slice(128, 144), jnp.concatenate([cy, cx], 0), jnp.concatenate([sy, sx], 0))
        keep(
            slice(144, 160),
            jnp.concatenate([single, blank], 0),
            jnp.concatenate([blank, blank], 0),
        )
        charge.append(everywhere(got[j, 3]))
        kinds[j : j + 1, :] = got[j, 4]
        near = jnp.concatenate([got[j, i] for i in range(5, lines)], 0)
        place.append((lane + near.astype(jnp.int32)) & (width - 1))

    for copy in bring:
        copy.wait()
    chi[...], hardness, bond[...] = lookup((chi_table, hard_table, bond_table), kinds[...])
    hard[...] = mixing / hardness
    even, odd, zero = weights[0:8, :], weights[8:16, :], weights[16:24, :]

    def coefficients(charge):
        for j in range(ranks):
            left[:, at(j)] = rows_of(
                charge[j] * z_cos[:, at(j)], charge[j] * z_sin[:, at(j)], charge[j] * single
            )
        t_cc, t_cs, t_c0 = product(left[...], cos_high[...], cos_low[...], NT)
        t_sc, t_ss, t_s0 = product(left[...], sin_high[...], sin_low[...], NT)
        v_cos = (even * t_cc - odd * t_ss, even * t_cs + odd * t_sc, zero * t_c0)
        v_sin = (even * t_sc + odd * t_cs, even * t_ss - odd * t_cc, zero * t_s0)
        return v_cos, v_sin

    for rounds in range(QITERS):
        v_cos, v_sin = coefficients(charge)
        from_cos = product(rows_of(*v_cos), cos_high[...], cos_low[...], NN)
        from_sin = product(rows_of(*v_sin), sin_high[...], sin_low[...], NN)
        u_c, u_s, u_0 = (a + b for a, b in zip(from_cos, from_sin))
        weighted = [everywhere(bond[j : j + 1, :]) * charge[j] for j in range(ranks)]
        relaxed = []
        total = blank
        for j in range(ranks):
            potential = scale * column_sum(
                z_cos[:, at(j)] * u_c[:, at(j)] + z_sin[:, at(j)] * u_s[:, at(j)] + u_0[:, at(j)]
            )
            before = weighted[(j - 1) % ranks]
            after = weighted[(j + 1) % ranks]
            lower = jnp.where(lane < 3 * width // 4, weighted[j], before)
            upper = jnp.where(lane >= width // 4, weighted[j], after)
            near = jnp.where(
                lane < width // 2,
                jnp.take_along_axis(lower, place[j], axis=1),
                jnp.take_along_axis(upper, place[j], axis=1),
            )
            new = (1.0 - mixing) * charge[j] - everywhere(hard[j : j + 1, :]) * (
                everywhere(chi[j : j + 1, :])
                + potential
                + everywhere(bond[j : j + 1, :]) * column_sum(near)
            )
            relaxed.append(new)
            total = total + new
        mean = jnp.sum(total, axis=1, keepdims=True) * inverse_atoms
        charge = [new - mean for new in relaxed]

    for j in range(ranks):
        charges[:, at(j)] = charge[j]
    (v_cc, v_cs, v_c0), (v_sc, v_ss, v_s0) = coefficients(charge)
    mode = lax.broadcasted_iota(jnp.int32, (8, MODES), 1)
    inner = mode & 15
    wave_x = jnp.where(
        mode < 128, (mode >> 4) + 1, jnp.where((mode >= 136) & (mode < 144), mode - 135, 0)
    ).astype(F32)
    wave_y = jnp.where(
        mode < 128,
        jnp.where(inner < 8, inner + 1, 7 - inner),
        jnp.where(mode < 136, mode - 127, 0),
    ).astype(F32)
    span = beads * width
    base = pl.multiple_of((rank_ref[0] // beads) * span, span)
    own = pl.ds(base, span)
    ch, cl, sh, sl = (ref[:, own] for ref in (cos_high, cos_low, sin_high, sin_low))
    zc, zs, q = z_cos[:, own], z_sin[:, own], charges[:, own]

    v_cos, v_sin = (v_cc, v_cs, v_c0), (v_sc, v_ss, v_s0)
    for_cos, for_sin = [rows_of(*v_cos)], [rows_of(*v_sin)]
    for wave in (wave_x, wave_y):
        for_cos.append(rows_of(*(-wave * v for v in v_sin)))
        for_sin.append(rows_of(*(wave * v for v in v_cos)))
    for_cos, for_sin = jnp.concatenate(for_cos, 0), jnp.concatenate(for_sin, 0)
    fields = sum(
        lax.dot_general(rows, part, NN, preferred_element_type=F32)
        for rows, part in ((for_cos, ch), (for_cos, cl), (for_sin, sh), (for_sin, sl))
    )
    (u_c, u_s, _), (x_c, x_s, x_0), (y_c, y_s, y_0) = (
        (f[0:8] + f[32:40], f[8:16] + f[40:48], f[16:24] + f[24:32])
        for f in (fields[48 * i : 48 * i + 48] for i in range(3))
    )
    along_x = zc * x_c + zs * x_s + x_0
    along_y = zc * y_c + zs * y_s + y_0
    wide_multiple = jnp.broadcast_to(multiple[:, 0:1], (8, span))
    along_z = wide_multiple * (zs * u_c - zc * u_s)
    factor = (two_pi * scale) * q
    for t in range(beads):
        cut = at(t)
        fx, fy, fz = (
            factor[:, cut] * column_sum(f[:, cut]) for f in (along_x, along_y, along_z)
        )
        mine[:, cut] = jnp.where(
            row == 0, fx, jnp.where(row == 1, fy, jnp.where(row == 2, fz, q[:, cut]))
        )
    for t in range(beads):
        there = pl.multiple_of(partner(me, t, beads) * width, width)
        outs[t][...] = mine[0:4, pl.ds(there, width)]


def move_kernel(low_at, high_at, rank_ref, pos, vel, low, high, pull, *refs):
    dims, beads, width = pos.shape
    got, (pos_out, vel_out, charge_out, home) = refs[:beads], refs[beads:]
    me = rank_ref[0] % beads
    for t in range(beads):
        bead = partner(me, -t, beads)
        for d in range(dims + 1):
            home[pl.ds(d * beads + bead, 1), :] = got[t][d : d + 1, :]
    gain = jnp.broadcast_to(pull[...], (beads, width))
    for d in range(dims):
        here = pos[d]
        before = jnp.concatenate([low[low_at + d : low_at + d + 1, :], here[: beads - 1]], 0)
        after = jnp.concatenate([here[1:], high[high_at + d : high_at + d + 1, :]], 0)
        laplace = 2.0 * here - before - after
        force = home[d * beads : (d + 1) * beads, :]
        fresh = vel[d] + (gain * force - (time_step * spring_rate) * laplace)
        vel_out[d] = fresh
        pos_out[d] = here + time_step * fresh
    charge_out[...] = home[dims * beads : (dims + 1) * beads, :]


VMEM = pl.BlockSpec(memory_space=pltpu.VMEM)
SMEM = pl.BlockSpec(memory_space=pltpu.SMEM)
ANY = pl.BlockSpec(memory_space=pl.ANY)
HBM = pl.BlockSpec(memory_space=pltpu.HBM)


def stay(x):
    return pltpu.with_memory_space_constraint(x, pltpu.HBM)


def params(mebibytes):
    return pltpu.CompilerParams(vmem_limit_bytes=mebibytes << 20)


def body(
    positions,
    velocities,
    charges_in,
    species,
    neighbors,
    k_index,
    kernel,
    chi_table,
    hard_table,
    bond_table,
    mass_table,
):
    beads, dims, width = positions.shape
    ranks = lax.axis_size("atoms")
    chain = lax.axis_size("beads")
    atoms = ranks * width
    scale = ewald_gain / math.sqrt(KVEC * atoms)
    kinds = species[None, :]
    shape = jax.ShapeDtypeStruct

    places = positions.transpose(1, 0, 2)
    speeds = velocities.transpose(1, 0, 2)

    rank = lax.axis_index("atoms").astype(jnp.int32)[None]
    def in_group(x, t):
        pairs = [(r, r // beads * beads + partner(r % beads, t, beads)) for r in range(ranks)]
        return lax.ppermute(x, "atoms", pairs)

    lines = dims + 2 + neighbors.shape[0]
    packed = pl.pallas_call(
        functools.partial(pack_kernel, ranks),
        out_shape=pltpu.VMEM((ranks, lines, 1, width), F32),
        in_specs=[HBM] * 4,
        out_specs=VMEM,
        scratch_shapes=[
            pltpu.VMEM(places.shape, F32),
            pltpu.VMEM(charges_in.shape, F32),
            pltpu.VMEM(kinds.shape, jnp.int32),
            pltpu.VMEM(neighbors.shape, jnp.int32),
            pltpu.SemaphoreType.DMA((4,)),
        ],
        compiler_params=params(4),
        name="pack",
    )(*map(stay, (places, charges_in, kinds, neighbors)))
    got = lax.all_to_all(packed, "atoms", 0, 0, tiled=True)

    weights, edges, pull = pl.pallas_call(
        weight_kernel,
        out_shape=(
            shape((24, MODES), F32),
            shape((2 * dims, width), F32),
            shape((1, width), F32),
        ),
        in_specs=[VMEM] * 4 + [SMEM, ANY],
        out_specs=(VMEM, VMEM, VMEM),
        compiler_params=params(8),
        name="weights",
        cost_estimate=pl.CostEstimate(flops=10**9, bytes_accessed=10**5, transcendentals=0),
    )(k_index, kernel[None, :], places, kinds, mass_table, packed)
    if chain == 2:
        low = high = lax.ppermute(edges, "beads", [(0, 1), (1, 0)])
        low_at, high_at = dims, 0
    else:
        forward = [(i, (i + 1) % chain) for i in range(chain)]
        low = lax.ppermute(edges[dims:], "beads", forward)
        high = lax.ppermute(edges[:dims], "beads", [(b, a) for a, b in forward])
        low_at, high_at = 0, 0

    results = pl.pallas_call(
        functools.partial(bead_kernel, scale, 1.0 / atoms, beads),
        out_shape=[shape((4, width), F32)] * beads,
        in_specs=[SMEM, ANY, VMEM] + [HBM] * 3,
        out_specs=[VMEM] * beads,
        scratch_shapes=[
            pltpu.VMEM((MODES, atoms), BF16),
            pltpu.VMEM((MODES, atoms), BF16),
            pltpu.VMEM((MODES, atoms), BF16),
            pltpu.VMEM((MODES, atoms), BF16),
            pltpu.VMEM((48, atoms), BF16),
            pltpu.VMEM((8, atoms), F32),
            pltpu.VMEM((8, atoms), F32),
            pltpu.VMEM((8, atoms), F32),
            pltpu.VMEM((24, MODES), F32),
            pltpu.VMEM((8, beads * width), F32),
            pltpu.VMEM((ranks, width), F32),
            pltpu.VMEM((ranks, width), F32),
            pltpu.VMEM((ranks, width), F32),
            pltpu.VMEM((ranks, width), F32),
            pltpu.SMEM((SPECIES,), F32),
            pltpu.SMEM((SPECIES,), F32),
            pltpu.SMEM((SPECIES,), F32),
            pltpu.SemaphoreType.DMA((4,)),
        ],
        compiler_params=params(24),
        name="bead",
        cost_estimate=pl.CostEstimate(flops=10**10, bytes_accessed=10**6, transcendentals=0),
    )(rank, weights, got, *map(stay, (chi_table, hard_table, bond_table)))

    home = [in_group(results[t], t) for t in range(beads - 1, 0, -1)]
    home = [results[0]] + home[::-1]

    new_places, new_speeds, charge = pl.pallas_call(
        functools.partial(move_kernel, low_at, high_at),
        out_shape=(
            shape(places.shape, F32),
            shape(places.shape, F32),
            shape(charges_in.shape, F32),
        ),
        in_specs=[SMEM] + [VMEM] * (5 + beads),
        out_specs=(VMEM, VMEM, VMEM),
        scratch_shapes=[pltpu.VMEM(((dims + 1) * beads, width), F32)],
        compiler_params=params(4),
        name="move",
    )(rank, places, speeds, low, high, pull, *home)
    return new_places.transpose(1, 0, 2), new_speeds.transpose(1, 0, 2), charge


def solution(mesh):
    return jax.shard_map(
        body,
        mesh=mesh,
        in_specs=(
            P("beads", None, "atoms"),
            P("beads", None, "atoms"),
            P("beads", "atoms"),
            P("atoms"),
            P(None, "atoms"),
            P(),
            P(),
            P(),
            P(),
            P(),
            P(),
        ),
        out_specs=(P("beads", None, "atoms"), P("beads", None, "atoms"), P("beads", "atoms")),
        check_vma=False,
    )
```

```python
import functools
import math

import jax
import jax.numpy as jnp
from jax import lax
from jax.experimental import pallas as pl
from jax.experimental.pallas import tpu as pltpu
from jax.sharding import PartitionSpec as P

KVEC = 2048
QITERS = 2
SPECIES = 8
KMAX = 8
MODES = 160

two_pi = 2.0 * math.pi
ewald_gain = 4.0
mixing = 0.5
spring_rate = 0.5
time_step = 0.05

COS = (
    0.9999999998855522,
    -19.739208743453656,
    64.93938907588092,
    -85.45665831455305,
    60.242131335932854,
    -26.404668174676782,
    7.800131403864327,
    -1.4531122801527303,
)
SIN = (
    6.2831853025115,
    -41.34170040531697,
    81.60513138577565,
    -76.70301535354703,
    42.02592698387527,
    -14.89984666196953,
    3.2381375032044204,
)

F32 = jnp.float32
BF16 = jnp.bfloat16
NT = (((1,), (1,)), ((), ()))
NN = (((1,), (0,)), ((), ()))


def horner(coeffs, x):
    value = jnp.full_like(x, coeffs[-1])
    for coeff in coeffs[-2::-1]:
        value = value * x + coeff
    return value


def turns(multiple, x):
    t = multiple * x
    t = t - jnp.floor(t + 0.5)
    square = t * t
    return horner(COS, square), t * horner(SIN, square)


def halves(x):
    high = x.astype(BF16)
    return high, (x - high.astype(F32)).astype(BF16)


def rows_of(one, two, rest):
    high, low = halves(jnp.concatenate([one, two], 0))
    rest_high = rest.astype(BF16).astype(F32)
    both = jnp.concatenate([rest_high, rest - rest_high], 0).astype(BF16)
    return jnp.concatenate([high, both, low], 0)


def product(left, high, low, dims):
    main = lax.dot_general(left, high, dims, preferred_element_type=F32)
    one = main[0:8] + main[32:40]
    two = main[8:16] + main[40:48]
    rest = main[16:24] + main[24:32]
    if low is not None:
        minor = lax.dot_general(left[0:32], low, dims, preferred_element_type=F32)
        one = one + minor[0:8]
        two = two + minor[8:16]
        rest = rest + minor[16:24]
    return one, two, rest


def partner(me, t, count):
    if count & (count - 1) == 0:
        return me ^ abs(t)
    return (me + t + count) % count


def lookup(tables, kinds):
    found = [jnp.zeros(kinds.shape, F32) for _ in tables]
    for kind in range(SPECIES):
        here = kinds == kind
        found = [jnp.where(here, table[kind], x) for table, x in zip(tables, found)]
    return found


def pack_kernel(
    ranks,
    pos_hbm,
    charge_hbm,
    species_hbm,
    neighbors_hbm,
    out,
    pos,
    charge,
    species,
    neighbors,
    arrived,
):
    sources = (pos_hbm, charge_hbm, species_hbm, neighbors_hbm)
    targets = (pos, charge, species, neighbors)
    copies = [
        pltpu.make_async_copy(source, target, arrived.at[i])
        for i, (source, target) in enumerate(zip(sources, targets))
    ]
    for copy in copies:
        copy.start()
    for copy in copies:
        copy.wait()
    dims, beads, _ = pos.shape
    near = neighbors[...].astype(F32)
    spec = species[...].astype(F32)
    for b in range(beads):
        for d in range(dims):
            out[b, d] = pos[d, b : b + 1, :]
        out[b, dims] = charge[b : b + 1, :]
        out[b, dims + 1] = spec
        for n in range(near.shape[0]):
            out[b, dims + 2 + n] = near[n : n + 1, :]
    for rank in range(beads, ranks):
        out[rank] = out[rank % beads]


def weight_kernel(k_index, kernel, pos, species, mass_table, after, out, edges, pull):
    del after
    (mass,) = lookup((mass_table,), species[...])
    pull[...] = time_step / mass
    dims, beads, _ = pos.shape
    for d in range(dims):
        edges[d : d + 1, :] = pos[d, 0:1, :]
        edges[dims + d : dims + d + 1, :] = pos[d, beads - 1 : beads, :]
    count = k_index.shape[1]
    k = k_index[...]
    first, second, third = k[0:1], k[1:2], k[2:3]
    flip = (first < 0) | ((first == 0) & (second < 0))
    sign = jnp.where(flip, -1, 1)
    p, q, r = sign * first, sign * second, sign * third
    wide = 16 * (p - 1)
    with_p = jnp.where(q > 0, wide + q - 1, jnp.where(q < 0, wide + 7 - q, 135 + p))
    without_p = jnp.where(q > 0, 127 + q, 144)
    mode = jnp.where(p > 0, with_p, without_p)
    at = lax.broadcasted_iota(jnp.int32, (MODES, count), 0)
    chosen = jnp.where(at == mode, 1.0, 0.0).astype(BF16)
    row = lax.broadcasted_iota(jnp.int32, (8, count), 0)
    weight = kernel[...]
    here = row + 1 == jnp.abs(r)
    even = jnp.where(here, weight, 0.0)
    odd = jnp.where(here, jnp.where(r < 0, -weight, weight), 0.0)
    zero = jnp.where((row == 0) & (r == 0), weight, 0.0)
    even, odd, zero = product(rows_of(even, odd, zero), chosen, None, NT)
    out[0:8, :] = even
    out[8:16, :] = odd
    out[16:24, :] = zero


def bead_kernel(
    scale,
    inverse_atoms,
    beads,
    rank_ref,
    weights_hbm,
    got,
    chi_hbm,
    hard_hbm,
    bond_hbm,
    *refs,
):
    outs = refs[:beads]
    (
        cos_high,
        cos_low,
        sin_high,
        sin_low,
        left,
        z_cos,
        z_sin,
        charges,
        weights,
        mine,
        kinds,
        chi,
        hard,
        bond,
        chi_table,
        hard_table,
        bond_table,
        arrived,
    ) = refs[beads:]
    bring = [
        pltpu.make_async_copy(source, target, arrived.at[i])
        for i, (source, target) in enumerate(
            (
                (weights_hbm, weights),
                (chi_hbm, chi_table),
                (hard_hbm, hard_table),
                (bond_hbm, bond_table),
            )
        )
    ]
    for copy in bring:
        copy.start()
    ranks, lines, _, width = got.shape
    me = rank_ref[0] % beads
    lane = lax.broadcasted_iota(jnp.int32, (8, width), 1)
    row = lax.broadcasted_iota(jnp.int32, (8, width), 0)
    multiple = (row + 1).astype(F32)
    single = jnp.where(row == 0, 1.0, 0.0)
    blank = jnp.zeros((8, width), F32)

    def at(j):
        return slice(j * width, (j + 1) * width)

    def everywhere(x):
        return jnp.broadcast_to(x, (8, width))

    def column_sum(x):
        return everywhere(jnp.sum(x, axis=0, keepdims=True))

    charge, place = [], []
    for j in range(ranks):
        cx, sx = turns(multiple, got[j, 0])
        cy, sy = turns(multiple, got[j, 1])
        cz, sz = turns(multiple, got[j, 2])
        z_cos[:, at(j)] = cz
        z_sin[:, at(j)] = sz

        def keep(rows, cosine, sine):
            high, low = halves(cosine)
            cos_high[rows, at(j)] = high
            cos_low[rows, at(j)] = low
            high, low = halves(sine)
            sin_high[rows, at(j)] = high
            sin_low[rows, at(j)] = low

        for p in range(8):
            cp, sp = everywhere(cx[p : p + 1]), everywhere(sx[p : p + 1])
            cc, ss, sc, cs = cp * cy, sp * sy, sp * cy, cp * sy
            keep(
                slice(16 * p, 16 * p + 16),
                jnp.concatenate([cc - ss, cc + ss], 0),
                jnp.concatenate([sc + cs, sc - cs], 0),
            )
        keep(slice(128, 144), jnp.concatenate([cy, cx], 0), jnp.concatenate([sy, sx], 0))
        keep(
            slice(144, 160),
            jnp.concatenate([single, blank], 0),
            jnp.concatenate([blank, blank], 0),
        )
        charge.append(everywhere(got[j, 3]))
        kinds[j : j + 1, :] = got[j, 4]
        near = jnp.concatenate([got[j, i] for i in range(5, lines)], 0)
        place.append((lane + near.astype(jnp.int32)) & (width - 1))

    for copy in bring:
        copy.wait()
    chi[...], hardness, bond[...] = lookup((chi_table, hard_table, bond_table), kinds[...])
    hard[...] = mixing / hardness
    even, odd, zero = weights[0:8, :], weights[8:16, :], weights[16:24, :]

    def coefficients(charge):
        for j in range(ranks):
            left[:, at(j)] = rows_of(
                charge[j] * z_cos[:, at(j)], charge[j] * z_sin[:, at(j)], charge[j] * single
            )
        t_cc, t_cs, t_c0 = product(left[...], cos_high[...], cos_low[...], NT)
        t_sc, t_ss, t_s0 = product(left[...], sin_high[...], sin_low[...], NT)
        v_cos = (even * t_cc - odd * t_ss, even * t_cs + odd * t_sc, zero * t_c0)
        v_sin = (even * t_sc + odd * t_cs, even * t_ss - odd * t_cc, zero * t_s0)
        return v_cos, v_sin

    for rounds in range(QITERS):
        v_cos, v_sin = coefficients(charge)
        rows_cos, rows_sin = rows_of(*v_cos), rows_of(*v_sin)
        potential = []
        for j in range(0, ranks, 2):
            cut = slice(j * width, (j + 2) * width)
            from_cos = product(rows_cos, cos_high[:, cut], cos_low[:, cut], NN)
            from_sin = product(rows_sin, sin_high[:, cut], sin_low[:, cut], NN)
            u_c, u_s, u_0 = (a + b for a, b in zip(from_cos, from_sin))
            terms = z_cos[:, cut] * u_c + z_sin[:, cut] * u_s + u_0
            potential += [scale * column_sum(terms[:, :width]), scale * column_sum(terms[:, width:])]
        weighted = [everywhere(bond[j : j + 1, :]) * charge[j] for j in range(ranks)]
        relaxed = []
        total = blank
        for j in range(ranks):
            before = weighted[(j - 1) % ranks]
            after = weighted[(j + 1) % ranks]
            lower = jnp.where(lane < 3 * width // 4, weighted[j], before)
            upper = jnp.where(lane >= width // 4, weighted[j], after)
            near = jnp.where(
                lane < width // 2,
                jnp.take_along_axis(lower, place[j], axis=1),
                jnp.take_along_axis(upper, place[j], axis=1),
            )
            new = (1.0 - mixing) * charge[j] - everywhere(hard[j : j + 1, :]) * (
                everywhere(chi[j : j + 1, :])
                + potential[j]
                + everywhere(bond[j : j + 1, :]) * column_sum(near)
            )
            relaxed.append(new)
            total = total + new
        mean = jnp.sum(total, axis=1, keepdims=True) * inverse_atoms
        charge = [new - mean for new in relaxed]

    for j in range(ranks):
        charges[:, at(j)] = charge[j]
    (v_cc, v_cs, v_c0), (v_sc, v_ss, v_s0) = coefficients(charge)
    mode = lax.broadcasted_iota(jnp.int32, (8, MODES), 1)
    inner = mode & 15
    wave_x = jnp.where(
        mode < 128, (mode >> 4) + 1, jnp.where((mode >= 136) & (mode < 144), mode - 135, 0)
    ).astype(F32)
    wave_y = jnp.where(
        mode < 128,
        jnp.where(inner < 8, inner + 1, 7 - inner),
        jnp.where(mode < 136, mode - 127, 0),
    ).astype(F32)
    span = beads * width
    base = pl.multiple_of((rank_ref[0] // beads) * span, span)
    own = pl.ds(base, span)
    ch, cl, sh, sl = (ref[:, own] for ref in (cos_high, cos_low, sin_high, sin_low))
    zc, zs, q = z_cos[:, own], z_sin[:, own], charges[:, own]

    v_cos, v_sin = (v_cc, v_cs, v_c0), (v_sc, v_ss, v_s0)
    for_cos, for_sin = [rows_of(*v_cos)], [rows_of(*v_sin)]
    for wave in (wave_x, wave_y):
        for_cos.append(rows_of(*(-wave * v for v in v_sin)))
        for_sin.append(rows_of(*(wave * v for v in v_cos)))
    for_cos, for_sin = jnp.concatenate(for_cos, 0), jnp.concatenate(for_sin, 0)
    fields = sum(
        lax.dot_general(rows, part, NN, preferred_element_type=F32)
        for rows, part in ((for_cos, ch), (for_cos, cl), (for_sin, sh), (for_sin, sl))
    )
    (u_c, u_s, _), (x_c, x_s, x_0), (y_c, y_s, y_0) = (
        (f[0:8] + f[32:40], f[8:16] + f[40:48], f[16:24] + f[24:32])
        for f in (fields[48 * i : 48 * i + 48] for i in range(3))
    )
    along_x = zc * x_c + zs * x_s + x_0
    along_y = zc * y_c + zs * y_s + y_0
    wide_multiple = jnp.broadcast_to(multiple[:, 0:1], (8, span))
    along_z = wide_multiple * (zs * u_c - zc * u_s)
    factor = (two_pi * scale) * q
    for t in range(beads):
        cut = at(t)
        fx, fy, fz = (
            factor[:, cut] * column_sum(f[:, cut]) for f in (along_x, along_y, along_z)
        )
        mine[:, cut] = jnp.where(
            row == 0, fx, jnp.where(row == 1, fy, jnp.where(row == 2, fz, q[:, cut]))
        )
    for t in range(beads):
        there = pl.multiple_of(partner(me, t, beads) * width, width)
        outs[t][...] = mine[0:4, pl.ds(there, width)]


def move_kernel(low_at, high_at, rank_ref, pos, vel, low, high, pull, *refs):
    dims, beads, width = pos.shape
    got, (pos_out, vel_out, charge_out, home) = refs[:beads], refs[beads:]
    me = rank_ref[0] % beads
    for t in range(beads):
        bead = partner(me, -t, beads)
        for d in range(dims + 1):
            home[pl.ds(d * beads + bead, 1), :] = got[t][d : d + 1, :]
    gain = jnp.broadcast_to(pull[...], (beads, width))
    for d in range(dims):
        here = pos[d]
        before = jnp.concatenate([low[low_at + d : low_at + d + 1, :], here[: beads - 1]], 0)
        after = jnp.concatenate([here[1:], high[high_at + d : high_at + d + 1, :]], 0)
        laplace = 2.0 * here - before - after
        force = home[d * beads : (d + 1) * beads, :]
        fresh = vel[d] + (gain * force - (time_step * spring_rate) * laplace)
        vel_out[d] = fresh
        pos_out[d] = here + time_step * fresh
    charge_out[...] = home[dims * beads : (dims + 1) * beads, :]


VMEM = pl.BlockSpec(memory_space=pltpu.VMEM)
SMEM = pl.BlockSpec(memory_space=pltpu.SMEM)
ANY = pl.BlockSpec(memory_space=pl.ANY)
HBM = pl.BlockSpec(memory_space=pltpu.HBM)


def stay(x):
    return pltpu.with_memory_space_constraint(x, pltpu.HBM)


def params(mebibytes):
    return pltpu.CompilerParams(vmem_limit_bytes=mebibytes << 20)


def body(
    positions,
    velocities,
    charges_in,
    species,
    neighbors,
    k_index,
    kernel,
    chi_table,
    hard_table,
    bond_table,
    mass_table,
):
    beads, dims, width = positions.shape
    ranks = lax.axis_size("atoms")
    chain = lax.axis_size("beads")
    atoms = ranks * width
    scale = ewald_gain / math.sqrt(KVEC * atoms)
    kinds = species[None, :]
    shape = jax.ShapeDtypeStruct

    places = positions.transpose(1, 0, 2)
    speeds = velocities.transpose(1, 0, 2)

    rank = lax.axis_index("atoms").astype(jnp.int32)[None]
    def in_group(x, t):
        pairs = [(r, r // beads * beads + partner(r % beads, t, beads)) for r in range(ranks)]
        return lax.ppermute(x, "atoms", pairs)

    lines = dims + 2 + neighbors.shape[0]
    packed = pl.pallas_call(
        functools.partial(pack_kernel, ranks),
        out_shape=pltpu.VMEM((ranks, lines, 1, width), F32),
        in_specs=[HBM] * 4,
        out_specs=VMEM,
        scratch_shapes=[
            pltpu.VMEM(places.shape, F32),
            pltpu.VMEM(charges_in.shape, F32),
            pltpu.VMEM(kinds.shape, jnp.int32),
            pltpu.VMEM(neighbors.shape, jnp.int32),
            pltpu.SemaphoreType.DMA((4,)),
        ],
        compiler_params=params(4),
        name="pack",
    )(*map(stay, (places, charges_in, kinds, neighbors)))
    got = lax.all_to_all(packed, "atoms", 0, 0, tiled=True)

    weights, edges, pull = pl.pallas_call(
        weight_kernel,
        out_shape=(
            shape((24, MODES), F32),
            shape((2 * dims, width), F32),
            shape((1, width), F32),
        ),
        in_specs=[VMEM] * 4 + [SMEM, ANY],
        out_specs=(VMEM, VMEM, VMEM),
        compiler_params=params(8),
        name="weights",
        cost_estimate=pl.CostEstimate(flops=10**9, bytes_accessed=10**5, transcendentals=0),
    )(k_index, kernel[None, :], places, kinds, mass_table, packed)
    if chain == 2:
        low = high = lax.ppermute(edges, "beads", [(0, 1), (1, 0)])
        low_at, high_at = dims, 0
    else:
        forward = [(i, (i + 1) % chain) for i in range(chain)]
        low = lax.ppermute(edges[dims:], "beads", forward)
        high = lax.ppermute(edges[:dims], "beads", [(b, a) for a, b in forward])
        low_at, high_at = 0, 0

    results = pl.pallas_call(
        functools.partial(bead_kernel, scale, 1.0 / atoms, beads),
        out_shape=[shape((4, width), F32)] * beads,
        in_specs=[SMEM, ANY, VMEM] + [HBM] * 3,
        out_specs=[VMEM] * beads,
        scratch_shapes=[
            pltpu.VMEM((MODES, atoms), BF16),
            pltpu.VMEM((MODES, atoms), BF16),
            pltpu.VMEM((MODES, atoms), BF16),
            pltpu.VMEM((MODES, atoms), BF16),
            pltpu.VMEM((48, atoms), BF16),
            pltpu.VMEM((8, atoms), F32),
            pltpu.VMEM((8, atoms), F32),
            pltpu.VMEM((8, atoms), F32),
            pltpu.VMEM((24, MODES), F32),
            pltpu.VMEM((8, beads * width), F32),
            pltpu.VMEM((ranks, width), F32),
            pltpu.VMEM((ranks, width), F32),
            pltpu.VMEM((ranks, width), F32),
            pltpu.VMEM((ranks, width), F32),
            pltpu.SMEM((SPECIES,), F32),
            pltpu.SMEM((SPECIES,), F32),
            pltpu.SMEM((SPECIES,), F32),
            pltpu.SemaphoreType.DMA((4,)),
        ],
        compiler_params=params(24),
        name="bead",
        cost_estimate=pl.CostEstimate(flops=10**10, bytes_accessed=10**6, transcendentals=0),
    )(rank, weights, got, *map(stay, (chi_table, hard_table, bond_table)))

    home = [in_group(results[t], t) for t in range(beads - 1, 0, -1)]
    home = [results[0]] + home[::-1]

    new_places, new_speeds, charge = pl.pallas_call(
        functools.partial(move_kernel, low_at, high_at),
        out_shape=(
            shape(places.shape, F32),
            shape(places.shape, F32),
            shape(charges_in.shape, F32),
        ),
        in_specs=[SMEM] + [VMEM] * (5 + beads),
        out_specs=(VMEM, VMEM, VMEM),
        scratch_shapes=[pltpu.VMEM(((dims + 1) * beads, width), F32)],
        compiler_params=params(4),
        name="move",
    )(rank, places, speeds, low, high, pull, *home)
    return new_places.transpose(1, 0, 2), new_speeds.transpose(1, 0, 2), charge


def solution(mesh):
    return jax.shard_map(
        body,
        mesh=mesh,
        in_specs=(
            P("beads", None, "atoms"),
            P("beads", None, "atoms"),
            P("beads", "atoms"),
            P("atoms"),
            P(None, "atoms"),
            P(),
            P(),
            P(),
            P(),
            P(),
            P(),
        ),
        out_specs=(P("beads", None, "atoms"), P("beads", None, "atoms"), P("beads", "atoms")),
        check_vma=False,
    )
```

```python
import functools
import math

import jax
import jax.numpy as jnp
from jax import lax
from jax.experimental import pallas as pl
from jax.experimental.pallas import tpu as pltpu
from jax.sharding import PartitionSpec as P

KVEC = 2048
QITERS = 2
SPECIES = 8
KMAX = 8
MODES = 160

two_pi = 2.0 * math.pi
ewald_gain = 4.0
mixing = 0.5
spring_rate = 0.5
time_step = 0.05

COS = (
    0.9999999998855522,
    -19.739208743453656,
    64.93938907588092,
    -85.45665831455305,
    60.242131335932854,
    -26.404668174676782,
    7.800131403864327,
    -1.4531122801527303,
)
SIN = (
    6.2831853025115,
    -41.34170040531697,
    81.60513138577565,
    -76.70301535354703,
    42.02592698387527,
    -14.89984666196953,
    3.2381375032044204,
)

F32 = jnp.float32
BF16 = jnp.bfloat16
NT = (((1,), (1,)), ((), ()))
NN = (((1,), (0,)), ((), ()))


def horner(coeffs, x):
    value = jnp.full_like(x, coeffs[-1])
    for coeff in coeffs[-2::-1]:
        value = value * x + coeff
    return value


def turns(multiple, x):
    t = multiple * x
    t = t - jnp.floor(t + 0.5)
    square = t * t
    return horner(COS, square), t * horner(SIN, square)


def halves(x):
    high = x.astype(BF16)
    return high, (x - high.astype(F32)).astype(BF16)


def rows_of(one, two, rest):
    high, low = halves(jnp.concatenate([one, two], 0))
    rest_high = rest.astype(BF16).astype(F32)
    both = jnp.concatenate([rest_high, rest - rest_high], 0).astype(BF16)
    return jnp.concatenate([high, both, low], 0)


def product(left, high, low, dims):
    main = lax.dot_general(left, high, dims, preferred_element_type=F32)
    one = main[0:8] + main[32:40]
    two = main[8:16] + main[40:48]
    rest = main[16:24] + main[24:32]
    if low is not None:
        minor = lax.dot_general(left[0:32], low, dims, preferred_element_type=F32)
        one = one + minor[0:8]
        two = two + minor[8:16]
        rest = rest + minor[16:24]
    return one, two, rest


def partner(me, t, count):
    if count & (count - 1) == 0:
        return me ^ abs(t)
    return (me + t + count) % count


def lookup(tables, kinds):
    found = [jnp.zeros(kinds.shape, F32) for _ in tables]
    for kind in range(SPECIES):
        here = kinds == kind
        found = [jnp.where(here, table[kind], x) for table, x in zip(tables, found)]
    return found


def pack_kernel(
    pos_hbm,
    charge_hbm,
    species_hbm,
    neighbors_hbm,
    chi_hbm,
    hard_hbm,
    bond_hbm,
    out,
    pos,
    charge,
    species,
    neighbors,
    chi_table,
    hard_table,
    bond_table,
    arrived,
):
    sources = (pos_hbm, charge_hbm, species_hbm, neighbors_hbm, chi_hbm, hard_hbm, bond_hbm)
    targets = (pos, charge, species, neighbors, chi_table, hard_table, bond_table)
    copies = [
        pltpu.make_async_copy(source, target, arrived.at[i])
        for i, (source, target) in enumerate(zip(sources, targets))
    ]
    for copy in copies:
        copy.start()
    for copy in copies:
        copy.wait()
    dims, beads, width = pos.shape
    chi, hard, bond = lookup((chi_table, hard_table, bond_table), species[...])
    shared = [chi, mixing / hard, bond, jnp.zeros((1, width), F32)]
    for b in range(beads):
        own = [pos[d, b : b + 1, :] for d in range(dims)] + [charge[b : b + 1, :]]
        out[b] = jnp.concatenate(own + shared, 0)
    out[beads] = neighbors[...].astype(F32)


def sort_kernel(beads, groups, rank_ref, *refs):
    got, outs = refs[:groups], refs[groups:]
    me, group = rank_ref[0] % beads, rank_ref[0] // beads
    for k in range(groups):
        source = partner(group, -k, groups)
        near = got[k][beads]
        for t in range(beads):
            outs[t][source, 0:8, :] = near
            outs[t][source, 8:16, :] = got[k][partner(me, t, beads)]


def weight_kernel(k_index, kernel, pos, species, mass_table, after, out, edges, pull):
    del after
    (mass,) = lookup((mass_table,), species[...])
    pull[...] = time_step / mass
    dims, beads, _ = pos.shape
    for d in range(dims):
        edges[d : d + 1, :] = pos[d, 0:1, :]
        edges[dims + d : dims + d + 1, :] = pos[d, beads - 1 : beads, :]
    count = k_index.shape[1]
    k = k_index[...]
    first, second, third = k[0:1], k[1:2], k[2:3]
    flip = (first < 0) | ((first == 0) & (second < 0))
    sign = jnp.where(flip, -1, 1)
    p, q, r = sign * first, sign * second, sign * third
    wide = 16 * (p - 1)
    with_p = jnp.where(q > 0, wide + q - 1, jnp.where(q < 0, wide + 7 - q, 135 + p))
    without_p = jnp.where(q > 0, 127 + q, 144)
    mode = jnp.where(p > 0, with_p, without_p)
    at = lax.broadcasted_iota(jnp.int32, (MODES, count), 0)
    chosen = jnp.where(at == mode, 1.0, 0.0).astype(BF16)
    row = lax.broadcasted_iota(jnp.int32, (8, count), 0)
    weight = kernel[...]
    here = row + 1 == jnp.abs(r)
    even = jnp.where(here, weight, 0.0)
    odd = jnp.where(here, jnp.where(r < 0, -weight, weight), 0.0)
    zero = jnp.where((row == 0) & (r == 0), weight, 0.0)
    even, odd, zero = product(rows_of(even, odd, zero), chosen, None, NT)
    out[0:8, :] = even
    out[8:16, :] = odd
    out[16:24, :] = zero


def bead_kernel(
    scale,
    inverse_atoms,
    beads,
    rank_ref,
    weights_hbm,
    *refs,
):
    blocks, outs = refs[:beads], refs[beads : 2 * beads]
    (
        got,
        cos_high,
        cos_low,
        sin_high,
        sin_low,
        left,
        z_cos,
        z_sin,
        charges,
        weights,
        mine,
        arrived,
    ) = refs[2 * beads :]
    bring = pltpu.make_async_copy(weights_hbm, weights, arrived)
    bring.start()
    ranks, _, width = got.shape
    me = rank_ref[0] % beads
    for t in range(beads):
        source = partner(me, -t, beads)
        for group in range(ranks // beads):
            got[group * beads + source] = blocks[t][group]
    lane = lax.broadcasted_iota(jnp.int32, (8, width), 1)
    row = lax.broadcasted_iota(jnp.int32, (8, width), 0)
    multiple = (row + 1).astype(F32)
    single = jnp.where(row == 0, 1.0, 0.0)
    blank = jnp.zeros((8, width), F32)

    def at(j):
        return slice(j * width, (j + 1) * width)

    def everywhere(x):
        return jnp.broadcast_to(x, (8, width))

    def column_sum(x):
        return everywhere(jnp.sum(x, axis=0, keepdims=True))

    chi, hard, bond, charge = [], [], [], []
    for j in range(ranks):
        cx, sx = turns(multiple, got[j, 8:9, :])
        cy, sy = turns(multiple, got[j, 9:10, :])
        cz, sz = turns(multiple, got[j, 10:11, :])
        z_cos[:, at(j)] = cz
        z_sin[:, at(j)] = sz

        def keep(rows, cosine, sine):
            high, low = halves(cosine)
            cos_high[rows, at(j)] = high
            cos_low[rows, at(j)] = low
            high, low = halves(sine)
            sin_high[rows, at(j)] = high
            sin_low[rows, at(j)] = low

        for p in range(8):
            cp, sp = everywhere(cx[p : p + 1]), everywhere(sx[p : p + 1])
            cc, ss, sc, cs = cp * cy, sp * sy, sp * cy, cp * sy
            keep(
                slice(16 * p, 16 * p + 16),
                jnp.concatenate([cc - ss, cc + ss], 0),
                jnp.concatenate([sc + cs, sc - cs], 0),
            )
        keep(slice(128, 144), jnp.concatenate([cy, cx], 0), jnp.concatenate([sy, sx], 0))
        keep(
            slice(144, 160),
            jnp.concatenate([single, blank], 0),
            jnp.concatenate([blank, blank], 0),
        )
        charge.append(everywhere(got[j, 11:12, :]))
        chi.append(everywhere(got[j, 12:13, :]))
        hard.append(everywhere(got[j, 13:14, :]))
        bond.append(everywhere(got[j, 14:15, :]))

    bring.wait()
    even, odd, zero = weights[0:8, :], weights[8:16, :], weights[16:24, :]

    def coefficients(charge):
        for j in range(ranks):
            left[:, at(j)] = rows_of(
                charge[j] * z_cos[:, at(j)], charge[j] * z_sin[:, at(j)], charge[j] * single
            )
        t_cc, t_cs, t_c0 = product(left[...], cos_high[...], cos_low[...], NT)
        t_sc, t_ss, t_s0 = product(left[...], sin_high[...], sin_low[...], NT)
        v_cos = (even * t_cc - odd * t_ss, even * t_cs + odd * t_sc, zero * t_c0)
        v_sin = (even * t_sc + odd * t_cs, even * t_ss - odd * t_cc, zero * t_s0)
        return v_cos, v_sin

    for rounds in range(QITERS):
        v_cos, v_sin = coefficients(charge)
        from_cos = product(rows_of(*v_cos), cos_high[...], cos_low[...], NN)
        from_sin = product(rows_of(*v_sin), sin_high[...], sin_low[...], NN)
        u_c, u_s, u_0 = (a + b for a, b in zip(from_cos, from_sin))
        weighted = [b * q for b, q in zip(bond, charge)]
        relaxed = []
        total = blank
        for j in range(ranks):
            potential = scale * column_sum(
                z_cos[:, at(j)] * u_c[:, at(j)] + z_sin[:, at(j)] * u_s[:, at(j)] + u_0[:, at(j)]
            )
            before = weighted[(j - 1) % ranks]
            after = weighted[(j + 1) % ranks]
            lower = jnp.where(lane < 3 * width // 4, weighted[j], before)
            upper = jnp.where(lane >= width // 4, weighted[j], after)
            place = (lane + got[j, 0:8, :].astype(jnp.int32)) & (width - 1)
            near = jnp.where(
                lane < width // 2,
                jnp.take_along_axis(lower, place, axis=1),
                jnp.take_along_axis(upper, place, axis=1),
            )
            new = (1.0 - mixing) * charge[j] - hard[j] * (
                chi[j] + potential + bond[j] * column_sum(near)
            )
            relaxed.append(new)
            total = total + new
        mean = jnp.sum(total, axis=1, keepdims=True) * inverse_atoms
        charge = [new - mean for new in relaxed]

    for j in range(ranks):
        charges[:, at(j)] = charge[j]
    (v_cc, v_cs, v_c0), (v_sc, v_ss, v_s0) = coefficients(charge)
    mode = lax.broadcasted_iota(jnp.int32, (8, MODES), 1)
    inner = mode & 15
    wave_x = jnp.where(
        mode < 128, (mode >> 4) + 1, jnp.where((mode >= 136) & (mode < 144), mode - 135, 0)
    ).astype(F32)
    wave_y = jnp.where(
        mode < 128,
        jnp.where(inner < 8, inner + 1, 7 - inner),
        jnp.where(mode < 136, mode - 127, 0),
    ).astype(F32)
    span = beads * width
    base = pl.multiple_of((rank_ref[0] // beads) * span, span)
    own = pl.ds(base, span)
    ch, cl, sh, sl = (ref[:, own] for ref in (cos_high, cos_low, sin_high, sin_low))
    zc, zs, q = z_cos[:, own], z_sin[:, own], charges[:, own]

    v_cos, v_sin = (v_cc, v_cs, v_c0), (v_sc, v_ss, v_s0)
    for_cos, for_sin = [rows_of(*v_cos)], [rows_of(*v_sin)]
    for wave in (wave_x, wave_y):
        for_cos.append(rows_of(*(-wave * v for v in v_sin)))
        for_sin.append(rows_of(*(wave * v for v in v_cos)))
    for_cos, for_sin = jnp.concatenate(for_cos, 0), jnp.concatenate(for_sin, 0)
    fields = sum(
        lax.dot_general(rows, part, NN, preferred_element_type=F32)
        for rows, part in ((for_cos, ch), (for_cos, cl), (for_sin, sh), (for_sin, sl))
    )
    (u_c, u_s, _), (x_c, x_s, x_0), (y_c, y_s, y_0) = (
        (f[0:8] + f[32:40], f[8:16] + f[40:48], f[16:24] + f[24:32])
        for f in (fields[48 * i : 48 * i + 48] for i in range(3))
    )
    along_x = zc * x_c + zs * x_s + x_0
    along_y = zc * y_c + zs * y_s + y_0
    wide_multiple = jnp.broadcast_to(multiple[:, 0:1], (8, span))
    along_z = wide_multiple * (zs * u_c - zc * u_s)
    factor = (two_pi * scale) * q
    for t in range(beads):
        cut = at(t)
        fx, fy, fz = (
            factor[:, cut] * column_sum(f[:, cut]) for f in (along_x, along_y, along_z)
        )
        mine[:, cut] = jnp.where(
            row == 0, fx, jnp.where(row == 1, fy, jnp.where(row == 2, fz, q[:, cut]))
        )
    for t in range(beads):
        there = pl.multiple_of(partner(me, t, beads) * width, width)
        outs[t][...] = mine[0:4, pl.ds(there, width)]


def move_kernel(low_at, high_at, rank_ref, pos, vel, low, high, pull, *refs):
    dims, beads, width = pos.shape
    got, (pos_out, vel_out, charge_out, home) = refs[:beads], refs[beads:]
    me = rank_ref[0] % beads
    for t in range(beads):
        bead = partner(me, -t, beads)
        for d in range(dims + 1):
            home[pl.ds(d * beads + bead, 1), :] = got[t][d : d + 1, :]
    gain = jnp.broadcast_to(pull[...], (beads, width))
    for d in range(dims):
        here = pos[d]
        before = jnp.concatenate([low[low_at + d : low_at + d + 1, :], here[: beads - 1]], 0)
        after = jnp.concatenate([here[1:], high[high_at + d : high_at + d + 1, :]], 0)
        laplace = 2.0 * here - before - after
        force = home[d * beads : (d + 1) * beads, :]
        fresh = vel[d] + (gain * force - (time_step * spring_rate) * laplace)
        vel_out[d] = fresh
        pos_out[d] = here + time_step * fresh
    charge_out[...] = home[dims * beads : (dims + 1) * beads, :]


VMEM = pl.BlockSpec(memory_space=pltpu.VMEM)
SMEM = pl.BlockSpec(memory_space=pltpu.SMEM)
ANY = pl.BlockSpec(memory_space=pl.ANY)
HBM = pl.BlockSpec(memory_space=pltpu.HBM)


def stay(x):
    return pltpu.with_memory_space_constraint(x, pltpu.HBM)


def params(mebibytes):
    return pltpu.CompilerParams(vmem_limit_bytes=mebibytes << 20)


def body(
    positions,
    velocities,
    charges_in,
    species,
    neighbors,
    k_index,
    kernel,
    chi_table,
    hard_table,
    bond_table,
    mass_table,
):
    beads, dims, width = positions.shape
    ranks = lax.axis_size("atoms")
    chain = lax.axis_size("beads")
    atoms = ranks * width
    scale = ewald_gain / math.sqrt(KVEC * atoms)
    kinds = species[None, :]
    shape = jax.ShapeDtypeStruct

    places = positions.transpose(1, 0, 2)
    speeds = velocities.transpose(1, 0, 2)

    rank = lax.axis_index("atoms").astype(jnp.int32)[None]
    groups = ranks // beads

    def among_groups(x, k):
        pairs = [(r, partner(r // beads, k, groups) * beads + r % beads) for r in range(ranks)]
        return lax.ppermute(x, "atoms", pairs)

    def in_group(x, t):
        pairs = [(r, r // beads * beads + partner(r % beads, t, beads)) for r in range(ranks)]
        return lax.ppermute(x, "atoms", pairs)

    packed = pl.pallas_call(
        pack_kernel,
        out_shape=shape((beads + 1, 8, width), F32),
        in_specs=[HBM] * 7,
        out_specs=VMEM,
        scratch_shapes=[
            pltpu.VMEM(places.shape, F32),
            pltpu.VMEM(charges_in.shape, F32),
            pltpu.VMEM(kinds.shape, jnp.int32),
            pltpu.VMEM(neighbors.shape, jnp.int32),
            pltpu.SMEM((SPECIES,), F32),
            pltpu.SMEM((SPECIES,), F32),
            pltpu.SMEM((SPECIES,), F32),
            pltpu.SemaphoreType.DMA((7,)),
        ],
        compiler_params=params(4),
        name="pack",
    )(*map(stay, (places, charges_in, kinds, neighbors, chi_table, hard_table, bond_table)))
    if groups & (groups - 1) == 0:
        known, step = {0: packed}, groups // 2
        while step:
            known.update({k ^ step: among_groups(x, step) for k, x in known.items()})
            step //= 2
        gathered = [known[k] for k in range(groups)]
    else:
        gathered = [packed] + [among_groups(packed, k) for k in range(1, groups)]
    sorted_blocks = pl.pallas_call(
        functools.partial(sort_kernel, beads, groups),
        out_shape=[shape((groups, 16, width), F32)] * beads,
        in_specs=[SMEM] + [VMEM] * groups,
        out_specs=[VMEM] * beads,
        compiler_params=params(4),
        name="sort",
    )(rank, *gathered)
    blocks = [sorted_blocks[0]] + [in_group(sorted_blocks[t], t) for t in range(1, beads)]

    weights, edges, pull = pl.pallas_call(
        weight_kernel,
        out_shape=(
            shape((24, MODES), F32),
            shape((2 * dims, width), F32),
            shape((1, width), F32),
        ),
        in_specs=[VMEM] * 4 + [SMEM, ANY],
        out_specs=(VMEM, VMEM, VMEM),
        compiler_params=params(8),
        name="weights",
        cost_estimate=pl.CostEstimate(flops=10**9, bytes_accessed=10**5, transcendentals=0),
    )(k_index, kernel[None, :], places, kinds, mass_table, packed)
    if chain == 2:
        low = high = lax.ppermute(edges, "beads", [(0, 1), (1, 0)])
        low_at, high_at = dims, 0
    else:
        forward = [(i, (i + 1) % chain) for i in range(chain)]
        low = lax.ppermute(edges[dims:], "beads", forward)
        high = lax.ppermute(edges[:dims], "beads", [(b, a) for a, b in forward])
        low_at, high_at = 0, 0

    results = pl.pallas_call(
        functools.partial(bead_kernel, scale, 1.0 / atoms, beads),
        out_shape=[shape((4, width), F32)] * beads,
        in_specs=[SMEM, ANY] + [VMEM] * beads,
        out_specs=[VMEM] * beads,
        scratch_shapes=[
            pltpu.VMEM((ranks, 16, width), F32),
            pltpu.VMEM((MODES, atoms), BF16),
            pltpu.VMEM((MODES, atoms), BF16),
            pltpu.VMEM((MODES, atoms), BF16),
            pltpu.VMEM((MODES, atoms), BF16),
            pltpu.VMEM((48, atoms), BF16),
            pltpu.VMEM((8, atoms), F32),
            pltpu.VMEM((8, atoms), F32),
            pltpu.VMEM((8, atoms), F32),
            pltpu.VMEM((24, MODES), F32),
            pltpu.VMEM((8, beads * width), F32),
            pltpu.SemaphoreType.DMA,
        ],
        compiler_params=params(24),
        name="bead",
        cost_estimate=pl.CostEstimate(flops=10**10, bytes_accessed=10**6, transcendentals=0),
    )(rank, weights, *blocks)

    home = [results[0]] + [in_group(results[t], t) for t in range(1, beads)]

    new_places, new_speeds, charge = pl.pallas_call(
        functools.partial(move_kernel, low_at, high_at),
        out_shape=(
            shape(places.shape, F32),
            shape(places.shape, F32),
            shape(charges_in.shape, F32),
        ),
        in_specs=[SMEM] + [VMEM] * (5 + beads),
        out_specs=(VMEM, VMEM, VMEM),
        scratch_shapes=[pltpu.VMEM(((dims + 1) * beads, width), F32)],
        compiler_params=params(4),
        name="move",
    )(rank, places, speeds, low, high, pull, *home)
    return new_places.transpose(1, 0, 2), new_speeds.transpose(1, 0, 2), charge


def solution(mesh):
    return jax.shard_map(
        body,
        mesh=mesh,
        in_specs=(
            P("beads", None, "atoms"),
            P("beads", None, "atoms"),
            P("beads", "atoms"),
            P("atoms"),
            P(None, "atoms"),
            P(),
            P(),
            P(),
            P(),
            P(),
            P(),
        ),
        out_specs=(P("beads", None, "atoms"), P("beads", None, "atoms"), P("beads", "atoms")),
        check_vma=False,
    )
```

```python
import functools
import math

import jax
import jax.numpy as jnp
from jax import lax
from jax.experimental import pallas as pl
from jax.experimental.pallas import tpu as pltpu
from jax.sharding import PartitionSpec as P

KVEC = 2048
QITERS = 2
SPECIES = 8
KMAX = 8
MODES = 160

two_pi = 2.0 * math.pi
ewald_gain = 4.0
mixing = 0.5
spring_rate = 0.5
time_step = 0.05

COS = (
    0.9999999998855522,
    -19.739208743453656,
    64.93938907588092,
    -85.45665831455305,
    60.242131335932854,
    -26.404668174676782,
    7.800131403864327,
    -1.4531122801527303,
)
SIN = (
    6.2831853025115,
    -41.34170040531697,
    81.60513138577565,
    -76.70301535354703,
    42.02592698387527,
    -14.89984666196953,
    3.2381375032044204,
)

F32 = jnp.float32
BF16 = jnp.bfloat16
NT = (((1,), (1,)), ((), ()))
NN = (((1,), (0,)), ((), ()))


def horner(coeffs, x):
    value = jnp.full_like(x, coeffs[-1])
    for coeff in coeffs[-2::-1]:
        value = value * x + coeff
    return value


def turns(multiple, x):
    t = multiple * x
    t = t - jnp.floor(t + 0.5)
    square = t * t
    return horner(COS, square), t * horner(SIN, square)


def halves(x):
    high = x.astype(BF16)
    return high, (x - high.astype(F32)).astype(BF16)


def rows_of(one, two, rest):
    high, low = halves(jnp.concatenate([one, two], 0))
    rest_high = rest.astype(BF16).astype(F32)
    both = jnp.concatenate([rest_high, rest - rest_high], 0).astype(BF16)
    return jnp.concatenate([high, both, low], 0)


def product(left, high, low, dims):
    main = lax.dot_general(left, high, dims, preferred_element_type=F32)
    one = main[0:8] + main[32:40]
    two = main[8:16] + main[40:48]
    rest = main[16:24] + main[24:32]
    if low is not None:
        minor = lax.dot_general(left[0:32], low, dims, preferred_element_type=F32)
        one = one + minor[0:8]
        two = two + minor[8:16]
        rest = rest + minor[16:24]
    return one, two, rest


def partner(me, t, count):
    if count & (count - 1) == 0:
        return me ^ abs(t)
    return (me + t + count) % count


def lookup(tables, kinds):
    found = [jnp.zeros(kinds.shape, F32) for _ in tables]
    for kind in range(SPECIES):
        here = kinds == kind
        found = [jnp.where(here, table[kind], x) for table, x in zip(tables, found)]
    return found


def pack_kernel(
    rank_ref,
    pos_hbm,
    charge_hbm,
    species_hbm,
    neighbors_hbm,
    chi_hbm,
    hard_hbm,
    bond_hbm,
    *refs,
):
    outs = refs[:-8]
    pos, charge, species, neighbors, chi_table, hard_table, bond_table, arrived = refs[-8:]
    sources = (pos_hbm, charge_hbm, species_hbm, neighbors_hbm, chi_hbm, hard_hbm, bond_hbm)
    targets = (pos, charge, species, neighbors, chi_table, hard_table, bond_table)
    copies = [
        pltpu.make_async_copy(source, target, arrived.at[i])
        for i, (source, target) in enumerate(zip(sources, targets))
    ]
    for copy in copies:
        copy.start()
    for copy in copies:
        copy.wait()
    dims, beads, width = pos.shape
    chi, hard, bond = lookup((chi_table, hard_table, bond_table), species[...])
    shared = [chi, mixing / hard, bond, jnp.zeros((1, width), F32)]
    near = neighbors[...].astype(F32)
    me = rank_ref[0] % beads
    for t in range(beads):
        bead = pl.ds(partner(me, t, beads), 1)
        own = [pos[d, bead, :] for d in range(dims)] + [charge[bead, :]]
        outs[t][0:8, :] = near
        outs[t][8:16, :] = jnp.concatenate(own + shared, 0)


def sort_kernel(beads, rank_ref, *refs):
    out = refs[beads]
    me = rank_ref[0] % beads
    for t in range(beads):
        out[partner(me, -t, beads)] = refs[t][...]


def weight_kernel(k_index, kernel, pos, species, mass_table, after, out, edges, pull):
    del after
    (mass,) = lookup((mass_table,), species[...])
    pull[...] = time_step / mass
    dims, beads, _ = pos.shape
    for d in range(dims):
        edges[d : d + 1, :] = pos[d, 0:1, :]
        edges[dims + d : dims + d + 1, :] = pos[d, beads - 1 : beads, :]
    count = k_index.shape[1]
    k = k_index[...]
    first, second, third = k[0:1], k[1:2], k[2:3]
    flip = (first < 0) | ((first == 0) & (second < 0))
    sign = jnp.where(flip, -1, 1)
    p, q, r = sign * first, sign * second, sign * third
    wide = 16 * (p - 1)
    with_p = jnp.where(q > 0, wide + q - 1, jnp.where(q < 0, wide + 7 - q, 135 + p))
    without_p = jnp.where(q > 0, 127 + q, 144)
    mode = jnp.where(p > 0, with_p, without_p)
    at = lax.broadcasted_iota(jnp.int32, (MODES, count), 0)
    chosen = jnp.where(at == mode, 1.0, 0.0).astype(BF16)
    row = lax.broadcasted_iota(jnp.int32, (8, count), 0)
    weight = kernel[...]
    here = row + 1 == jnp.abs(r)
    even = jnp.where(here, weight, 0.0)
    odd = jnp.where(here, jnp.where(r < 0, -weight, weight), 0.0)
    zero = jnp.where((row == 0) & (r == 0), weight, 0.0)
    even, odd, zero = product(rows_of(even, odd, zero), chosen, None, NT)
    out[0:8, :] = even
    out[8:16, :] = odd
    out[16:24, :] = zero


def bead_kernel(
    scale,
    inverse_atoms,
    beads,
    groups,
    rank_ref,
    weights_hbm,
    *refs,
):
    blocks, outs = refs[:groups], refs[groups : groups + beads]
    (
        got,
        cos_high,
        cos_low,
        sin_high,
        sin_low,
        left,
        z_cos,
        z_sin,
        charges,
        weights,
        mine,
        arrived,
    ) = refs[groups + beads :]
    bring = pltpu.make_async_copy(weights_hbm, weights, arrived)
    bring.start()
    ranks, _, width = got.shape
    me = rank_ref[0] % beads
    for k in range(groups):
        source = partner(rank_ref[0] // beads, -k, groups) * beads
        for member in range(beads):
            got[source + member] = blocks[k][member]
    lane = lax.broadcasted_iota(jnp.int32, (8, width), 1)
    row = lax.broadcasted_iota(jnp.int32, (8, width), 0)
    multiple = (row + 1).astype(F32)
    single = jnp.where(row == 0, 1.0, 0.0)
    blank = jnp.zeros((8, width), F32)

    def at(j):
        return slice(j * width, (j + 1) * width)

    def everywhere(x):
        return jnp.broadcast_to(x, (8, width))

    def column_sum(x):
        return everywhere(jnp.sum(x, axis=0, keepdims=True))

    chi, hard, bond, charge = [], [], [], []
    for j in range(ranks):
        cx, sx = turns(multiple, got[j, 8:9, :])
        cy, sy = turns(multiple, got[j, 9:10, :])
        cz, sz = turns(multiple, got[j, 10:11, :])
        z_cos[:, at(j)] = cz
        z_sin[:, at(j)] = sz

        def keep(rows, cosine, sine):
            high, low = halves(cosine)
            cos_high[rows, at(j)] = high
            cos_low[rows, at(j)] = low
            high, low = halves(sine)
            sin_high[rows, at(j)] = high
            sin_low[rows, at(j)] = low

        for p in range(8):
            cp, sp = everywhere(cx[p : p + 1]), everywhere(sx[p : p + 1])
            cc, ss, sc, cs = cp * cy, sp * sy, sp * cy, cp * sy
            keep(
                slice(16 * p, 16 * p + 16),
                jnp.concatenate([cc - ss, cc + ss], 0),
                jnp.concatenate([sc + cs, sc - cs], 0),
            )
        keep(slice(128, 144), jnp.concatenate([cy, cx], 0), jnp.concatenate([sy, sx], 0))
        keep(
            slice(144, 160),
            jnp.concatenate([single, blank], 0),
            jnp.concatenate([blank, blank], 0),
        )
        charge.append(everywhere(got[j, 11:12, :]))
        chi.append(everywhere(got[j, 12:13, :]))
        hard.append(everywhere(got[j, 13:14, :]))
        bond.append(everywhere(got[j, 14:15, :]))

    bring.wait()
    even, odd, zero = weights[0:8, :], weights[8:16, :], weights[16:24, :]

    def coefficients(charge):
        for j in range(ranks):
            left[:, at(j)] = rows_of(
                charge[j] * z_cos[:, at(j)], charge[j] * z_sin[:, at(j)], charge[j] * single
            )
        t_cc, t_cs, t_c0 = product(left[...], cos_high[...], cos_low[...], NT)
        t_sc, t_ss, t_s0 = product(left[...], sin_high[...], sin_low[...], NT)
        v_cos = (even * t_cc - odd * t_ss, even * t_cs + odd * t_sc, zero * t_c0)
        v_sin = (even * t_sc + odd * t_cs, even * t_ss - odd * t_cc, zero * t_s0)
        return v_cos, v_sin

    for rounds in range(QITERS):
        v_cos, v_sin = coefficients(charge)
        from_cos = product(rows_of(*v_cos), cos_high[...], cos_low[...], NN)
        from_sin = product(rows_of(*v_sin), sin_high[...], sin_low[...], NN)
        u_c, u_s, u_0 = (a + b for a, b in zip(from_cos, from_sin))
        weighted = [b * q for b, q in zip(bond, charge)]
        relaxed = []
        total = blank
        for j in range(ranks):
            potential = scale * column_sum(
                z_cos[:, at(j)] * u_c[:, at(j)] + z_sin[:, at(j)] * u_s[:, at(j)] + u_0[:, at(j)]
            )
            before = weighted[(j - 1) % ranks]
            after = weighted[(j + 1) % ranks]
            lower = jnp.where(lane < 3 * width // 4, weighted[j], before)
            upper = jnp.where(lane >= width // 4, weighted[j], after)
            place = (lane + got[j, 0:8, :].astype(jnp.int32)) & (width - 1)
            near = jnp.where(
                lane < width // 2,
                jnp.take_along_axis(lower, place, axis=1),
                jnp.take_along_axis(upper, place, axis=1),
            )
            new = (1.0 - mixing) * charge[j] - hard[j] * (
                chi[j] + potential + bond[j] * column_sum(near)
            )
            relaxed.append(new)
            total = total + new
        mean = jnp.sum(total, axis=1, keepdims=True) * inverse_atoms
        charge = [new - mean for new in relaxed]

    for j in range(ranks):
        charges[:, at(j)] = charge[j]
    (v_cc, v_cs, v_c0), (v_sc, v_ss, v_s0) = coefficients(charge)
    mode = lax.broadcasted_iota(jnp.int32, (8, MODES), 1)
    inner = mode & 15
    wave_x = jnp.where(
        mode < 128, (mode >> 4) + 1, jnp.where((mode >= 136) & (mode < 144), mode - 135, 0)
    ).astype(F32)
    wave_y = jnp.where(
        mode < 128,
        jnp.where(inner < 8, inner + 1, 7 - inner),
        jnp.where(mode < 136, mode - 127, 0),
    ).astype(F32)
    span = beads * width
    base = pl.multiple_of((rank_ref[0] // beads) * span, span)
    own = pl.ds(base, span)
    ch, cl, sh, sl = (ref[:, own] for ref in (cos_high, cos_low, sin_high, sin_low))
    zc, zs, q = z_cos[:, own], z_sin[:, own], charges[:, own]

    v_cos, v_sin = (v_cc, v_cs, v_c0), (v_sc, v_ss, v_s0)
    for_cos, for_sin = [rows_of(*v_cos)], [rows_of(*v_sin)]
    for wave in (wave_x, wave_y):
        for_cos.append(rows_of(*(-wave * v for v in v_sin)))
        for_sin.append(rows_of(*(wave * v for v in v_cos)))
    for_cos, for_sin = jnp.concatenate(for_cos, 0), jnp.concatenate(for_sin, 0)
    fields = sum(
        lax.dot_general(rows, part, NN, preferred_element_type=F32)
        for rows, part in ((for_cos, ch), (for_cos, cl), (for_sin, sh), (for_sin, sl))
    )
    (u_c, u_s, _), (x_c, x_s, x_0), (y_c, y_s, y_0) = (
        (f[0:8] + f[32:40], f[8:16] + f[40:48], f[16:24] + f[24:32])
        for f in (fields[48 * i : 48 * i + 48] for i in range(3))
    )
    along_x = zc * x_c + zs * x_s + x_0
    along_y = zc * y_c + zs * y_s + y_0
    wide_multiple = jnp.broadcast_to(multiple[:, 0:1], (8, span))
    along_z = wide_multiple * (zs * u_c - zc * u_s)
    factor = (two_pi * scale) * q
    for t in range(beads):
        cut = at(t)
        fx, fy, fz = (
            factor[:, cut] * column_sum(f[:, cut]) for f in (along_x, along_y, along_z)
        )
        mine[:, cut] = jnp.where(
            row == 0, fx, jnp.where(row == 1, fy, jnp.where(row == 2, fz, q[:, cut]))
        )
    for t in range(beads):
        there = pl.multiple_of(partner(me, t, beads) * width, width)
        outs[t][...] = mine[0:4, pl.ds(there, width)]


def move_kernel(low_at, high_at, rank_ref, pos, vel, low, high, pull, *refs):
    dims, beads, width = pos.shape
    got, (pos_out, vel_out, charge_out, home) = refs[:beads], refs[beads:]
    me = rank_ref[0] % beads
    for t in range(beads):
        bead = partner(me, -t, beads)
        for d in range(dims + 1):
            home[pl.ds(d * beads + bead, 1), :] = got[t][d : d + 1, :]
    gain = jnp.broadcast_to(pull[...], (beads, width))
    for d in range(dims):
        here = pos[d]
        before = jnp.concatenate([low[low_at + d : low_at + d + 1, :], here[: beads - 1]], 0)
        after = jnp.concatenate([here[1:], high[high_at + d : high_at + d + 1, :]], 0)
        laplace = 2.0 * here - before - after
        force = home[d * beads : (d + 1) * beads, :]
        fresh = vel[d] + (gain * force - (time_step * spring_rate) * laplace)
        vel_out[d] = fresh
        pos_out[d] = here + time_step * fresh
    charge_out[...] = home[dims * beads : (dims + 1) * beads, :]


VMEM = pl.BlockSpec(memory_space=pltpu.VMEM)
SMEM = pl.BlockSpec(memory_space=pltpu.SMEM)
ANY = pl.BlockSpec(memory_space=pl.ANY)
HBM = pl.BlockSpec(memory_space=pltpu.HBM)


def stay(x):
    return pltpu.with_memory_space_constraint(x, pltpu.HBM)


def params(mebibytes):
    return pltpu.CompilerParams(vmem_limit_bytes=mebibytes << 20)


def body(
    positions,
    velocities,
    charges_in,
    species,
    neighbors,
    k_index,
    kernel,
    chi_table,
    hard_table,
    bond_table,
    mass_table,
):
    beads, dims, width = positions.shape
    ranks = lax.axis_size("atoms")
    chain = lax.axis_size("beads")
    atoms = ranks * width
    scale = ewald_gain / math.sqrt(KVEC * atoms)
    kinds = species[None, :]
    shape = jax.ShapeDtypeStruct

    places = positions.transpose(1, 0, 2)
    speeds = velocities.transpose(1, 0, 2)

    rank = lax.axis_index("atoms").astype(jnp.int32)[None]
    groups = ranks // beads

    def among_groups(x, k):
        pairs = [(r, partner(r // beads, k, groups) * beads + r % beads) for r in range(ranks)]
        return lax.ppermute(x, "atoms", pairs)

    def in_group(x, t):
        pairs = [(r, r // beads * beads + partner(r % beads, t, beads)) for r in range(ranks)]
        return lax.ppermute(x, "atoms", pairs)

    packed = pl.pallas_call(
        pack_kernel,
        out_shape=[shape((16, width), F32)] * beads,
        in_specs=[SMEM] + [HBM] * 7,
        out_specs=[VMEM] * beads,
        scratch_shapes=[
            pltpu.VMEM(places.shape, F32),
            pltpu.VMEM(charges_in.shape, F32),
            pltpu.VMEM(kinds.shape, jnp.int32),
            pltpu.VMEM(neighbors.shape, jnp.int32),
            pltpu.SMEM((SPECIES,), F32),
            pltpu.SMEM((SPECIES,), F32),
            pltpu.SMEM((SPECIES,), F32),
            pltpu.SemaphoreType.DMA((7,)),
        ],
        compiler_params=params(4),
        name="pack",
    )(rank, *map(stay, (places, charges_in, kinds, neighbors, chi_table, hard_table, bond_table)))
    gathered = [packed[0]] + [in_group(packed[t], t) for t in range(1, beads)]
    together = pl.pallas_call(
        functools.partial(sort_kernel, beads),
        out_shape=shape((beads, 16, width), F32),
        in_specs=[SMEM] + [VMEM] * beads,
        out_specs=VMEM,
        compiler_params=params(4),
        name="sort",
    )(rank, *gathered)
    if groups & (groups - 1) == 0:
        known, step = {0: together}, groups // 2
        while step:
            known.update({k ^ step: among_groups(x, step) for k, x in known.items()})
            step //= 2
        blocks = [known[k] for k in range(groups)]
    else:
        blocks = [together] + [among_groups(together, k) for k in range(1, groups)]

    weights, edges, pull = pl.pallas_call(
        weight_kernel,
        out_shape=(
            shape((24, MODES), F32),
            shape((2 * dims, width), F32),
            shape((1, width), F32),
        ),
        in_specs=[VMEM] * 4 + [SMEM, ANY],
        out_specs=(VMEM, VMEM, VMEM),
        compiler_params=params(8),
        name="weights",
        cost_estimate=pl.CostEstimate(flops=10**9, bytes_accessed=10**5, transcendentals=0),
    )(k_index, kernel[None, :], places, kinds, mass_table, packed[0])
    if chain == 2:
        low = high = lax.ppermute(edges, "beads", [(0, 1), (1, 0)])
        low_at, high_at = dims, 0
    else:
        forward = [(i, (i + 1) % chain) for i in range(chain)]
        low = lax.ppermute(edges[dims:], "beads", forward)
        high = lax.ppermute(edges[:dims], "beads", [(b, a) for a, b in forward])
        low_at, high_at = 0, 0

    results = pl.pallas_call(
        functools.partial(bead_kernel, scale, 1.0 / atoms, beads, groups),
        out_shape=[shape((4, width), F32)] * beads,
        in_specs=[SMEM, ANY] + [VMEM] * groups,
        out_specs=[VMEM] * beads,
        scratch_shapes=[
            pltpu.VMEM((ranks, 16, width), F32),
            pltpu.VMEM((MODES, atoms), BF16),
            pltpu.VMEM((MODES, atoms), BF16),
            pltpu.VMEM((MODES, atoms), BF16),
            pltpu.VMEM((MODES, atoms), BF16),
            pltpu.VMEM((48, atoms), BF16),
            pltpu.VMEM((8, atoms), F32),
            pltpu.VMEM((8, atoms), F32),
            pltpu.VMEM((8, atoms), F32),
            pltpu.VMEM((24, MODES), F32),
            pltpu.VMEM((8, beads * width), F32),
            pltpu.SemaphoreType.DMA,
        ],
        compiler_params=params(24),
        name="bead",
        cost_estimate=pl.CostEstimate(flops=10**10, bytes_accessed=10**6, transcendentals=0),
    )(rank, weights, *blocks)

    home = [results[0]] + [in_group(results[t], t) for t in range(1, beads)]

    new_places, new_speeds, charge = pl.pallas_call(
        functools.partial(move_kernel, low_at, high_at),
        out_shape=(
            shape(places.shape, F32),
            shape(places.shape, F32),
            shape(charges_in.shape, F32),
        ),
        in_specs=[SMEM] + [VMEM] * (5 + beads),
        out_specs=(VMEM, VMEM, VMEM),
        scratch_shapes=[pltpu.VMEM(((dims + 1) * beads, width), F32)],
        compiler_params=params(4),
        name="move",
    )(rank, places, speeds, low, high, pull, *home)
    return new_places.transpose(1, 0, 2), new_speeds.transpose(1, 0, 2), charge


def solution(mesh):
    return jax.shard_map(
        body,
        mesh=mesh,
        in_specs=(
            P("beads", None, "atoms"),
            P("beads", None, "atoms"),
            P("beads", "atoms"),
            P("atoms"),
            P(None, "atoms"),
            P(),
            P(),
            P(),
            P(),
            P(),
            P(),
        ),
        out_specs=(P("beads", None, "atoms"), P("beads", None, "atoms"), P("beads", "atoms")),
        check_vma=False,
    )
```
